32 devices in a mesh: lat: 4 (over x, core), lon: 8 (over z, y).
Axes of the slice: x: 2, y: 2, z: 4, core: 2. Of those that a mesh axis runs over, the one named last changes fastest.
Arguments:
- state: bfloat16 [64, 64, 256], P('lat', 'lon'), may hold values from -45 to 45
- cotangent: bfloat16 [64, 64, 256], P('lat', 'lon'), may hold values from -6 to 6
- land_sea: int32 [64, 64], P('lat', 'lon'), may hold values 0 or 1
- regime: int32 [4, 8, 16, 8, 1], P('lat', 'lon'), may hold values from 0 to 15; in each aligned block of 128 rows (0 to 127, 128 to 255, ..., all dimensions but the last counted through in order) at most 16 rows name the same one
- first_gain: float32 [256], replicated, may hold values from 0.1 to 1.9
- second_gain: float32 [256], replicated, may hold values from 0.1 to 1.9
- project_weight: bfloat16 [256, 768], replicated, may hold values from -0.375 to 0.375
- out_weight: bfloat16 [256, 256], replicated, may hold values from -0.375 to 0.375
- pos_bias: float32 [8, 49], replicated, may hold values from -3 to 315
- up_weight: bfloat16 [256, 16384], P(None, 'lon'), may hold values from -0.375 to 0.375
- down_weight: bfloat16 [16384, 256], P('lon'), may hold values from -0.1875 to 0.1875
Outputs:
- block_out: bfloat16 [64, 64, 256], P('lat', 'lon')
- grad_up: float32 [256, 16384], P(None, 'lon')
- grad_down: float32 [16384, 256], P('lon')
The draws below stay inside these ranges and needn't reach their ends.
Inputs may be any that keep to these rules, and one draw needn't show every extreme that they name: Among the 16 x 8 cells of one tile at most 16 share a regime, and some tile has exactly 16 cells of one regime. Every regime occurs somewhere.
All inputs are finite; a program needn't handle non-finite values. No bound on the sum of `land_sea` on one device may be relied on, other than what follows from the above.
Results may differ from the reference program's by a relative error of at most 0.022.
Values may be sent and summed in bfloat16 or wider, within the bound.
A program may use at most 64 MiB of HBM per device.

```python
import math
import jax
import jax.numpy as jnp
import numpy as np
from jax import lax

D = 256
HEADS = 8
HD = 32
WINDOW = 7
EXPERTS = 16
FF = 1024
LAT_DEV = 16
LON_DEV = 8
CAP = 16
NLAT = 64
NLON = 64
N_LAT = 4
N_LON = 8


def draw_state(key, part):
    key = jax.random.fold_in(key, 11)
    normal_key, row_key, column_key = jax.random.split(key, 3)
    grid_shape = (NLAT, NLON, D)
    normal_part = jax.random.truncated_normal(normal_key, -3.0, 3.0, grid_shape, jnp.float32)
    row_scale = jnp.exp(jax.random.uniform(row_key, (NLAT, NLON, 1), jnp.float32, math.log(0.3), math.log(3.0)))
    column_scale = jnp.exp(jax.random.uniform(column_key, (1, 1, D), jnp.float32, math.log(0.3), math.log(3.0)))
    return (normal_part * row_scale * column_scale).astype(jnp.bfloat16)


def draw_pos_bias(key, part):
    key = jax.random.fold_in(key, 23)
    key_list = jax.random.split(key, 1)
    tap_count = WINDOW * WINDOW
    normal_part = jax.random.truncated_normal(key_list[0], -3.0, 3.0, (HEADS, tap_count), jnp.float32)
    return normal_part


def with_ends(result, stream_key, smallest, largest):
    extent = result.shape
    place = [jax.random.randint(jax.random.fold_in(stream_key, axis), (), 0, extent[axis]) for axis in range(len(extent))]
    result = result.at[tuple(place)].set(smallest)
    longest = extent.index(max(extent))
    place[longest] = (place[longest] + 1) % extent[longest]
    return result.at[tuple(place)].set(largest)


def shard_levels(rng, dims, shards, least, high):
    def one(axis_at, shards_of):
        draws = jax.random.uniform(jax.random.fold_in(jax.random.fold_in(rng, 6), axis_at), (shards_of,), jnp.float32, least / len(shards), high / len(shards))
        return jnp.repeat(jnp.exp(draws), dims[axis_at] // shards_of).reshape((-1,) + (1,) * (len(dims) - axis_at - 1))

    factor_of = one(*shards[0])
    for cut in shards[1:]:
        factor_of = factor_of * one(*cut)
    return factor_of


def deal_out(rng, own, number, rows, count, top, bound, skew):
    sequence = jax.random.permutation(rng, count)
    packed, usual = load_shares(count, rows * top, bound, skew, True), load_shares(count, rows * top, bound, skew, False)
    places = jnp.arange(count)

    def named(tallies, rotation):
        used = int((tallies > 0).sum())
        fixed = max(1, used // 4)
        moved = fixed + (places - fixed + rotation * (used - fixed)) % max(1, count - fixed)
        return jnp.zeros((count,), jnp.int32).at[sequence[jnp.where(places < fixed, places, moved)]].set(jnp.asarray(tallies, jnp.int32))

    tallies = jnp.where(number % 4 == 0, named(packed, number // 4), named(usual, number - number // 4 - 1))
    mixed = jax.random.permutation(jax.random.fold_in(own, 3), count)
    donor, sink = mixed[0:count // 2 * 2:2], mixed[1:count // 2 * 2:2]
    slack = jnp.minimum(tallies[donor] - 1, bound - tallies[sink]) // 2
    slack = jnp.where((donor == sequence[0]) | (sink == sequence[0]) | (tallies[sink] == 0), 0, jnp.maximum(slack, 0))
    moved = jax.random.randint(jax.random.fold_in(own, 4), (count // 2,), 0, 1 << 20) % (slack + 1)
    tallies = tallies.at[donor].add(-moved).at[sink].add(moved)
    items = jnp.searchsorted(jnp.cumsum(tallies), jnp.arange(rows * top), side="right").astype(jnp.int32)
    table = items.reshape(top, rows).T
    table = table[jax.random.permutation(jax.random.fold_in(own, 1), rows)]
    rotation = jax.random.randint(jax.random.fold_in(own, 2), (rows, 1), 0, top)
    return jnp.take_along_axis(table, (jnp.arange(top)[None, :] + rotation) % top, axis=1)


def load_shares(amount, total, limit, skew, full):
    weights = [(1 << 20) // math.isqrt(rank ** skew) + 1 for rank in range(1, amount + 1)]
    largest = limit if full else min(limit, max(-(-total // amount), total * weights[0] // sum(weights)))
    least = 1 if total - largest >= amount - 1 else 0
    given, surplus = [largest] + [least] * (amount - 1), total - largest - least * (amount - 1)
    while surplus > 0:
        movable = [i for i in range(1, amount) if given[i] < largest] or [i for i in range(1, amount) if given[i] < limit]
        whole, remaining = sum([weights[i] for i in movable]), surplus
        for i in movable:
            extra = min(limit - given[i], max(1, remaining * weights[i] // whole), surplus)
            given[i] = given[i] + extra
            surplus = surplus - extra
    return np.array(given)


def scatter_about(own_key, extent, scale, most, cuts=(), held_as=jnp.bfloat16):
    entries = scale * jax.random.normal(own_key, extent, jnp.float32)
    if cuts:
        entries = entries * shard_levels(own_key, extent, cuts, -0.22, 0.18)
    return jnp.clip(entries, -most, most).astype(held_as)


def setup_inputs(seed: int = 0) -> dict:
    streams_of = jax.random.split(jax.random.key(seed), 12)
    state = draw_state(jax.random.fold_in(streams_of[11], 71), 0)
    cotangent = scatter_about(streams_of[1], (NLAT, NLON, D), (64.0 / (NLAT * NLON) ** 0.5), 6.0, ((0, 4), (1, 8)))
    land_sea = with_ends((jax.random.randint(streams_of[2], (NLAT, NLON), 0, 10) < 7).astype(jnp.int32), jax.random.fold_in(streams_of[2], 1), 0, 1)
    regime_keys = jax.random.split(jax.random.fold_in(streams_of[3], 1), N_LAT * N_LON * LAT_DEV * LON_DEV // (LAT_DEV * LON_DEV))
    regime_turns = jax.random.permutation(jax.random.fold_in(streams_of[3], 3), N_LAT * N_LON * LAT_DEV * LON_DEV // (LAT_DEV * LON_DEV))
    regime = jax.vmap(lambda own, number: deal_out(jax.random.fold_in(streams_of[3], 2), own, number, LAT_DEV * LON_DEV, EXPERTS, 1, CAP, 2))(regime_keys, regime_turns).reshape((N_LAT, N_LON, LAT_DEV, LON_DEV, 1))
    first_gain = jnp.clip(1.0 + 0.18 * jax.random.normal(streams_of[4], (D,), jnp.float32), 0.1, 1.9)
    second_gain = jnp.clip(1.0 + 0.18 * jax.random.normal(streams_of[5], (D,), jnp.float32), 0.1, 1.9)
    project_weight = scatter_about(streams_of[6], (D, 3 * D), D ** -0.5, 0.375)
    out_weight = scatter_about(streams_of[7], (D, D), D ** -0.5, 0.375)
    pos_bias = draw_pos_bias(jax.random.fold_in(streams_of[11], 71), 0)
    up_weight = scatter_about(streams_of[9], (D, EXPERTS * FF), D ** -0.5, 0.375, ((1, 8),))
    down_weight = scatter_about(streams_of[10], (EXPERTS * FF, D), FF ** -0.5, 0.1875, ((0, 8),))
    return dict(state=state, cotangent=cotangent, land_sea=land_sea, regime=regime, first_gain=first_gain, second_gain=second_gain, project_weight=project_weight, out_weight=out_weight, pos_bias=pos_bias, up_weight=up_weight, down_weight=down_weight)


def layer_norm(values, gain_vec):
    values = values.astype(jnp.float32)
    mean_val = lax.optimization_barrier(jnp.mean(values, axis=-1, keepdims=True))
    spread = lax.optimization_barrier(jnp.mean(jnp.square(values - mean_val), axis=-1, keepdims=True))
    return ((values - mean_val) * lax.rsqrt(spread + 1e-05) * gain_vec).astype(jnp.bfloat16)

def gelu_value(inputs):
    return 0.5 * inputs * (1.0 + jax.scipy.special.erf(inputs * 0.7071067811865476))

def gelu_slope(inputs):
    return 0.5 * (1.0 + jax.scipy.special.erf(inputs * 0.7071067811865476)) + inputs * jnp.exp(-0.5 * inputs * inputs) * 0.3989422804014327

def reference(state, cotangent, land_sea, regime, first_gain, second_gain, project_weight, out_weight, pos_bias, up_weight, down_weight):
    cell_count = NLAT * NLON
    window_reach = WINDOW // 2
    center = WINDOW * WINDOW // 2
    score_scale = 1.0 / math.sqrt(HD)
    normed_in = layer_norm(state, first_gain).reshape(cell_count, D)
    triple = jnp.dot(normed_in, project_weight, preferred_element_type=jnp.float32).astype(jnp.bfloat16)
    queries = triple[:, :D].astype(jnp.float32).reshape(NLAT, NLON, HEADS, HD)
    lat_pad = ((window_reach, window_reach), (0, 0), (0, 0))
    key_rows = jnp.pad(triple[:, D:2 * D].reshape(NLAT, NLON, D), lat_pad)
    value_rows = jnp.pad(triple[:, 2 * D:].reshape(NLAT, NLON, D), lat_pad)
    mask_rows = jnp.pad(land_sea, ((window_reach, window_reach), (0, 0)))
    score_list = []
    valid_list = []
    for row_shift in range(WINDOW):
        for col_shift in range(WINDOW):
            tap_index = row_shift * WINDOW + col_shift
            moved_keys = jnp.roll(key_rows[row_shift:row_shift + NLAT], window_reach - col_shift, axis=1)
            moved_keys = moved_keys.astype(jnp.float32).reshape(NLAT, NLON, HEADS, HD)
            score_list.append(lax.optimization_barrier(jnp.sum(queries * moved_keys, axis=-1)) * score_scale + pos_bias[:, tap_index])
            moved_mask = jnp.roll(mask_rows[row_shift:row_shift + NLAT], window_reach - col_shift, axis=1)
            valid_list.append(jnp.logical_or(moved_mask > 0, tap_index == center))
    scores = jnp.stack(score_list)
    valid_mask = jnp.stack(valid_list)[..., None]
    row_top = lax.optimization_barrier(jnp.max(jnp.where(valid_mask, scores, -jnp.inf), axis=0, keepdims=True))
    raw_weights = jnp.exp(jnp.where(valid_mask, scores - row_top, -jnp.inf))
    weights = (raw_weights / lax.optimization_barrier(jnp.sum(raw_weights, axis=0, keepdims=True))).astype(jnp.bfloat16)
    attended = jnp.zeros((NLAT, NLON, HEADS, HD), jnp.float32)
    for row_shift in range(WINDOW):
        for col_shift in range(WINDOW):
            tap_index = row_shift * WINDOW + col_shift
            moved_values = jnp.roll(value_rows[row_shift:row_shift + NLAT], window_reach - col_shift, axis=1)
            moved_values = moved_values.astype(jnp.float32).reshape(NLAT, NLON, HEADS, HD)
            attended = attended + weights[tap_index][..., None].astype(jnp.float32) * moved_values
    attended = attended.reshape(cell_count, D).astype(jnp.bfloat16)
    residual = (state.reshape(cell_count, D).astype(jnp.float32) + jnp.dot(attended, out_weight, preferred_element_type=jnp.float32)).astype(jnp.bfloat16)
    second = layer_norm(residual, second_gain)
    land_flat = land_sea.reshape(cell_count, 1)
    tangent = cotangent.reshape(cell_count, D) * land_flat.astype(jnp.bfloat16)
    labels = regime.transpose(0, 2, 1, 3, 4).reshape(cell_count).astype(jnp.int32)
    sorted_ids = jnp.argsort(labels, stable=True).astype(jnp.int32)
    counts = lax.optimization_barrier(jnp.sum((labels[:, None] == jnp.arange(EXPERTS, dtype=jnp.int32)[None, :]).astype(jnp.int32), axis=0)).astype(jnp.int32)
    starts = (jnp.cumsum(counts) - counts).astype(jnp.int32)
    block_rows = 2048
    sorted_pad = jnp.concatenate([sorted_ids, jnp.full((block_rows,), cell_count, jnp.int32)])
    input_pad = jnp.concatenate([second, jnp.zeros((1, D), jnp.bfloat16)])
    tangent_pad = jnp.concatenate([tangent, jnp.zeros((1, D), jnp.bfloat16)])
    expert_out = jnp.zeros((cell_count + 1, D), jnp.bfloat16)
    up_list = []
    down_list = []
    for expert in range(EXPERTS):
        up_block = up_weight[:, expert * FF:(expert + 1) * FF]
        down_block = down_weight[expert * FF:(expert + 1) * FF]

        def block_step(block_index, state_carry):
            out_rows, acc_up, acc_down = state_carry
            offset = (starts[expert] + block_index * block_rows).astype(jnp.int32)
            picked = lax.dynamic_slice_in_dim(sorted_pad, offset, block_rows)
            inside = block_index * block_rows + jnp.arange(block_rows, dtype=jnp.int32) < counts[expert]
            picked = jnp.where(inside, picked, cell_count).astype(jnp.int32)
            row_data = input_pad[picked]
            row_tangent = tangent_pad[picked]
            hidden = jnp.dot(row_data, up_block, preferred_element_type=jnp.float32)
            active = gelu_value(hidden).astype(jnp.bfloat16)
            produced = jnp.dot(active, down_block, preferred_element_type=jnp.float32).astype(jnp.bfloat16)
            out_rows = out_rows.at[picked].set(produced)
            back_act = jnp.dot(row_tangent, down_block.T, preferred_element_type=jnp.float32)
            pre_act = (back_act * gelu_slope(hidden)).astype(jnp.bfloat16)
            acc_down = acc_down + jnp.dot(active.T, row_tangent, preferred_element_type=jnp.float32)
            acc_up = acc_up + jnp.dot(row_data.T, pre_act, preferred_element_type=jnp.float32)
            return (out_rows, acc_up, acc_down)
        block_total = ((counts[expert] + block_rows - 1) // block_rows).astype(jnp.int32)
        expert_out, acc_up, acc_down = lax.fori_loop(0, block_total, block_step, (expert_out, jnp.zeros((D, FF), jnp.float32), jnp.zeros((FF, D), jnp.float32)))
        up_list.append(acc_up)
        down_list.append(acc_down)
    grad_up = jnp.concatenate(up_list, axis=1)
    grad_down = jnp.concatenate(down_list, axis=0)
    block_out = (land_flat.astype(jnp.float32) * (residual.astype(jnp.float32) + expert_out[:cell_count].astype(jnp.float32))).astype(jnp.bfloat16)
    return (block_out.reshape(NLAT, NLON, D), grad_up, grad_down)
```

```python
import functools
import math

import jax
import jax.numpy as jnp
from jax import lax
from jax.experimental import pallas as pl
from jax.experimental.pallas import tpu as pltpu
from jax.sharding import PartitionSpec as P

WINDOW = 7
EXPERTS = 16


def from_partner(value, axis, apart):
    mask = 2**apart
    pairs = [(source, source ^ mask) for source in range(lax.axis_size(axis))]
    return lax.ppermute(value, axis, pairs)


def extended(cells, sides, width, closed):
    for axis, dim in sides:
        count = lax.axis_size(axis)
        ends = count if closed else count - 1
        head = lax.slice_in_dim(cells, 0, width, axis=dim)
        tail = lax.slice_in_dim(cells, cells.shape[dim] - width, cells.shape[dim], axis=dim)
        cells = jnp.concatenate(
            [
                lax.ppermute(tail, axis, [(i, (i + 1) % count) for i in range(ends)]),
                cells,
                lax.ppermute(head, axis, [((i + 1) % count, i) for i in range(ends)]),
            ],
            axis=dim,
        )
    return cells


def layer_norm(values, gain_vec):
    values = values.astype(jnp.float32)
    mean_val = jnp.mean(values, axis=-1, keepdims=True)
    spread = jnp.mean(jnp.square(values - mean_val), axis=-1, keepdims=True)
    return ((values - mean_val) * lax.rsqrt(spread + 1e-05) * gain_vec).astype(jnp.bfloat16)


def gelu_value(inputs):
    return 0.5 * inputs * (1.0 + jax.scipy.special.erf(inputs * 0.7071067811865476))


def gelu_slope(inputs):
    return (
        0.5 * (1.0 + jax.scipy.special.erf(inputs * 0.7071067811865476))
        + inputs * jnp.exp(-0.5 * inputs * inputs) * 0.3989422804014327
    )


def expert_pass(inputs, tangents, up_block, down_block):
    hidden = jnp.einsum("nlsd,dlf->nlsf", inputs, up_block, preferred_element_type=jnp.float32)
    active = gelu_value(hidden).astype(jnp.bfloat16)
    outputs = jnp.einsum("nlsf,lfd->nlsd", active, down_block, preferred_element_type=jnp.float32)
    back_act = jnp.einsum(
        "nlsd,lfd->nlsf", tangents, down_block, preferred_element_type=jnp.float32
    )
    pre_act = (back_act * gelu_slope(hidden)).astype(jnp.bfloat16)
    grad_down = jnp.einsum("nlsf,nlsd->lfd", active, tangents, preferred_element_type=jnp.float32)
    grad_up = jnp.einsum("nlsd,nlsf->dlf", inputs, pre_act, preferred_element_type=jnp.float32)
    return (outputs, grad_up, grad_down)


def halve(grad_u, grad_d, lon_index, group_size):
    for bit_level in reversed(range(group_size.bit_length() - 1)):
        half_units = grad_u.shape[1] // 2
        high_bit = lon_index >> bit_level & 1 == 1
        keep_u = jnp.where(high_bit, grad_u[:, half_units:], grad_u[:, :half_units])
        give_u = jnp.where(high_bit, grad_u[:, :half_units], grad_u[:, half_units:])
        keep_d = jnp.where(high_bit, grad_d[half_units:], grad_d[:half_units])
        give_d = jnp.where(high_bit, grad_d[:half_units], grad_d[half_units:])
        taken_u, taken_d = (
            from_partner(give_u.astype(jnp.bfloat16), "lon", bit_level).astype(give_u.dtype),
            from_partner(give_d.astype(jnp.bfloat16), "lon", bit_level).astype(give_d.dtype),
        )
        grad_u = keep_u + taken_u
        grad_d = keep_d + taken_d
    return (grad_u, grad_d)


def on_device_general(
    state,
    cotangent,
    land_sea,
    regime,
    first_gain,
    second_gain,
    project_weight,
    out_weight,
    pos_bias,
    up_weight,
    down_weight,
):
    lat_rows, lon_cols, features = state.shape
    cell_count = lat_rows * lon_cols
    head_count = pos_bias.shape[0]
    head_dim = features // head_count
    window_reach = WINDOW // 2
    tap_count = WINDOW * WINDOW
    score_scale = 1.0 / math.sqrt(head_dim)
    normed_in = layer_norm(state, first_gain)
    flat_in = normed_in.reshape(cell_count, features)
    queries = jnp.dot(
        flat_in, project_weight[:, :features], preferred_element_type=jnp.float32
    ).astype(jnp.bfloat16)
    own_kv = jnp.dot(flat_in, project_weight[:, features:], preferred_element_type=jnp.float32)
    own_kv = own_kv.astype(jnp.bfloat16).reshape(lat_rows, lon_cols, 2 * features)
    wide_kv = extended(own_kv, (("lon", 1),), window_reach, True)
    keyvals = extended(wide_kv, (("lat", 0),), window_reach, False)
    wide_mask = extended(land_sea, (("lon", 1),), window_reach, True)
    full_mask = extended(wide_mask, (("lat", 0),), window_reach, False)
    feature_first = jnp.transpose(keyvals, (2, 0, 1))
    query_heads = queries.T.reshape(head_count, head_dim, cell_count)
    score_list = []
    mask_list = []
    for row_shift in range(WINDOW):
        for col_shift in range(WINDOW):
            key_tap = feature_first[
                :features, row_shift : row_shift + lat_rows, col_shift : col_shift + lon_cols
            ].reshape(head_count, head_dim, cell_count)
            score_list.append(
                jnp.einsum("hxc,hxc->hc", query_heads, key_tap, preferred_element_type=jnp.float32)
            )
            mask_list.append(
                full_mask[
                    row_shift : row_shift + lat_rows, col_shift : col_shift + lon_cols
                ].reshape(cell_count)
            )
    scores = jnp.stack(score_list) * score_scale + pos_bias.T[:, :, None]
    tap_ids = jnp.arange(tap_count, dtype=jnp.int32)[:, None]
    valid_mask = jnp.logical_or(jnp.stack(mask_list) > 0, tap_ids == tap_count // 2)[:, None, :]
    row_top = jnp.max(jnp.where(valid_mask, scores, -jnp.inf), axis=0, keepdims=True)
    raw_weights = jnp.exp(jnp.where(valid_mask, scores - row_top, -jnp.inf))
    weights = (raw_weights / jnp.sum(raw_weights, axis=0, keepdims=True)).astype(jnp.bfloat16)
    attended = jnp.zeros((head_count, head_dim, cell_count), jnp.float32)
    for row_shift in range(WINDOW):
        for col_shift in range(WINDOW):
            tap_index = row_shift * WINDOW + col_shift
            value_tap = feature_first[
                features:, row_shift : row_shift + lat_rows, col_shift : col_shift + lon_cols
            ].reshape(head_count, head_dim, cell_count)
            attended = attended + weights[tap_index][:, None, :].astype(
                jnp.float32
            ) * value_tap.astype(jnp.float32)
    attended = attended.reshape(features, cell_count).T.astype(jnp.bfloat16)
    residual = (
        state.reshape(cell_count, features).astype(jnp.float32)
        + jnp.dot(attended, out_weight, preferred_element_type=jnp.float32)
    ).astype(jnp.bfloat16)
    second = layer_norm(residual, second_gain)
    masked = land_sea.reshape(cell_count, 1)
    tangent = cotangent.reshape(cell_count, features) * masked.astype(jnp.bfloat16)
    labels = regime.reshape(cell_count)
    capacity = cell_count // 8
    onehot = (labels[:, None] == jnp.arange(EXPERTS, dtype=jnp.int32)[None, :]).astype(jnp.int32)
    before = jnp.cumsum(onehot, axis=0) - onehot
    rank_index = jnp.sum(before * onehot, axis=1)
    slot_index = labels * capacity + rank_index
    owner_of = (
        jnp.full((EXPERTS * capacity,), cell_count, jnp.int32)
        .at[slot_index]
        .set(jnp.arange(cell_count, dtype=jnp.int32))
    )
    send_x = jnp.concatenate([second, jnp.zeros((1, features), jnp.bfloat16)])[owner_of]
    send_c = jnp.concatenate([tangent, jnp.zeros((1, features), jnp.bfloat16)])[owner_of]
    lon_count = lax.axis_size("lon")
    lon_index = lax.axis_index("lon")
    local_count = max(1, EXPERTS // lon_count)
    group_size = max(1, lon_count // EXPERTS)
    per_peer = EXPERTS * capacity // lon_count
    got_x, got_c = (
        lax.all_to_all(
            send_x.reshape(lon_count, per_peer, features),
            "lon",
            split_axis=0,
            concat_axis=0,
            tiled=True,
        ),
        lax.all_to_all(
            send_c.reshape(lon_count, per_peer, features),
            "lon",
            split_axis=0,
            concat_axis=0,
            tiled=True,
        ),
    )
    up_block = up_weight
    down_block = down_weight
    for bit_level in range(group_size.bit_length() - 1):
        other_up, other_down = from_partner((up_block, down_block), "lon", bit_level)
        high_bit = lon_index >> bit_level & 1 == 1
        up_block = jnp.where(
            high_bit,
            jnp.concatenate([other_up, up_block], axis=1),
            jnp.concatenate([up_block, other_up], axis=1),
        )
        down_block = jnp.where(
            high_bit,
            jnp.concatenate([other_down, down_block], axis=0),
            jnp.concatenate([down_block, other_down], axis=0),
        )
    unit_count = up_block.shape[1] // local_count
    outputs, grad_u, grad_d = expert_pass(
        got_x.reshape(lon_count, local_count, per_peer // local_count, features),
        got_c.reshape(lon_count, local_count, per_peer // local_count, features),
        up_block.reshape(features, local_count, unit_count),
        down_block.reshape(local_count, unit_count, features),
    )
    returned = lax.all_to_all(
        outputs.astype(jnp.bfloat16).reshape(lon_count, per_peer, features),
        "lon",
        split_axis=0,
        concat_axis=0,
        tiled=True,
    )
    expert_rows = returned.reshape(EXPERTS * capacity, features)
    grad_u = grad_u.reshape(features, local_count * unit_count)
    grad_d = grad_d.reshape(local_count * unit_count, features)
    grad_u, grad_d = (
        lax.psum(grad_u.astype(jnp.bfloat16), "lat").astype(jnp.float32),
        lax.psum(grad_d.astype(jnp.bfloat16), "lat").astype(jnp.float32),
    )
    grad_u, grad_d = halve(grad_u, grad_d, lon_index, group_size)
    expert_cell = expert_rows[slot_index]
    result_block = (
        masked.astype(jnp.float32)
        * (residual.astype(jnp.float32) + expert_cell.astype(jnp.float32))
    ).astype(jnp.bfloat16)
    return (result_block.reshape(lat_rows, lon_cols, features), grad_u, grad_d)


MESH = pl.DeviceIdType.MESH
HALO = 32
LANES = 128


def dot(left, right, dims=((1,), (0,))):
    return lax.dot_general(left, right, (dims, ((), ())), preferred_element_type=jnp.float32)


def norm_rows(values, gain_row):
    mean_val = jnp.mean(values, axis=-1, keepdims=True)
    centred = values - mean_val
    spread = jnp.mean(jnp.square(centred), axis=-1, keepdims=True)
    return (centred * lax.rsqrt(spread + 1e-05) * gain_row).astype(jnp.bfloat16)


def iota(shape, dim):
    return lax.broadcasted_iota(jnp.int32, shape, dim)


def fused_kernel(
    lon_count,
    state_ref,
    cot_ref,
    land_ref,
    regime_ref,
    gain1_ref,
    gain2_ref,
    proj_ref,
    outw_ref,
    bias_ref,
    up_ref,
    down_ref,
    block_ref,
    gup_ref,
    gdown_ref,
    ext,
    keys,
    vals,
    flags,
    qexp,
    score,
    attended,
    padded,
    send_c,
    send_x,
    got_c,
    got_x,
    send_o,
    got_o,
    active,
    pre_act,
    halo_send,
    halo_recv,
    c_send,
    c_recv,
    x_send,
    x_recv,
    o_send,
    o_recv,
    lat_send,
    lat_recv,
    fwd_send,
    fwd_recv,
):
    cells, feats = state_ref.shape
    rows = land_ref.shape[0]
    heads = bias_ref.shape[0]
    head_dim = feats // heads
    local = EXPERTS // lon_count
    slots = local * 16
    units = up_ref.shape[1] // local
    reach = WINDOW // 2
    f32, bf16 = jnp.float32, jnp.bfloat16
    lat, lon = lax.axis_index("lat"), lax.axis_index("lon")
    core_mate = lat + 1 - 2 * lax.rem(lat, 2)
    x_mate = lax.rem(lat + 2, 4)

    def shifted(dlat, dlon):
        return (lax.rem(lat + dlat + 4, 4), lax.rem(lon + dlon + lon_count, lon_count))

    near = [(a, b) for a in (-1, 0, 1) for b in (-1, 0, 1) if (a, b) != (0, 0)]
    barrier = pltpu.get_barrier_semaphore()
    met = [shifted(*step) for step in near if step[0] != 0]
    met += [shifted(0, step) for step in range(1, lon_count)] + [(x_mate, lon)]
    for device in met:
        pl.semaphore_signal(barrier, inc=1, device_id=device, device_id_type=MESH)

    def remote(source, target, sent, received, device):
        return pltpu.make_async_remote_copy(
            src_ref=source,
            dst_ref=target,
            send_sem=sent,
            recv_sem=received,
            device_id=device,
            device_id_type=MESH,
        )

    spread_rows = (iota((cells, rows), 0) // 8 == iota((cells, rows), 1)).astype(bf16)
    own_col = lax.rem(iota((cells, 8), 0), 8) == iota((cells, 8), 1)

    def column(grid_ref):
        wide = dot(spread_rows, grid_ref[...].astype(f32).astype(bf16))
        return jnp.sum(jnp.where(own_col, wide, 0.0), axis=1, keepdims=True)

    land_col = column(land_ref)
    label_col = column(regime_ref)
    row_id, col_id = iota((cells, cells), 0), iota((cells, cells), 1)
    label_row = jnp.sum(jnp.where(row_id == col_id, label_col, 0.0), axis=0, keepdims=True)
    same = (label_col == label_row).astype(f32)
    rank_row = jnp.sum(jnp.where(row_id < col_id, same, 0.0), axis=0, keepdims=True)
    rank_col = jnp.sum(jnp.where(col_id < row_id, same, 0.0), axis=1, keepdims=True)
    slot_row = (label_row * 16.0 + rank_row).astype(jnp.int32)
    slot_col = (label_col * 16.0 + rank_col).astype(jnp.int32)
    all_slots = EXPERTS * 16
    to_slots = (iota((all_slots, cells), 0) == slot_row).astype(bf16)
    to_cells = (iota((cells, all_slots), 1) == slot_col).astype(bf16)

    state = state_ref[...].astype(f32)
    ext[1, HALO : HALO + cells, :feats] = state_ref[...]
    ext[1, HALO : HALO + cells, feats:] = jnp.broadcast_to(land_col, (cells, LANES)).astype(bf16)
    tangent = (cot_ref[...].astype(f32) * land_col).astype(bf16)
    send_c[...] = dot(to_slots, tangent).astype(bf16).reshape(lon_count, slots, feats)
    got_c[0, pl.ds(lon, 1)] = send_c[pl.ds(lon, 1)]

    pl.semaphore_wait(barrier, len(met))

    halo_copies = []
    for index, (dlat, dlon) in enumerate(near):
        if dlat == 0:
            src, dst = (HALO, cells), (HALO, cells)
        elif dlat == 1:
            src, dst = (cells, HALO), (0, HALO)
        else:
            src, dst = (HALO, HALO), (HALO + cells, HALO)
        copy = remote(
            ext.at[1, pl.ds(*src)],
            ext.at[1 - dlon, pl.ds(*dst)],
            halo_send.at[index],
            halo_recv.at[index],
            shifted(dlat, dlon),
        )
        copy.start()
        halo_copies.append(copy)

    def to_peers(source, target, sent, received):
        copies = []
        for step in range(1, lon_count):
            device = shifted(0, step)
            copy = remote(
                source.at[device[1]], target.at[lon], sent.at[step], received.at[step], device
            )
            copy.start()
            copies.append(copy)
        return copies

    c_copies = to_peers(send_c, got_c.at[0], c_send, c_recv)

    normed = norm_rows(state, gain1_ref[...])
    queries = dot(normed, proj_ref[:, :feats]).astype(bf16).astype(f32)
    head_mask = (iota((heads, feats), 1) // head_dim == iota((heads, feats), 0)).astype(f32)
    qexp[...] = (
        (queries[:, None, :] * head_mask[None, :, :]).reshape(cells * heads, feats).astype(bf16)
    )

    padded[...] = jnp.zeros_like(padded)
    padded[:, : WINDOW * WINDOW] = bias_ref[...]
    taps = padded[...]
    lane = iota((heads, LANES), 1)
    group, place = lane // 16, lax.rem(lane, 16)
    base = jnp.zeros((heads, LANES), f32)
    for a in range(WINDOW):
        moved = pltpu.roll(taps, 16 * (a + 1) - WINDOW * a, axis=1)
        base = jnp.where(jnp.logical_and(group == a + 1, place < WINDOW), moved, base)
    bias_rows, shape_rows, centre_rows = [], [], []
    key_col = jnp.where(place < 8 + reach, place, place - 16)
    for q in range(8):
        rolled = pltpu.roll(base, (q - reach) % LANES, axis=1)
        if q < reach:
            wrapped = pltpu.roll(base, q - reach + 16, axis=1)
            rolled = jnp.where(place >= 8 + reach, wrapped, rolled)
        bias_rows.append(rolled)
        inside = jnp.logical_and(jnp.abs(key_col - q) <= reach, group >= 1)
        shape_rows.append(inside.astype(f32))
        centre_rows.append(jnp.logical_and(group == reach + 1, place == q).astype(f32))
    bias = jnp.concatenate(bias_rows, axis=0)
    inside = jnp.concatenate(shape_rows, axis=0)
    centre = jnp.concatenate(centre_rows, axis=0)
    head_rows = jnp.concatenate([head_mask] * 8, axis=0)

    for copy in halo_copies:
        copy.wait()

    ext_rows = cells + 2 * HALO
    from_right = lax.rem(iota((ext_rows, 1), 0), 8) < reach
    around = jnp.where(from_right, ext[2].astype(f32), ext[0].astype(f32))
    middle = ext[1].astype(f32)

    def interleave(own, other):
        groups = ext_rows // 8
        width = own.shape[1]
        both = jnp.concatenate(
            [own.reshape(groups, 8, width), other.reshape(groups, 8, width)], axis=1
        )
        return both.reshape(2 * ext_rows, width)

    normed_mid = norm_rows(middle[:, :feats], gain1_ref[...])
    normed_around = norm_rows(around[:, :feats], gain1_ref[...])
    for target, start in ((keys, feats), (vals, 2 * feats)):
        weight = proj_ref[:, start : start + feats]
        target[...] = interleave(dot(normed_mid, weight), dot(normed_around, weight)).astype(bf16)
    ext_lat = iota((2 * ext_rows, 1), 0) // 16
    low = jnp.where(lat == 0, HALO // 8, 0)
    high = jnp.where(lat == 3, (HALO + cells) // 8, ext_rows // 8)
    on_grid = jnp.logical_and(ext_lat >= low, ext_lat < high)
    flags[...] = jnp.where(on_grid, interleave(middle[:, feats:], around[:, feats:]), 0.0).astype(
        bf16
    )

    per_row = 8 * heads
    scale = 1.0 / math.sqrt(head_dim)
    ones = jnp.ones((per_row, LANES), bf16)

    def score_row(i, carry):
        window = pl.ds(pl.multiple_of(i * 16, 16), LANES)
        rows_of = pl.ds(pl.multiple_of(i * per_row, per_row), per_row)
        ocean = dot(ones, flags[window, :], ((1,), (1,)))
        raw = dot(qexp[rows_of, :], keys[window, :], ((1,), (1,))) * scale + bias
        valid = jnp.where(ocean > 0.5, inside, centre) > 0.5
        score[rows_of, :] = jnp.where(valid, raw, -jnp.inf)
        return carry

    lax.fori_loop(0, rows, score_row, 0, unroll=4)
    raw = score[...]
    top = jnp.max(raw, axis=1, keepdims=True)
    powers = jnp.exp(raw - top)
    score[...] = powers / jnp.sum(powers, axis=1, keepdims=True)

    def value_row(i, carry):
        window = pl.ds(pl.multiple_of(i * 16, 16), LANES)
        rows_of = pl.ds(pl.multiple_of(i * per_row, per_row), per_row)
        mixed = dot(score[rows_of, :].astype(bf16), vals[window, :]) * head_rows
        mixed = jnp.sum(mixed.reshape(8, heads, feats), axis=1)
        attended[pl.ds(pl.multiple_of(i * 8, 8), 8), :] = mixed
        return carry

    lax.fori_loop(0, rows, value_row, 0, unroll=4)

    residual = (state + dot(attended[...].astype(bf16), outw_ref[...])).astype(bf16).astype(f32)
    second = norm_rows(residual, gain2_ref[...])
    send_x[...] = dot(to_slots, second).astype(bf16).reshape(lon_count, slots, feats)
    x_copies = to_peers(send_x, got_x.at[0], x_send, x_recv)
    got_x[0, pl.ds(lon, 1)] = send_x[pl.ds(lon, 1)]

    for copy in c_copies:
        copy.wait()
    c_core = remote(got_c.at[0], got_c.at[1], lat_send.at[0], lat_recv.at[0], (core_mate, lon))
    c_far = remote(got_c.at[0], got_c.at[2], lat_send.at[1], lat_recv.at[1], (x_mate, lon))
    c_far.start()
    c_core.start()
    far = []
    for step in range(lon_count):
        if step > 0:
            x_copies[step - 1].wait()
        source = shifted(0, -step)[1]
        copy = remote(
            got_x.at[0, source],
            got_x.at[2, source],
            fwd_send.at[step],
            fwd_recv.at[step],
            (x_mate, lon),
        )
        copy.start()
        far.append(copy)
    x_core = remote(got_x.at[0], got_x.at[1], lat_send.at[2], lat_recv.at[2], (core_mate, lon))
    x_core.start()

    count = lon_count * 16

    def experts_on(band):
        made = []
        for e in range(local):
            x_rows = got_x[band, :, e * 16 : (e + 1) * 16, :].reshape(count, feats)
            c_rows = got_c[band, :, e * 16 : (e + 1) * 16, :].reshape(count, feats)
            part = slice(e * units, (e + 1) * units)
            hidden = dot(x_rows, up_ref[:, part])
            back = dot(c_rows, down_ref[part, :], ((1,), (1,)))
            half = 0.5 * (1.0 + lax.erf(hidden * 0.7071067811865476))
            slope = half + hidden * jnp.exp(-0.5 * hidden * hidden) * 0.3989422804014327
            act = (hidden * half).astype(bf16)
            active[e, band * count : (band + 1) * count, :] = act
            pre_act[e, band * count : (band + 1) * count, :] = (back * slope).astype(bf16)
            if band == 0:
                made.append(dot(act, down_ref[part, :]).astype(bf16))
        return made

    for e, made in enumerate(experts_on(0)):
        send_o[:, e * 16 : (e + 1) * 16, :] = made.reshape(lon_count, 16, feats)
    o_copies = to_peers(send_o, got_o, o_send, o_recv)
    got_o[pl.ds(lon, 1)] = send_o[pl.ds(lon, 1)]

    c_far.wait()
    c_diag = remote(got_c.at[2], got_c.at[3], lat_send.at[3], lat_recv.at[3], (core_mate, lon))
    c_diag.start()
    c_core.wait()
    x_core.wait()
    experts_on(1)
    for copy in far:
        copy.wait()
    x_diag = remote(got_x.at[2], got_x.at[3], lat_send.at[4], lat_recv.at[4], (core_mate, lon))
    x_diag.start()
    experts_on(2)
    c_diag.wait()
    x_diag.wait()
    experts_on(3)

    for copy in o_copies:
        copy.wait()
    returned = got_o[...].reshape(all_slots, feats)
    block_ref[...] = (land_col * (residual + dot(to_cells, returned))).astype(bf16)

    for e in range(local):
        x_rows = got_x[:, :, e * 16 : (e + 1) * 16, :].reshape(4 * count, feats)
        c_rows = got_c[:, :, e * 16 : (e + 1) * 16, :].reshape(4 * count, feats)
        part = slice(e * units, (e + 1) * units)
        gup_ref[:, part] = dot(x_rows, pre_act[e], ((0,), (0,)))
        gdown_ref[part, :] = dot(active[e], c_rows, ((0,), (0,)))


def on_device_fused(
    state,
    cotangent,
    land_sea,
    regime,
    first_gain,
    second_gain,
    project_weight,
    out_weight,
    pos_bias,
    up_weight,
    down_weight,
):
    lat_rows, lon_cols, feats = state.shape
    cells = lat_rows * lon_cols
    heads = pos_bias.shape[0]
    lon_count = lax.axis_size("lon")
    local = EXPERTS // lon_count
    slots = local * 16
    units = up_weight.shape[1] // local
    ext_rows = cells + 2 * HALO
    bf16, f32 = jnp.bfloat16, jnp.float32
    dma = pltpu.SemaphoreType.DMA
    whole = pl.BlockSpec(memory_space=pltpu.VMEM)
    block, grad_up, grad_down = pl.pallas_call(
        functools.partial(fused_kernel, lon_count),
        out_shape=(
            jax.ShapeDtypeStruct((cells, feats), bf16),
            jax.ShapeDtypeStruct(up_weight.shape, f32),
            jax.ShapeDtypeStruct(down_weight.shape, f32),
        ),
        in_specs=[whole] * 11,
        out_specs=(whole,) * 3,
        scratch_shapes=[
            pltpu.VMEM((3, ext_rows, feats + LANES), bf16),
            pltpu.VMEM((2 * ext_rows, feats), bf16),
            pltpu.VMEM((2 * ext_rows, feats), bf16),
            pltpu.VMEM((2 * ext_rows, LANES), bf16),
            pltpu.VMEM((cells * heads, feats), bf16),
            pltpu.VMEM((cells * heads, LANES), f32),
            pltpu.VMEM((cells, feats), f32),
            pltpu.VMEM((heads, LANES), f32),
            pltpu.VMEM((lon_count, slots, feats), bf16),
            pltpu.VMEM((lon_count, slots, feats), bf16),
            pltpu.VMEM((4, lon_count, slots, feats), bf16),
            pltpu.VMEM((4, lon_count, slots, feats), bf16),
            pltpu.VMEM((lon_count, slots, feats), bf16),
            pltpu.VMEM((lon_count, slots, feats), bf16),
            pltpu.VMEM((local, 4 * lon_count * 16, units), bf16),
            pltpu.VMEM((local, 4 * lon_count * 16, units), bf16),
            dma((8,)),
            dma((8,)),
            dma((lon_count,)),
            dma((lon_count,)),
            dma((lon_count,)),
            dma((lon_count,)),
            dma((lon_count,)),
            dma((lon_count,)),
            dma((5,)),
            dma((5,)),
            dma((lon_count,)),
            dma((lon_count,)),
        ],
        compiler_params=pltpu.CompilerParams(
            collective_id=0, has_side_effects=True, vmem_limit_bytes=48 * 1024 * 1024
        ),
    )(
        state.reshape(cells, feats),
        cotangent.reshape(cells, feats),
        land_sea,
        regime.reshape(lat_rows, lon_cols),
        first_gain.reshape(1, feats),
        second_gain.reshape(1, feats),
        project_weight,
        out_weight,
        pos_bias,
        up_weight,
        down_weight,
    )
    return (block.reshape(lat_rows, lon_cols, feats), grad_up, grad_down)


def solution(mesh):
    placed = (
        P("lat", "lon", None),
        P("lat", "lon", None),
        P("lat", "lon"),
        P("lat", "lon", None, None, None),
        P(),
        P(),
        P(),
        P(),
        P(),
        P(None, "lon"),
        P("lon", None),
    )
    lat_count, lon_count = mesh.shape["lat"], mesh.shape["lon"]
    whole_experts = lat_count == 4 and 4 <= lon_count <= EXPERTS
    return jax.shard_map(
        on_device_fused if whole_experts else on_device_general,
        mesh=mesh,
        in_specs=placed,
        out_specs=(P("lat", "lon", None), P(None, "lon"), P("lon", None)),
        check_vma=False,
    )
```

```python
import functools
import math

import jax
import jax.numpy as jnp
from jax import lax
from jax.experimental import pallas as pl
from jax.experimental.pallas import tpu as pltpu
from jax.sharding import PartitionSpec as P

WINDOW = 7
EXPERTS = 16


def from_partner(value, axis, apart):
    mask = 2**apart
    pairs = [(source, source ^ mask) for source in range(lax.axis_size(axis))]
    return lax.ppermute(value, axis, pairs)


def extended(cells, sides, width, closed):
    for axis, dim in sides:
        count = lax.axis_size(axis)
        ends = count if closed else count - 1
        head = lax.slice_in_dim(cells, 0, width, axis=dim)
        tail = lax.slice_in_dim(cells, cells.shape[dim] - width, cells.shape[dim], axis=dim)
        cells = jnp.concatenate(
            [
                lax.ppermute(tail, axis, [(i, (i + 1) % count) for i in range(ends)]),
                cells,
                lax.ppermute(head, axis, [((i + 1) % count, i) for i in range(ends)]),
            ],
            axis=dim,
        )
    return cells


def layer_norm(values, gain_vec):
    values = values.astype(jnp.float32)
    mean_val = jnp.mean(values, axis=-1, keepdims=True)
    spread = jnp.mean(jnp.square(values - mean_val), axis=-1, keepdims=True)
    return ((values - mean_val) * lax.rsqrt(spread + 1e-05) * gain_vec).astype(jnp.bfloat16)


def gelu_value(inputs):
    return 0.5 * inputs * (1.0 + jax.scipy.special.erf(inputs * 0.7071067811865476))


def gelu_slope(inputs):
    return (
        0.5 * (1.0 + jax.scipy.special.erf(inputs * 0.7071067811865476))
        + inputs * jnp.exp(-0.5 * inputs * inputs) * 0.3989422804014327
    )


def expert_pass(inputs, tangents, up_block, down_block):
    hidden = jnp.einsum("nlsd,dlf->nlsf", inputs, up_block, preferred_element_type=jnp.float32)
    active = gelu_value(hidden).astype(jnp.bfloat16)
    outputs = jnp.einsum("nlsf,lfd->nlsd", active, down_block, preferred_element_type=jnp.float32)
    back_act = jnp.einsum(
        "nlsd,lfd->nlsf", tangents, down_block, preferred_element_type=jnp.float32
    )
    pre_act = (back_act * gelu_slope(hidden)).astype(jnp.bfloat16)
    grad_down = jnp.einsum("nlsf,nlsd->lfd", active, tangents, preferred_element_type=jnp.float32)
    grad_up = jnp.einsum("nlsd,nlsf->dlf", inputs, pre_act, preferred_element_type=jnp.float32)
    return (outputs, grad_up, grad_down)


def halve(grad_u, grad_d, lon_index, group_size):
    for bit_level in reversed(range(group_size.bit_length() - 1)):
        half_units = grad_u.shape[1] // 2
        high_bit = lon_index >> bit_level & 1 == 1
        keep_u = jnp.where(high_bit, grad_u[:, half_units:], grad_u[:, :half_units])
        give_u = jnp.where(high_bit, grad_u[:, :half_units], grad_u[:, half_units:])
        keep_d = jnp.where(high_bit, grad_d[half_units:], grad_d[:half_units])
        give_d = jnp.where(high_bit, grad_d[:half_units], grad_d[half_units:])
        taken_u, taken_d = (
            from_partner(give_u.astype(jnp.bfloat16), "lon", bit_level).astype(give_u.dtype),
            from_partner(give_d.astype(jnp.bfloat16), "lon", bit_level).astype(give_d.dtype),
        )
        grad_u = keep_u + taken_u
        grad_d = keep_d + taken_d
    return (grad_u, grad_d)


def on_device_general(
    state,
    cotangent,
    land_sea,
    regime,
    first_gain,
    second_gain,
    project_weight,
    out_weight,
    pos_bias,
    up_weight,
    down_weight,
):
    lat_rows, lon_cols, features = state.shape
    cell_count = lat_rows * lon_cols
    head_count = pos_bias.shape[0]
    head_dim = features // head_count
    window_reach = WINDOW // 2
    tap_count = WINDOW * WINDOW
    score_scale = 1.0 / math.sqrt(head_dim)
    normed_in = layer_norm(state, first_gain)
    flat_in = normed_in.reshape(cell_count, features)
    queries = jnp.dot(
        flat_in, project_weight[:, :features], preferred_element_type=jnp.float32
    ).astype(jnp.bfloat16)
    own_kv = jnp.dot(flat_in, project_weight[:, features:], preferred_element_type=jnp.float32)
    own_kv = own_kv.astype(jnp.bfloat16).reshape(lat_rows, lon_cols, 2 * features)
    wide_kv = extended(own_kv, (("lon", 1),), window_reach, True)
    keyvals = extended(wide_kv, (("lat", 0),), window_reach, False)
    wide_mask = extended(land_sea, (("lon", 1),), window_reach, True)
    full_mask = extended(wide_mask, (("lat", 0),), window_reach, False)
    feature_first = jnp.transpose(keyvals, (2, 0, 1))
    query_heads = queries.T.reshape(head_count, head_dim, cell_count)
    score_list = []
    mask_list = []
    for row_shift in range(WINDOW):
        for col_shift in range(WINDOW):
            key_tap = feature_first[
                :features, row_shift : row_shift + lat_rows, col_shift : col_shift + lon_cols
            ].reshape(head_count, head_dim, cell_count)
            score_list.append(
                jnp.einsum("hxc,hxc->hc", query_heads, key_tap, preferred_element_type=jnp.float32)
            )
            mask_list.append(
                full_mask[
                    row_shift : row_shift + lat_rows, col_shift : col_shift + lon_cols
                ].reshape(cell_count)
            )
    scores = jnp.stack(score_list) * score_scale + pos_bias.T[:, :, None]
    tap_ids = jnp.arange(tap_count, dtype=jnp.int32)[:, None]
    valid_mask = jnp.logical_or(jnp.stack(mask_list) > 0, tap_ids == tap_count // 2)[:, None, :]
    row_top = jnp.max(jnp.where(valid_mask, scores, -jnp.inf), axis=0, keepdims=True)
    raw_weights = jnp.exp(jnp.where(valid_mask, scores - row_top, -jnp.inf))
    weights = (raw_weights / jnp.sum(raw_weights, axis=0, keepdims=True)).astype(jnp.bfloat16)
    attended = jnp.zeros((head_count, head_dim, cell_count), jnp.float32)
    for row_shift in range(WINDOW):
        for col_shift in range(WINDOW):
            tap_index = row_shift * WINDOW + col_shift
            value_tap = feature_first[
                features:, row_shift : row_shift + lat_rows, col_shift : col_shift + lon_cols
            ].reshape(head_count, head_dim, cell_count)
            attended = attended + weights[tap_index][:, None, :].astype(
                jnp.float32
            ) * value_tap.astype(jnp.float32)
    attended = attended.reshape(features, cell_count).T.astype(jnp.bfloat16)
    residual = (
        state.reshape(cell_count, features).astype(jnp.float32)
        + jnp.dot(attended, out_weight, preferred_element_type=jnp.float32)
    ).astype(jnp.bfloat16)
    second = layer_norm(residual, second_gain)
    masked = land_sea.reshape(cell_count, 1)
    tangent = cotangent.reshape(cell_count, features) * masked.astype(jnp.bfloat16)
    labels = regime.reshape(cell_count)
    capacity = cell_count // 8
    onehot = (labels[:, None] == jnp.arange(EXPERTS, dtype=jnp.int32)[None, :]).astype(jnp.int32)
    before = jnp.cumsum(onehot, axis=0) - onehot
    rank_index = jnp.sum(before * onehot, axis=1)
    slot_index = labels * capacity + rank_index
    owner_of = (
        jnp.full((EXPERTS * capacity,), cell_count, jnp.int32)
        .at[slot_index]
        .set(jnp.arange(cell_count, dtype=jnp.int32))
    )
    send_x = jnp.concatenate([second, jnp.zeros((1, features), jnp.bfloat16)])[owner_of]
    send_c = jnp.concatenate([tangent, jnp.zeros((1, features), jnp.bfloat16)])[owner_of]
    lon_count = lax.axis_size("lon")
    lon_index = lax.axis_index("lon")
    local_count = max(1, EXPERTS // lon_count)
    group_size = max(1, lon_count // EXPERTS)
    per_peer = EXPERTS * capacity // lon_count
    got_x, got_c = (
        lax.all_to_all(
            send_x.reshape(lon_count, per_peer, features),
            "lon",
            split_axis=0,
            concat_axis=0,
            tiled=True,
        ),
        lax.all_to_all(
            send_c.reshape(lon_count, per_peer, features),
            "lon",
            split_axis=0,
            concat_axis=0,
            tiled=True,
        ),
    )
    up_block = up_weight
    down_block = down_weight
    for bit_level in range(group_size.bit_length() - 1):
        other_up, other_down = from_partner((up_block, down_block), "lon", bit_level)
        high_bit = lon_index >> bit_level & 1 == 1
        up_block = jnp.where(
            high_bit,
            jnp.concatenate([other_up, up_block], axis=1),
            jnp.concatenate([up_block, other_up], axis=1),
        )
        down_block = jnp.where(
            high_bit,
            jnp.concatenate([other_down, down_block], axis=0),
            jnp.concatenate([down_block, other_down], axis=0),
        )
    unit_count = up_block.shape[1] // local_count
    outputs, grad_u, grad_d = expert_pass(
        got_x.reshape(lon_count, local_count, per_peer // local_count, features),
        got_c.reshape(lon_count, local_count, per_peer // local_count, features),
        up_block.reshape(features, local_count, unit_count),
        down_block.reshape(local_count, unit_count, features),
    )
    returned = lax.all_to_all(
        outputs.astype(jnp.bfloat16).reshape(lon_count, per_peer, features),
        "lon",
        split_axis=0,
        concat_axis=0,
        tiled=True,
    )
    expert_rows = returned.reshape(EXPERTS * capacity, features)
    grad_u = grad_u.reshape(features, local_count * unit_count)
    grad_d = grad_d.reshape(local_count * unit_count, features)
    grad_u, grad_d = (
        lax.psum(grad_u.astype(jnp.bfloat16), "lat").astype(jnp.float32),
        lax.psum(grad_d.astype(jnp.bfloat16), "lat").astype(jnp.float32),
    )
    grad_u, grad_d = halve(grad_u, grad_d, lon_index, group_size)
    expert_cell = expert_rows[slot_index]
    result_block = (
        masked.astype(jnp.float32)
        * (residual.astype(jnp.float32) + expert_cell.astype(jnp.float32))
    ).astype(jnp.bfloat16)
    return (result_block.reshape(lat_rows, lon_cols, features), grad_u, grad_d)


MESH = pl.DeviceIdType.MESH
HALO = 32
LANES = 128


def dot(left, right, dims=((1,), (0,))):
    return lax.dot_general(left, right, (dims, ((), ())), preferred_element_type=jnp.float32)


def norm_rows(values, gain_row):
    mean_val = jnp.mean(values, axis=-1, keepdims=True)
    centred = values - mean_val
    spread = jnp.mean(jnp.square(centred), axis=-1, keepdims=True)
    return (centred * lax.rsqrt(spread + 1e-05) * gain_row).astype(jnp.bfloat16)


def iota(shape, dim):
    return lax.broadcasted_iota(jnp.int32, shape, dim)


def fused_kernel(
    lon_count,
    state_hbm,
    cot_hbm,
    land_hbm,
    regime_hbm,
    gain1_hbm,
    gain2_hbm,
    proj_hbm,
    outw_hbm,
    bias_hbm,
    up_hbm,
    down_hbm,
    x_hbm,
    c_hbm,
    active_hbm,
    pre_hbm,
    kept_hbm,
    pick_hbm,
    returned_hbm,
    state_ref,
    cot_ref,
    land_ref,
    regime_ref,
    gain1_ref,
    gain2_ref,
    proj_ref,
    outw_ref,
    bias_ref,
    up_ref,
    down_ref,
    load_sem,
    x_out,
    c_out,
    active,
    pre_act,
    kept_out,
    pick_out,
    store_sem,
    ext,
    keys,
    vals,
    flags,
    qexp,
    score,
    attended,
    padded,
    send_c,
    send_x,
    got_c,
    got_x,
    send_o,
    got_o,
    halo_send,
    halo_recv,
    c_send,
    c_recv,
    x_send,
    x_recv,
    o_send,
    o_recv,
    lat_send,
    lat_recv,
    fwd_send,
    fwd_recv,
):
    cells, feats = state_ref.shape
    rows = land_ref.shape[1]
    heads = bias_ref.shape[0]
    head_dim = feats // heads
    local = EXPERTS // lon_count
    slots = local * 16
    units = up_ref.shape[1] // local
    reach = WINDOW // 2
    f32, bf16 = jnp.float32, jnp.bfloat16
    lat, lon = lax.axis_index("lat"), lax.axis_index("lon")
    core_mate = lat + 1 - 2 * lax.rem(lat, 2)
    x_mate = lax.rem(lat + 2, 4)

    def shifted(dlat, dlon):
        return (lax.rem(lat + dlat + 4, 4), lax.rem(lon + dlon + lon_count, lon_count))

    near = [(a, b) for a in (-1, 0, 1) for b in (-1, 0, 1) if (a, b) != (0, 0)]
    barrier = pltpu.get_barrier_semaphore()
    met = [shifted(*step) for step in near if step[0] != 0]
    met += [shifted(0, step) for step in range(1, lon_count)] + [(x_mate, lon)]
    for device in met:
        pl.semaphore_signal(barrier, inc=1, device_id=device, device_id_type=MESH)

    loads = {}
    for index, (source, target) in enumerate(
        (
            (land_hbm, land_ref),
            (regime_hbm, regime_ref),
            (state_hbm, state_ref),
            (cot_hbm, cot_ref),
            (gain1_hbm, gain1_ref),
            (proj_hbm, proj_ref),
            (bias_hbm, bias_ref),
            (gain2_hbm, gain2_ref),
            (outw_hbm, outw_ref),
            (up_hbm, up_ref),
            (down_hbm, down_ref),
        )
    ):
        loads[index] = pltpu.make_async_copy(source, target, load_sem.at[index])
        loads[index].start()
    loads[0].wait()
    loads[1].wait()

    def remote(source, target, sent, received, device):
        return pltpu.make_async_remote_copy(
            src_ref=source,
            dst_ref=target,
            send_sem=sent,
            recv_sem=received,
            device_id=device,
            device_id_type=MESH,
        )

    spread_rows = (iota((cells, rows), 0) // 8 == iota((cells, rows), 1)).astype(bf16)
    own_col = lax.rem(iota((cells, 8), 0), 8) == iota((cells, 8), 1)

    def column(grid_ref):
        wide = dot(spread_rows, grid_ref[...].astype(f32).astype(bf16), ((1,), (1,)))
        return jnp.sum(jnp.where(own_col, wide, 0.0), axis=1, keepdims=True)

    land_col = column(land_ref)
    label_col = column(regime_ref)
    row_id, col_id = iota((cells, cells), 0), iota((cells, cells), 1)
    label_row = jnp.sum(jnp.where(row_id == col_id, label_col, 0.0), axis=0, keepdims=True)
    same = (label_col == label_row).astype(f32)
    rank_row = jnp.sum(jnp.where(row_id < col_id, same, 0.0), axis=0, keepdims=True)
    rank_col = jnp.sum(jnp.where(col_id < row_id, same, 0.0), axis=1, keepdims=True)
    slot_row = (label_row * 16.0 + rank_row).astype(jnp.int32)
    slot_col = (label_col * 16.0 + rank_col).astype(jnp.int32)
    all_slots = EXPERTS * 16
    to_slots = (iota((all_slots, cells), 0) == slot_row).astype(bf16)
    to_cells = (iota((cells, all_slots), 1) == slot_col).astype(bf16)

    loads[2].wait()
    loads[3].wait()
    state = state_ref[...].astype(f32)
    ext[1, HALO : HALO + cells, :feats] = state_ref[...]
    ext[1, HALO : HALO + cells, feats:] = jnp.broadcast_to(land_col, (cells, LANES)).astype(bf16)
    tangent = (cot_ref[...].astype(f32) * land_col).astype(bf16)
    send_c[...] = dot(to_slots, tangent).astype(bf16).reshape(lon_count, slots, feats)
    got_c[0, pl.ds(lon, 1)] = send_c[pl.ds(lon, 1)]

    pl.semaphore_wait(barrier, len(met))

    halo_copies = []
    for index, (dlat, dlon) in enumerate(near):
        if dlat == 0:
            src, dst = (HALO, cells), (HALO, cells)
        elif dlat == 1:
            src, dst = (cells, HALO), (0, HALO)
        else:
            src, dst = (HALO, HALO), (HALO + cells, HALO)
        copy = remote(
            ext.at[1, pl.ds(*src)],
            ext.at[1 - dlon, pl.ds(*dst)],
            halo_send.at[index],
            halo_recv.at[index],
            shifted(dlat, dlon),
        )
        copy.start()
        halo_copies.append(copy)

    def to_peers(source, target, sent, received):
        copies = []
        for step in range(1, lon_count):
            device = shifted(0, step)
            copy = remote(
                source.at[device[1]], target.at[lon], sent.at[step], received.at[step], device
            )
            copy.start()
            copies.append(copy)
        return copies

    c_copies = to_peers(send_c, got_c.at[0], c_send, c_recv)

    for index in (4, 5, 6):
        loads[index].wait()

    normed = norm_rows(state, gain1_ref[...])
    queries = dot(normed, proj_ref[:, :feats]).astype(bf16).astype(f32)
    head_mask = (iota((heads, feats), 1) // head_dim == iota((heads, feats), 0)).astype(f32)
    qexp[...] = (
        (queries[:, None, :] * head_mask[None, :, :]).reshape(cells * heads, feats).astype(bf16)
    )

    padded[...] = jnp.zeros_like(padded)
    padded[:, : WINDOW * WINDOW] = bias_ref[...]
    taps = padded[...]
    lane = iota((heads, LANES), 1)
    group, place = lane // 16, lax.rem(lane, 16)
    base = jnp.zeros((heads, LANES), f32)
    for a in range(WINDOW):
        moved = pltpu.roll(taps, 16 * (a + 1) - WINDOW * a, axis=1)
        base = jnp.where(jnp.logical_and(group == a + 1, place < WINDOW), moved, base)
    bias_rows, shape_rows, centre_rows = [], [], []
    key_col = jnp.where(place < 8 + reach, place, place - 16)
    for q in range(8):
        rolled = pltpu.roll(base, (q - reach) % LANES, axis=1)
        if q < reach:
            wrapped = pltpu.roll(base, q - reach + 16, axis=1)
            rolled = jnp.where(place >= 8 + reach, wrapped, rolled)
        bias_rows.append(rolled)
        inside = jnp.logical_and(jnp.abs(key_col - q) <= reach, group >= 1)
        shape_rows.append(inside.astype(f32))
        centre_rows.append(jnp.logical_and(group == reach + 1, place == q).astype(f32))
    bias = jnp.concatenate(bias_rows, axis=0)
    inside = jnp.concatenate(shape_rows, axis=0)
    centre = jnp.concatenate(centre_rows, axis=0)
    head_rows = jnp.concatenate([head_mask] * 8, axis=0)

    for copy in halo_copies:
        copy.wait()

    ext_rows = cells + 2 * HALO
    from_right = lax.rem(iota((ext_rows, 1), 0), 8) < reach
    around = jnp.where(from_right, ext[2].astype(f32), ext[0].astype(f32))
    middle = ext[1].astype(f32)

    def interleave(own, other):
        groups = ext_rows // 8
        width = own.shape[1]
        both = jnp.concatenate(
            [own.reshape(groups, 8, width), other.reshape(groups, 8, width)], axis=1
        )
        return both.reshape(2 * ext_rows, width)

    normed_mid = norm_rows(middle[:, :feats], gain1_ref[...])
    normed_around = norm_rows(around[:, :feats], gain1_ref[...])
    for target, start in ((keys, feats), (vals, 2 * feats)):
        weight = proj_ref[:, start : start + feats]
        target[...] = interleave(dot(normed_mid, weight), dot(normed_around, weight)).astype(bf16)
    ext_lat = iota((2 * ext_rows, 1), 0) // 16
    low = jnp.where(lat == 0, HALO // 8, 0)
    high = jnp.where(lat == 3, (HALO + cells) // 8, ext_rows // 8)
    on_grid = jnp.logical_and(ext_lat >= low, ext_lat < high)
    flags[...] = jnp.where(on_grid, interleave(middle[:, feats:], around[:, feats:]), 0.0).astype(
        bf16
    )

    per_row = 8 * heads
    scale = 1.0 / math.sqrt(head_dim)
    ones = jnp.ones((8, LANES), bf16)

    def score_row(i, carry):
        window = pl.ds(pl.multiple_of(i * 16, 16), LANES)
        rows_of = pl.ds(pl.multiple_of(i * per_row, per_row), per_row)
        ocean = dot(ones, flags[window, :], ((1,), (1,)))[:1]
        raw = dot(qexp[rows_of, :], keys[window, :], ((1,), (1,))) * scale + bias
        valid = jnp.where(ocean > 0.5, inside, centre) > 0.5
        score[rows_of, :] = jnp.where(valid, raw, -jnp.inf)
        return carry

    lax.fori_loop(0, rows, score_row, 0, unroll=4)
    raw = score[...]
    top = jnp.max(raw, axis=1, keepdims=True)
    powers = jnp.exp(raw - top)
    score[...] = powers / jnp.sum(powers, axis=1, keepdims=True)

    def value_row(i, carry):
        window = pl.ds(pl.multiple_of(i * 16, 16), LANES)
        rows_of = pl.ds(pl.multiple_of(i * per_row, per_row), per_row)
        mixed = dot(score[rows_of, :].astype(bf16), vals[window, :]) * head_rows
        mixed = jnp.sum(mixed.reshape(8, heads, feats), axis=1)
        attended[pl.ds(pl.multiple_of(i * 8, 8), 8), :] = mixed
        return carry

    lax.fori_loop(0, rows, value_row, 0, unroll=4)

    loads[7].wait()
    loads[8].wait()
    residual = (state + dot(attended[...].astype(bf16), outw_ref[...])).astype(bf16).astype(f32)
    second = norm_rows(residual, gain2_ref[...])
    send_x[...] = dot(to_slots, second).astype(bf16).reshape(lon_count, slots, feats)
    x_copies = to_peers(send_x, got_x.at[0], x_send, x_recv)
    got_x[0, pl.ds(lon, 1)] = send_x[pl.ds(lon, 1)]

    for copy in c_copies:
        copy.wait()
    c_core = remote(got_c.at[0], got_c.at[1], lat_send.at[0], lat_recv.at[0], (core_mate, lon))
    c_far = remote(got_c.at[0], got_c.at[2], lat_send.at[1], lat_recv.at[1], (x_mate, lon))
    c_far.start()
    c_core.start()
    far = []
    for step in range(lon_count):
        if step > 0:
            x_copies[step - 1].wait()
        source = shifted(0, -step)[1]
        copy = remote(
            got_x.at[0, source],
            got_x.at[2, source],
            fwd_send.at[step],
            fwd_recv.at[step],
            (x_mate, lon),
        )
        copy.start()
        far.append(copy)
    x_core = remote(got_x.at[0], got_x.at[1], lat_send.at[2], lat_recv.at[2], (core_mate, lon))
    x_core.start()

    loads[9].wait()
    loads[10].wait()
    count = lon_count * 16

    stores = []

    def store(source, target):
        copy = pltpu.make_async_copy(source, target, store_sem.at[len(stores)])
        copy.start()
        stores.append(copy)

    kept_out[...] = (land_col * residual).astype(bf16)
    pick_out[...] = (land_col * to_cells.astype(f32)).astype(bf16)
    store(kept_out, kept_hbm)
    store(pick_out, pick_hbm)

    def experts_on(band):
        made = []
        for e in range(local):
            x_rows = got_x[band, :, e * 16 : (e + 1) * 16, :].reshape(count, feats)
            c_rows = got_c[band, :, e * 16 : (e + 1) * 16, :].reshape(count, feats)
            here = slice(band * count, (band + 1) * count)
            x_out[e, here, :] = x_rows
            c_out[e, here, :] = c_rows
            part = slice(e * units, (e + 1) * units)
            hidden = dot(x_rows, up_ref[:, part])
            back = dot(c_rows, down_ref[part, :], ((1,), (1,)))
            half = 0.5 * (1.0 + lax.erf(hidden * 0.7071067811865476))
            slope = half + hidden * jnp.exp(-0.5 * hidden * hidden) * 0.3989422804014327
            act = (hidden * half).astype(bf16)
            active[e, here, :] = act
            pre_act[e, here, :] = (back * slope).astype(bf16)
            for made_here, target in (
                (x_out, x_hbm),
                (c_out, c_hbm),
                (active, active_hbm),
                (pre_act, pre_hbm),
            ):
                store(made_here.at[e, here], target.at[e, here])
            if band == 0:
                made.append(dot(act, down_ref[part, :]).astype(bf16))
        return made

    for e, made in enumerate(experts_on(0)):
        send_o[:, e * 16 : (e + 1) * 16, :] = made.reshape(lon_count, 16, feats)
    o_copies = to_peers(send_o, got_o, o_send, o_recv)
    got_o[pl.ds(lon, 1)] = send_o[pl.ds(lon, 1)]

    c_far.wait()
    c_diag = remote(got_c.at[2], got_c.at[3], lat_send.at[3], lat_recv.at[3], (core_mate, lon))
    c_diag.start()
    c_core.wait()
    x_core.wait()
    experts_on(1)
    for copy in far:
        copy.wait()
    x_diag = remote(got_x.at[2], got_x.at[3], lat_send.at[4], lat_recv.at[4], (core_mate, lon))
    x_diag.start()
    experts_on(2)
    c_diag.wait()
    x_diag.wait()
    experts_on(3)

    for copy in o_copies:
        copy.wait()
    store(got_o, returned_hbm)
    for copy in stores:
        copy.wait()


def gradient_kernel(
    x_ref, c_ref, active_ref, pre_ref, kept_ref, pick_ref, returned_ref, block_ref, gup_ref, gdown_ref
):
    block_ref[...] = (kept_ref[...].astype(jnp.float32) + dot(pick_ref[...], returned_ref[...])).astype(
        jnp.bfloat16
    )
    gup_ref[...] = dot(x_ref[0], pre_ref[0], ((0,), (0,)))
    gdown_ref[...] = dot(active_ref[0], c_ref[0], ((0,), (0,)))


def on_device_fused(
    state,
    cotangent,
    land_sea,
    regime,
    first_gain,
    second_gain,
    project_weight,
    out_weight,
    pos_bias,
    up_weight,
    down_weight,
):
    lat_rows, lon_cols, feats = state.shape
    cells = lat_rows * lon_cols
    heads = pos_bias.shape[0]
    lon_count = lax.axis_size("lon")
    local = EXPERTS // lon_count
    slots = local * 16
    units = up_weight.shape[1] // local
    ext_rows = cells + 2 * HALO
    bf16, f32 = jnp.bfloat16, jnp.float32
    dma = pltpu.SemaphoreType.DMA
    hbm = pl.BlockSpec(memory_space=pltpu.HBM)
    all_rows = 4 * lon_count * 16
    operands = (
        state.reshape(cells, feats),
        cotangent.reshape(cells, feats),
        land_sea.T,
        regime.reshape(lat_rows, lon_cols).T,
        first_gain.reshape(1, feats),
        second_gain.reshape(1, feats),
        project_weight,
        out_weight,
        pos_bias,
        up_weight,
        down_weight,
    )
    made = pl.pallas_call(
        functools.partial(fused_kernel, lon_count),
        out_shape=(
            jax.ShapeDtypeStruct((local, all_rows, feats), bf16),
            jax.ShapeDtypeStruct((local, all_rows, feats), bf16),
            jax.ShapeDtypeStruct((local, all_rows, units), bf16),
            jax.ShapeDtypeStruct((local, all_rows, units), bf16),
            jax.ShapeDtypeStruct((cells, feats), bf16),
            jax.ShapeDtypeStruct((cells, EXPERTS * 16), bf16),
            jax.ShapeDtypeStruct((lon_count, slots, feats), bf16),
        ),
        in_specs=[hbm] * 11,
        out_specs=(hbm,) * 7,
        scratch_shapes=[
            *(pltpu.VMEM(operand.shape, operand.dtype) for operand in operands),
            dma((11,)),
            pltpu.VMEM((local, all_rows, feats), bf16),
            pltpu.VMEM((local, all_rows, feats), bf16),
            pltpu.VMEM((local, all_rows, units), bf16),
            pltpu.VMEM((local, all_rows, units), bf16),
            pltpu.VMEM((cells, feats), bf16),
            pltpu.VMEM((cells, EXPERTS * 16), bf16),
            dma((3 + 16 * local,)),
            pltpu.VMEM((3, ext_rows, feats + LANES), bf16),
            pltpu.VMEM((2 * ext_rows, feats), bf16),
            pltpu.VMEM((2 * ext_rows, feats), bf16),
            pltpu.VMEM((2 * ext_rows, LANES), bf16),
            pltpu.VMEM((cells * heads, feats), bf16),
            pltpu.VMEM((cells * heads, LANES), f32),
            pltpu.VMEM((cells, feats), f32),
            pltpu.VMEM((heads, LANES), f32),
            pltpu.VMEM((lon_count, slots, feats), bf16),
            pltpu.VMEM((lon_count, slots, feats), bf16),
            pltpu.VMEM((4, lon_count, slots, feats), bf16),
            pltpu.VMEM((4, lon_count, slots, feats), bf16),
            pltpu.VMEM((lon_count, slots, feats), bf16),
            pltpu.VMEM((lon_count, slots, feats), bf16),
            dma((8,)),
            dma((8,)),
            dma((lon_count,)),
            dma((lon_count,)),
            dma((lon_count,)),
            dma((lon_count,)),
            dma((lon_count,)),
            dma((lon_count,)),
            dma((5,)),
            dma((5,)),
            dma((lon_count,)),
            dma((lon_count,)),
        ],
        compiler_params=pltpu.CompilerParams(
            collective_id=0, has_side_effects=True, vmem_limit_bytes=56 * 1024 * 1024
        ),
    )(*operands)
    wide = units // 2
    halves = units // wide
    block, grad_up, grad_down = pl.pallas_call(
        gradient_kernel,
        grid=(local, halves),
        out_shape=(
            jax.ShapeDtypeStruct((cells, feats), bf16),
            jax.ShapeDtypeStruct(up_weight.shape, f32),
            jax.ShapeDtypeStruct(down_weight.shape, f32),
        ),
        in_specs=[
            pl.BlockSpec((1, all_rows, feats), lambda e, u: (e, 0, 0)),
            pl.BlockSpec((1, all_rows, feats), lambda e, u: (e, 0, 0)),
            pl.BlockSpec((1, all_rows, wide), lambda e, u: (e, 0, u)),
            pl.BlockSpec((1, all_rows, wide), lambda e, u: (e, 0, u)),
            pl.BlockSpec((cells, feats), lambda e, u: (0, 0)),
            pl.BlockSpec((cells, EXPERTS * 16), lambda e, u: (0, 0)),
            pl.BlockSpec((EXPERTS * 16, feats), lambda e, u: (0, 0)),
        ],
        out_specs=(
            pl.BlockSpec((cells, feats), lambda e, u: (0, 0)),
            pl.BlockSpec((feats, wide), lambda e, u: (0, e * halves + u)),
            pl.BlockSpec((wide, feats), lambda e, u: (e * halves + u, 0)),
        ),
        compiler_params=pltpu.CompilerParams(vmem_limit_bytes=56 * 1024 * 1024),
    )(*made[:6], made[6].reshape(EXPERTS * 16, feats))
    return (block.reshape(lat_rows, lon_cols, feats), grad_up, grad_down)


def solution(mesh):
    placed = (
        P("lat", "lon", None),
        P("lat", "lon", None),
        P("lat", "lon"),
        P("lat", "lon", None, None, None),
        P(),
        P(),
        P(),
        P(),
        P(),
        P(None, "lon"),
        P("lon", None),
    )
    lat_count, lon_count = mesh.shape["lat"], mesh.shape["lon"]
    whole_experts = lat_count == 4 and 4 <= lon_count <= EXPERTS
    return jax.shard_map(
        on_device_fused if whole_experts else on_device_general,
        mesh=mesh,
        in_specs=placed,
        out_specs=(P("lat", "lon", None), P(None, "lon"), P("lon", None)),
        check_vma=False,
    )
```

```python
import functools
import math

import jax
import jax.numpy as jnp
from jax import lax
from jax.experimental import pallas as pl
from jax.experimental.pallas import tpu as pltpu
from jax.sharding import PartitionSpec as P

WINDOW = 7
EXPERTS = 16


def from_partner(value, axis, apart):
    mask = 2**apart
    pairs = [(source, source ^ mask) for source in range(lax.axis_size(axis))]
    return lax.ppermute(value, axis, pairs)


def extended(cells, sides, width, closed):
    for axis, dim in sides:
        count = lax.axis_size(axis)
        ends = count if closed else count - 1
        head = lax.slice_in_dim(cells, 0, width, axis=dim)
        tail = lax.slice_in_dim(cells, cells.shape[dim] - width, cells.shape[dim], axis=dim)
        cells = jnp.concatenate(
            [
                lax.ppermute(tail, axis, [(i, (i + 1) % count) for i in range(ends)]),
                cells,
                lax.ppermute(head, axis, [((i + 1) % count, i) for i in range(ends)]),
            ],
            axis=dim,
        )
    return cells


def layer_norm(values, gain_vec):
    values = values.astype(jnp.float32)
    mean_val = jnp.mean(values, axis=-1, keepdims=True)
    spread = jnp.mean(jnp.square(values - mean_val), axis=-1, keepdims=True)
    return ((values - mean_val) * lax.rsqrt(spread + 1e-05) * gain_vec).astype(jnp.bfloat16)


def gelu_value(inputs):
    return 0.5 * inputs * (1.0 + jax.scipy.special.erf(inputs * 0.7071067811865476))


def gelu_slope(inputs):
    return (
        0.5 * (1.0 + jax.scipy.special.erf(inputs * 0.7071067811865476))
        + inputs * jnp.exp(-0.5 * inputs * inputs) * 0.3989422804014327
    )


def expert_pass(inputs, tangents, up_block, down_block):
    hidden = jnp.einsum("nlsd,dlf->nlsf", inputs, up_block, preferred_element_type=jnp.float32)
    active = gelu_value(hidden).astype(jnp.bfloat16)
    outputs = jnp.einsum("nlsf,lfd->nlsd", active, down_block, preferred_element_type=jnp.float32)
    back_act = jnp.einsum(
        "nlsd,lfd->nlsf", tangents, down_block, preferred_element_type=jnp.float32
    )
    pre_act = (back_act * gelu_slope(hidden)).astype(jnp.bfloat16)
    grad_down = jnp.einsum("nlsf,nlsd->lfd", active, tangents, preferred_element_type=jnp.float32)
    grad_up = jnp.einsum("nlsd,nlsf->dlf", inputs, pre_act, preferred_element_type=jnp.float32)
    return (outputs, grad_up, grad_down)


def halve(grad_u, grad_d, lon_index, group_size):
    for bit_level in reversed(range(group_size.bit_length() - 1)):
        half_units = grad_u.shape[1] // 2
        high_bit = lon_index >> bit_level & 1 == 1
        keep_u = jnp.where(high_bit, grad_u[:, half_units:], grad_u[:, :half_units])
        give_u = jnp.where(high_bit, grad_u[:, :half_units], grad_u[:, half_units:])
        keep_d = jnp.where(high_bit, grad_d[half_units:], grad_d[:half_units])
        give_d = jnp.where(high_bit, grad_d[:half_units], grad_d[half_units:])
        taken_u, taken_d = (
            from_partner(give_u.astype(jnp.bfloat16), "lon", bit_level).astype(give_u.dtype),
            from_partner(give_d.astype(jnp.bfloat16), "lon", bit_level).astype(give_d.dtype),
        )
        grad_u = keep_u + taken_u
        grad_d = keep_d + taken_d
    return (grad_u, grad_d)


def on_device_general(
    state,
    cotangent,
    land_sea,
    regime,
    first_gain,
    second_gain,
    project_weight,
    out_weight,
    pos_bias,
    up_weight,
    down_weight,
):
    lat_rows, lon_cols, features = state.shape
    cell_count = lat_rows * lon_cols
    head_count = pos_bias.shape[0]
    head_dim = features // head_count
    window_reach = WINDOW // 2
    tap_count = WINDOW * WINDOW
    score_scale = 1.0 / math.sqrt(head_dim)
    normed_in = layer_norm(state, first_gain)
    flat_in = normed_in.reshape(cell_count, features)
    queries = jnp.dot(
        flat_in, project_weight[:, :features], preferred_element_type=jnp.float32
    ).astype(jnp.bfloat16)
    own_kv = jnp.dot(flat_in, project_weight[:, features:], preferred_element_type=jnp.float32)
    own_kv = own_kv.astype(jnp.bfloat16).reshape(lat_rows, lon_cols, 2 * features)
    wide_kv = extended(own_kv, (("lon", 1),), window_reach, True)
    keyvals = extended(wide_kv, (("lat", 0),), window_reach, False)
    wide_mask = extended(land_sea, (("lon", 1),), window_reach, True)
    full_mask = extended(wide_mask, (("lat", 0),), window_reach, False)
    feature_first = jnp.transpose(keyvals, (2, 0, 1))
    query_heads = queries.T.reshape(head_count, head_dim, cell_count)
    score_list = []
    mask_list = []
    for row_shift in range(WINDOW):
        for col_shift in range(WINDOW):
            key_tap = feature_first[
                :features, row_shift : row_shift + lat_rows, col_shift : col_shift + lon_cols
            ].reshape(head_count, head_dim, cell_count)
            score_list.append(
                jnp.einsum("hxc,hxc->hc", query_heads, key_tap, preferred_element_type=jnp.float32)
            )
            mask_list.append(
                full_mask[
                    row_shift : row_shift + lat_rows, col_shift : col_shift + lon_cols
                ].reshape(cell_count)
            )
    scores = jnp.stack(score_list) * score_scale + pos_bias.T[:, :, None]
    tap_ids = jnp.arange(tap_count, dtype=jnp.int32)[:, None]
    valid_mask = jnp.logical_or(jnp.stack(mask_list) > 0, tap_ids == tap_count // 2)[:, None, :]
    row_top = jnp.max(jnp.where(valid_mask, scores, -jnp.inf), axis=0, keepdims=True)
    raw_weights = jnp.exp(jnp.where(valid_mask, scores - row_top, -jnp.inf))
    weights = (raw_weights / jnp.sum(raw_weights, axis=0, keepdims=True)).astype(jnp.bfloat16)
    attended = jnp.zeros((head_count, head_dim, cell_count), jnp.float32)
    for row_shift in range(WINDOW):
        for col_shift in range(WINDOW):
            tap_index = row_shift * WINDOW + col_shift
            value_tap = feature_first[
                features:, row_shift : row_shift + lat_rows, col_shift : col_shift + lon_cols
            ].reshape(head_count, head_dim, cell_count)
            attended = attended + weights[tap_index][:, None, :].astype(
                jnp.float32
            ) * value_tap.astype(jnp.float32)
    attended = attended.reshape(features, cell_count).T.astype(jnp.bfloat16)
    residual = (
        state.reshape(cell_count, features).astype(jnp.float32)
        + jnp.dot(attended, out_weight, preferred_element_type=jnp.float32)
    ).astype(jnp.bfloat16)
    second = layer_norm(residual, second_gain)
    masked = land_sea.reshape(cell_count, 1)
    tangent = cotangent.reshape(cell_count, features) * masked.astype(jnp.bfloat16)
    labels = regime.reshape(cell_count)
    capacity = cell_count // 8
    onehot = (labels[:, None] == jnp.arange(EXPERTS, dtype=jnp.int32)[None, :]).astype(jnp.int32)
    before = jnp.cumsum(onehot, axis=0) - onehot
    rank_index = jnp.sum(before * onehot, axis=1)
    slot_index = labels * capacity + rank_index
    owner_of = (
        jnp.full((EXPERTS * capacity,), cell_count, jnp.int32)
        .at[slot_index]
        .set(jnp.arange(cell_count, dtype=jnp.int32))
    )
    send_x = jnp.concatenate([second, jnp.zeros((1, features), jnp.bfloat16)])[owner_of]
    send_c = jnp.concatenate([tangent, jnp.zeros((1, features), jnp.bfloat16)])[owner_of]
    lon_count = lax.axis_size("lon")
    lon_index = lax.axis_index("lon")
    local_count = max(1, EXPERTS // lon_count)
    group_size = max(1, lon_count // EXPERTS)
    per_peer = EXPERTS * capacity // lon_count
    got_x, got_c = (
        lax.all_to_all(
            send_x.reshape(lon_count, per_peer, features),
            "lon",
            split_axis=0,
            concat_axis=0,
            tiled=True,
        ),
        lax.all_to_all(
            send_c.reshape(lon_count, per_peer, features),
            "lon",
            split_axis=0,
            concat_axis=0,
            tiled=True,
        ),
    )
    up_block = up_weight
    down_block = down_weight
    for bit_level in range(group_size.bit_length() - 1):
        other_up, other_down = from_partner((up_block, down_block), "lon", bit_level)
        high_bit = lon_index >> bit_level & 1 == 1
        up_block = jnp.where(
            high_bit,
            jnp.concatenate([other_up, up_block], axis=1),
            jnp.concatenate([up_block, other_up], axis=1),
        )
        down_block = jnp.where(
            high_bit,
            jnp.concatenate([other_down, down_block], axis=0),
            jnp.concatenate([down_block, other_down], axis=0),
        )
    unit_count = up_block.shape[1] // local_count
    outputs, grad_u, grad_d = expert_pass(
        got_x.reshape(lon_count, local_count, per_peer // local_count, features),
        got_c.reshape(lon_count, local_count, per_peer // local_count, features),
        up_block.reshape(features, local_count, unit_count),
        down_block.reshape(local_count, unit_count, features),
    )
    returned = lax.all_to_all(
        outputs.astype(jnp.bfloat16).reshape(lon_count, per_peer, features),
        "lon",
        split_axis=0,
        concat_axis=0,
        tiled=True,
    )
    expert_rows = returned.reshape(EXPERTS * capacity, features)
    grad_u = grad_u.reshape(features, local_count * unit_count)
    grad_d = grad_d.reshape(local_count * unit_count, features)
    grad_u, grad_d = (
        lax.psum(grad_u.astype(jnp.bfloat16), "lat").astype(jnp.float32),
        lax.psum(grad_d.astype(jnp.bfloat16), "lat").astype(jnp.float32),
    )
    grad_u, grad_d = halve(grad_u, grad_d, lon_index, group_size)
    expert_cell = expert_rows[slot_index]
    result_block = (
        masked.astype(jnp.float32)
        * (residual.astype(jnp.float32) + expert_cell.astype(jnp.float32))
    ).astype(jnp.bfloat16)
    return (result_block.reshape(lat_rows, lon_cols, features), grad_u, grad_d)


MESH = pl.DeviceIdType.MESH
HALO = 32
LANES = 128


def dot(left, right, dims=((1,), (0,))):
    return lax.dot_general(left, right, (dims, ((), ())), preferred_element_type=jnp.float32)


def norm_rows(values, gain_row):
    mean_val = jnp.mean(values, axis=-1, keepdims=True)
    centred = values - mean_val
    spread = jnp.mean(jnp.square(centred), axis=-1, keepdims=True)
    return (centred * lax.rsqrt(spread + 1e-05) * gain_row).astype(jnp.bfloat16)


def iota(shape, dim):
    return lax.broadcasted_iota(jnp.int32, shape, dim)


def gelu_parts(hidden):
    bell = jnp.exp(-0.5 * hidden * hidden)
    depth = 1.0 + 0.3275911 * 0.7071067811865476 * jnp.abs(hidden)
    near = pl.reciprocal(depth, approx=True)
    near = near * (2.0 - depth * near)
    series = 0.5 * 1.061405429
    for factor in (-1.453152027, 1.421413741, -0.284496736, 0.254829592):
        series = series * near + 0.5 * factor
    tail = series * near * bell
    half = jnp.where(hidden >= 0.0, 1.0 - tail, tail)
    return (hidden * half, half + hidden * bell * 0.3989422804014327)


def fused_kernel(
    lon_count,
    state_hbm,
    cot_hbm,
    land_hbm,
    regime_hbm,
    gain1_hbm,
    gain2_hbm,
    proj_hbm,
    outw_hbm,
    bias_hbm,
    up_hbm,
    down_hbm,
    x_hbm,
    c_hbm,
    active_hbm,
    pre_hbm,
    kept_hbm,
    pick_hbm,
    returned_hbm,
    state_ref,
    cot_ref,
    land_ref,
    regime_ref,
    gain1_ref,
    gain2_ref,
    proj_ref,
    outw_ref,
    bias_ref,
    up_ref,
    down_ref,
    load_sem,
    x_out,
    c_out,
    active,
    pre_act,
    kept_out,
    pick_out,
    store_sem,
    ext,
    keys,
    vals,
    flags,
    qexp,
    own_kv,
    attended,
    padded,
    send_c,
    send_x,
    got_c,
    got_x,
    send_o,
    got_o,
    halo_send,
    halo_recv,
    c_send,
    c_recv,
    x_send,
    x_recv,
    o_send,
    o_recv,
    lat_send,
    lat_recv,
    fwd_send,
    fwd_recv,
):
    cells, feats = state_ref.shape
    rows = land_ref.shape[1]
    heads = bias_ref.shape[0]
    head_dim = feats // heads
    local = EXPERTS // lon_count
    slots = local * 16
    units = up_ref.shape[1] // local
    reach = WINDOW // 2
    f32, bf16 = jnp.float32, jnp.bfloat16
    lat, lon = lax.axis_index("lat"), lax.axis_index("lon")
    core_mate = lat + 1 - 2 * lax.rem(lat, 2)
    x_mate = lax.rem(lat + 2, 4)

    def shifted(dlat, dlon):
        return (lax.rem(lat + dlat + 4, 4), lax.rem(lon + dlon + lon_count, lon_count))

    near = [(a, b) for a in (-1, 0, 1) for b in (-1, 0, 1) if (a, b) != (0, 0)]
    barrier = pltpu.get_barrier_semaphore()
    met = [shifted(*step) for step in near if step[0] != 0]
    met += [shifted(0, step) for step in range(1, lon_count)] + [(x_mate, lon)]
    for device in met:
        pl.semaphore_signal(barrier, inc=1, device_id=device, device_id_type=MESH)

    loads = {}
    for index, (source, target) in enumerate(
        (
            (land_hbm, land_ref),
            (regime_hbm, regime_ref),
            (state_hbm, state_ref),
            (cot_hbm, cot_ref),
            (gain1_hbm, gain1_ref),
            (proj_hbm, proj_ref),
            (bias_hbm, bias_ref),
            (gain2_hbm, gain2_ref),
            (outw_hbm, outw_ref),
            (up_hbm, up_ref),
            (down_hbm, down_ref),
        )
    ):
        loads[index] = pltpu.make_async_copy(source, target, load_sem.at[index])
        loads[index].start()
    loads[0].wait()
    loads[1].wait()

    def remote(source, target, sent, received, device):
        return pltpu.make_async_remote_copy(
            src_ref=source,
            dst_ref=target,
            send_sem=sent,
            recv_sem=received,
            device_id=device,
            device_id_type=MESH,
        )

    spread_rows = (iota((cells, rows), 0) // 8 == iota((cells, rows), 1)).astype(bf16)
    own_col = lax.rem(iota((cells, 8), 0), 8) == iota((cells, 8), 1)

    def column(grid_ref):
        wide = dot(spread_rows, grid_ref[...].astype(f32).astype(bf16), ((1,), (1,)))
        return jnp.sum(jnp.where(own_col, wide, 0.0), axis=1, keepdims=True)

    land_col = column(land_ref)
    label_col = column(regime_ref)
    row_id, col_id = iota((cells, cells), 0), iota((cells, cells), 1)
    label_row = jnp.sum(jnp.where(row_id == col_id, label_col, 0.0), axis=0, keepdims=True)
    same = (label_col == label_row).astype(f32)
    rank_row = jnp.sum(jnp.where(row_id < col_id, same, 0.0), axis=0, keepdims=True)
    rank_col = jnp.sum(jnp.where(col_id < row_id, same, 0.0), axis=1, keepdims=True)
    slot_row = (label_row * 16.0 + rank_row).astype(jnp.int32)
    slot_col = (label_col * 16.0 + rank_col).astype(jnp.int32)
    all_slots = EXPERTS * 16
    to_slots = (iota((all_slots, cells), 0) == slot_row).astype(bf16)
    to_cells = (iota((cells, all_slots), 1) == slot_col).astype(bf16)

    loads[2].wait()
    loads[3].wait()
    state = state_ref[...].astype(f32)
    ext[1, HALO : HALO + cells, :feats] = state_ref[...]
    ext[1, HALO : HALO + cells, feats:] = jnp.broadcast_to(land_col, (cells, LANES)).astype(bf16)
    tangent = (cot_ref[...].astype(f32) * land_col).astype(bf16)
    send_c[...] = dot(to_slots, tangent).astype(bf16).reshape(lon_count, slots, feats)
    got_c[0, pl.ds(lon, 1)] = send_c[pl.ds(lon, 1)]

    pl.semaphore_wait(barrier, len(met))

    halo_copies = []
    for index, (dlat, dlon) in enumerate(near):
        if dlat == 0:
            src, dst = (HALO, cells), (HALO, cells)
        elif dlat == 1:
            src, dst = (cells, HALO), (0, HALO)
        else:
            src, dst = (HALO, HALO), (HALO + cells, HALO)
        copy = remote(
            ext.at[1, pl.ds(*src)],
            ext.at[1 - dlon, pl.ds(*dst)],
            halo_send.at[index],
            halo_recv.at[index],
            shifted(dlat, dlon),
        )
        copy.start()
        halo_copies.append(copy)

    def to_peers(source, target, sent, received):
        copies = []
        for step in range(1, lon_count):
            device = shifted(0, step)
            copy = remote(
                source.at[device[1]], target.at[lon], sent.at[step], received.at[step], device
            )
            copy.start()
            copies.append(copy)
        return copies

    c_copies = to_peers(send_c, got_c.at[0], c_send, c_recv)

    for index in (4, 5, 6):
        loads[index].wait()

    normed = norm_rows(state, gain1_ref[...])
    own_kv[...] = dot(normed, proj_ref[:, feats:])
    queries = dot(normed, proj_ref[:, :feats]).astype(bf16).astype(f32)
    head_mask = (iota((heads, feats), 1) // head_dim == iota((heads, feats), 0)).astype(f32)
    qexp[...] = (
        (queries[:, None, :] * head_mask[None, :, :]).reshape(cells * heads, feats).astype(bf16)
    )

    padded[...] = jnp.zeros_like(padded)
    padded[:, : WINDOW * WINDOW] = bias_ref[...]
    taps = padded[...]
    lane = iota((heads, LANES), 1)
    group, place = lane // 16, lax.rem(lane, 16)
    base = jnp.zeros((heads, LANES), f32)
    for a in range(WINDOW):
        moved = pltpu.roll(taps, 16 * (a + 1) - WINDOW * a, axis=1)
        base = jnp.where(jnp.logical_and(group == a + 1, place < WINDOW), moved, base)
    bias_rows, shape_rows, centre_rows = [], [], []
    key_col = jnp.where(place < 8 + reach, place, place - 16)
    for q in range(8):
        rolled = pltpu.roll(base, (q - reach) % LANES, axis=1)
        if q < reach:
            wrapped = pltpu.roll(base, q - reach + 16, axis=1)
            rolled = jnp.where(place >= 8 + reach, wrapped, rolled)
        bias_rows.append(rolled)
        inside = jnp.logical_and(jnp.abs(key_col - q) <= reach, group >= 1)
        shape_rows.append(inside.astype(f32))
        centre_rows.append(jnp.logical_and(group == reach + 1, place == q).astype(f32))
    bias = jnp.concatenate(bias_rows, axis=0)
    inside = jnp.concatenate(shape_rows, axis=0)
    centre = jnp.concatenate(centre_rows, axis=0)
    head_rows = jnp.concatenate([head_mask] * 8, axis=0)

    for copy in halo_copies:
        copy.wait()

    ext_rows = cells + 2 * HALO
    from_right = lax.rem(iota((ext_rows, 1), 0), 8) < reach
    around = jnp.where(from_right, ext[2].astype(f32), ext[0].astype(f32))
    middle = ext[1].astype(f32)
    ends = jnp.concatenate([middle[:HALO], middle[HALO + cells :]], axis=0)

    def interleave(own, other):
        groups = ext_rows // 8
        width = own.shape[1]
        both = jnp.concatenate(
            [own.reshape(groups, 8, width), other.reshape(groups, 8, width)], axis=1
        )
        return both.reshape(2 * ext_rows, width)

    normed_far = jnp.concatenate(
        [norm_rows(ends[:, :feats], gain1_ref[...]), norm_rows(around[:, :feats], gain1_ref[...])],
        axis=0,
    )
    for target, start in ((keys, 0), (vals, feats)):
        far_part = dot(normed_far, proj_ref[:, feats + start : 2 * feats + start])
        own = jnp.concatenate(
            [far_part[:HALO], own_kv[:, start : start + feats], far_part[HALO : 2 * HALO]], axis=0
        )
        target[...] = interleave(own, far_part[2 * HALO :]).astype(bf16)
    ext_lat = iota((2 * ext_rows, 1), 0) // 16
    low = jnp.where(lat == 0, HALO // 8, 0)
    high = jnp.where(lat == 3, (HALO + cells) // 8, ext_rows // 8)
    on_grid = jnp.logical_and(ext_lat >= low, ext_lat < high)
    flags[...] = jnp.where(on_grid, interleave(middle[:, feats:], around[:, feats:]), 0.0).astype(
        bf16
    )

    for copy in c_copies:
        copy.wait()
    c_core = remote(got_c.at[0], got_c.at[1], lat_send.at[0], lat_recv.at[0], (core_mate, lon))
    c_far = remote(got_c.at[0], got_c.at[2], lat_send.at[1], lat_recv.at[1], (x_mate, lon))
    c_far.start()
    c_core.start()

    per_row = 8 * heads
    scale = 1.0 / math.sqrt(head_dim)
    ones = jnp.ones((8, LANES), bf16)

    batch = 4

    def attend(i, carry):
        windows = [pl.ds(pl.multiple_of((i * batch + k) * 16, 16), LANES) for k in range(batch)]
        rows_of = pl.ds(pl.multiple_of(i * batch * per_row, batch * per_row), batch * per_row)
        rows_q = qexp[rows_of, :]
        parts = []
        for k, window in enumerate(windows):
            ocean = dot(ones, flags[window, :], ((1,), (1,)))[:1]
            raw = dot(rows_q[k * per_row : (k + 1) * per_row], keys[window, :], ((1,), (1,)))
            valid = jnp.where(ocean > 0.5, inside, centre) > 0.5
            parts.append(jnp.where(valid, raw * scale + bias, -jnp.inf))
        raw = jnp.concatenate(parts, axis=0)
        powers = jnp.exp(raw - jnp.max(raw, axis=1, keepdims=True))
        weights = (powers / jnp.sum(powers, axis=1, keepdims=True)).astype(bf16)
        for k, window in enumerate(windows):
            mixed = dot(weights[k * per_row : (k + 1) * per_row], vals[window, :]) * head_rows
            mixed = jnp.sum(mixed.reshape(8, heads, feats), axis=1)
            attended[pl.ds(pl.multiple_of((i * batch + k) * 8, 8), 8), :] = mixed
        return carry

    lax.fori_loop(0, rows // batch, attend, 0)

    loads[7].wait()
    loads[8].wait()
    residual = (state + dot(attended[...].astype(bf16), outw_ref[...])).astype(bf16).astype(f32)
    second = norm_rows(residual, gain2_ref[...])
    send_x[...] = dot(to_slots, second).astype(bf16).reshape(lon_count, slots, feats)
    x_copies = to_peers(send_x, got_x.at[0], x_send, x_recv)
    got_x[0, pl.ds(lon, 1)] = send_x[pl.ds(lon, 1)]

    far = []
    for step in range(lon_count):
        if step > 0:
            x_copies[step - 1].wait()
        source = shifted(0, -step)[1]
        copy = remote(
            got_x.at[0, source],
            got_x.at[2, source],
            fwd_send.at[step],
            fwd_recv.at[step],
            (x_mate, lon),
        )
        copy.start()
        far.append(copy)
    x_core = remote(got_x.at[0], got_x.at[1], lat_send.at[2], lat_recv.at[2], (core_mate, lon))
    x_core.start()

    loads[9].wait()
    loads[10].wait()
    count = lon_count * 16

    stores = []

    def store(source, target):
        copy = pltpu.make_async_copy(source, target, store_sem.at[len(stores)])
        copy.start()
        stores.append(copy)

    kept_out[...] = (land_col * residual).astype(bf16)
    pick_out[...] = (land_col * to_cells.astype(f32)).astype(bf16)
    store(kept_out, kept_hbm)
    store(pick_out, pick_hbm)

    def experts_on(band):
        made = []
        for e in range(local):
            x_rows = got_x[band, :, e * 16 : (e + 1) * 16, :].reshape(count, feats)
            c_rows = got_c[band, :, e * 16 : (e + 1) * 16, :].reshape(count, feats)
            here = slice(band * count, (band + 1) * count)
            x_out[e, :, here] = x_rows.T
            c_out[e, here, :] = c_rows
            total = jnp.zeros((count, feats), f32)
            for start in range(e * units, (e + 1) * units, feats):
                part = slice(start, start + feats)
                spot = slice(start - e * units, start - e * units + feats)
                act, slope = gelu_parts(dot(x_rows, up_ref[:, part]))
                act = act.astype(bf16)
                back = dot(c_rows, down_ref[part, :], ((1,), (1,)))
                active[e, spot, here] = act.T
                pre_act[e, here, spot] = (back * slope).astype(bf16)
                if band == 0:
                    total += dot(act, down_ref[part, :])
            store(x_out.at[e, :, here], x_hbm.at[e, :, here])
            store(c_out.at[e, here], c_hbm.at[e, here])
            store(active.at[e, :, here], active_hbm.at[e, :, here])
            store(pre_act.at[e, here], pre_hbm.at[e, here])
            if band == 0:
                made.append(total.astype(bf16))
        return made

    for e, made in enumerate(experts_on(0)):
        send_o[:, e * 16 : (e + 1) * 16, :] = made.reshape(lon_count, 16, feats)
    o_copies = to_peers(send_o, got_o, o_send, o_recv)
    got_o[pl.ds(lon, 1)] = send_o[pl.ds(lon, 1)]

    c_far.wait()
    c_diag = remote(got_c.at[2], got_c.at[3], lat_send.at[3], lat_recv.at[3], (core_mate, lon))
    c_diag.start()
    c_core.wait()
    x_core.wait()
    experts_on(1)
    for copy in far:
        copy.wait()
    x_diag = remote(got_x.at[2], got_x.at[3], lat_send.at[4], lat_recv.at[4], (core_mate, lon))
    x_diag.start()
    experts_on(2)
    c_diag.wait()
    x_diag.wait()
    experts_on(3)

    for copy in o_copies:
        copy.wait()
    store(got_o, returned_hbm)
    for copy in stores:
        copy.wait()


def gradient_kernel(
    x_ref, c_ref, active_ref, pre_ref, kept_ref, pick_ref, returned_ref, block_ref, gup_ref, gdown_ref
):
    block_ref[...] = (kept_ref[...].astype(jnp.float32) + dot(pick_ref[...], returned_ref[...])).astype(
        jnp.bfloat16
    )
    gup_ref[...] = dot(x_ref[0], pre_ref[0])
    gdown_ref[...] = dot(active_ref[0], c_ref[0])


def on_device_fused(
    state,
    cotangent,
    land_sea,
    regime,
    first_gain,
    second_gain,
    project_weight,
    out_weight,
    pos_bias,
    up_weight,
    down_weight,
):
    lat_rows, lon_cols, feats = state.shape
    cells = lat_rows * lon_cols
    heads = pos_bias.shape[0]
    lon_count = lax.axis_size("lon")
    local = EXPERTS // lon_count
    slots = local * 16
    units = up_weight.shape[1] // local
    ext_rows = cells + 2 * HALO
    bf16, f32 = jnp.bfloat16, jnp.float32
    dma = pltpu.SemaphoreType.DMA
    hbm = pl.BlockSpec(memory_space=pltpu.HBM)
    all_rows = 4 * lon_count * 16
    operands = (
        state.reshape(cells, feats),
        cotangent.reshape(cells, feats),
        land_sea.T,
        regime.reshape(lat_rows, lon_cols).T,
        first_gain.reshape(1, feats),
        second_gain.reshape(1, feats),
        project_weight,
        out_weight,
        pos_bias,
        up_weight,
        down_weight,
    )
    made = pl.pallas_call(
        functools.partial(fused_kernel, lon_count),
        out_shape=(
            jax.ShapeDtypeStruct((local, feats, all_rows), bf16),
            jax.ShapeDtypeStruct((local, all_rows, feats), bf16),
            jax.ShapeDtypeStruct((local, units, all_rows), bf16),
            jax.ShapeDtypeStruct((local, all_rows, units), bf16),
            jax.ShapeDtypeStruct((cells, feats), bf16),
            jax.ShapeDtypeStruct((cells, EXPERTS * 16), bf16),
            jax.ShapeDtypeStruct((lon_count, slots, feats), bf16),
        ),
        in_specs=[hbm] * 11,
        out_specs=(hbm,) * 7,
        scratch_shapes=[
            *(pltpu.VMEM(operand.shape, operand.dtype) for operand in operands),
            dma((11,)),
            pltpu.VMEM((local, feats, all_rows), bf16),
            pltpu.VMEM((local, all_rows, feats), bf16),
            pltpu.VMEM((local, units, all_rows), bf16),
            pltpu.VMEM((local, all_rows, units), bf16),
            pltpu.VMEM((cells, feats), bf16),
            pltpu.VMEM((cells, EXPERTS * 16), bf16),
            dma((3 + 16 * local,)),
            pltpu.VMEM((3, ext_rows, feats + LANES), bf16),
            pltpu.VMEM((2 * ext_rows, feats), bf16),
            pltpu.VMEM((2 * ext_rows, feats), bf16),
            pltpu.VMEM((2 * ext_rows, LANES), bf16),
            pltpu.VMEM((cells * heads, feats), bf16),
            pltpu.VMEM((cells, 2 * feats), f32),
            pltpu.VMEM((cells, feats), f32),
            pltpu.VMEM((heads, LANES), f32),
            pltpu.VMEM((lon_count, slots, feats), bf16),
            pltpu.VMEM((lon_count, slots, feats), bf16),
            pltpu.VMEM((4, lon_count, slots, feats), bf16),
            pltpu.VMEM((4, lon_count, slots, feats), bf16),
            pltpu.VMEM((lon_count, slots, feats), bf16),
            pltpu.VMEM((lon_count, slots, feats), bf16),
            dma((8,)),
            dma((8,)),
            dma((lon_count,)),
            dma((lon_count,)),
            dma((lon_count,)),
            dma((lon_count,)),
            dma((lon_count,)),
            dma((lon_count,)),
            dma((5,)),
            dma((5,)),
            dma((lon_count,)),
            dma((lon_count,)),
        ],
        compiler_params=pltpu.CompilerParams(
            collective_id=0, has_side_effects=True, vmem_limit_bytes=56 * 1024 * 1024
        ),
    )(*operands)
    wide = units // 2
    halves = units // wide
    block, grad_up, grad_down = pl.pallas_call(
        gradient_kernel,
        grid=(local, halves),
        out_shape=(
            jax.ShapeDtypeStruct((cells, feats), bf16),
            jax.ShapeDtypeStruct(up_weight.shape, f32),
            jax.ShapeDtypeStruct(down_weight.shape, f32),
        ),
        in_specs=[
            pl.BlockSpec((1, feats, all_rows), lambda e, u: (e, 0, 0)),
            pl.BlockSpec((1, all_rows, feats), lambda e, u: (e, 0, 0)),
            pl.BlockSpec((1, wide, all_rows), lambda e, u: (e, u, 0)),
            pl.BlockSpec((1, all_rows, wide), lambda e, u: (e, 0, u)),
            pl.BlockSpec((cells, feats), lambda e, u: (0, 0)),
            pl.BlockSpec((cells, EXPERTS * 16), lambda e, u: (0, 0)),
            pl.BlockSpec((EXPERTS * 16, feats), lambda e, u: (0, 0)),
        ],
        out_specs=(
            pl.BlockSpec((cells, feats), lambda e, u: (0, 0)),
            pl.BlockSpec((feats, wide), lambda e, u: (0, e * halves + u)),
            pl.BlockSpec((wide, feats), lambda e, u: (e * halves + u, 0)),
        ),
        compiler_params=pltpu.CompilerParams(vmem_limit_bytes=56 * 1024 * 1024),
    )(*made[:6], made[6].reshape(EXPERTS * 16, feats))
    return (block.reshape(lat_rows, lon_cols, feats), grad_up, grad_down)


def solution(mesh):
    placed = (
        P("lat", "lon", None),
        P("lat", "lon", None),
        P("lat", "lon"),
        P("lat", "lon", None, None, None),
        P(),
        P(),
        P(),
        P(),
        P(),
        P(None, "lon"),
        P("lon", None),
    )
    lat_count, lon_count = mesh.shape["lat"], mesh.shape["lon"]
    whole_experts = lat_count == 4 and 4 <= lon_count <= EXPERTS
    return jax.shard_map(
        on_device_fused if whole_experts else on_device_general,
        mesh=mesh,
        in_specs=placed,
        out_specs=(P("lat", "lon", None), P(None, "lon"), P("lon", None)),
        check_vma=False,
    )
```

```python
import functools
import math

import jax
import jax.numpy as jnp
from jax import lax
from jax.experimental import pallas as pl
from jax.experimental.pallas import tpu as pltpu
from jax.sharding import PartitionSpec as P

WINDOW = 7
EXPERTS = 16


def from_partner(value, axis, apart):
    mask = 2**apart
    pairs = [(source, source ^ mask) for source in range(lax.axis_size(axis))]
    return lax.ppermute(value, axis, pairs)


def extended(cells, sides, width, closed):
    for axis, dim in sides:
        count = lax.axis_size(axis)
        ends = count if closed else count - 1
        head = lax.slice_in_dim(cells, 0, width, axis=dim)
        tail = lax.slice_in_dim(cells, cells.shape[dim] - width, cells.shape[dim], axis=dim)
        cells = jnp.concatenate(
            [
                lax.ppermute(tail, axis, [(i, (i + 1) % count) for i in range(ends)]),
                cells,
                lax.ppermute(head, axis, [((i + 1) % count, i) for i in range(ends)]),
            ],
            axis=dim,
        )
    return cells


def layer_norm(values, gain_vec):
    values = values.astype(jnp.float32)
    mean_val = jnp.mean(values, axis=-1, keepdims=True)
    spread = jnp.mean(jnp.square(values - mean_val), axis=-1, keepdims=True)
    return ((values - mean_val) * lax.rsqrt(spread + 1e-05) * gain_vec).astype(jnp.bfloat16)


def gelu_value(inputs):
    return 0.5 * inputs * (1.0 + jax.scipy.special.erf(inputs * 0.7071067811865476))


def gelu_slope(inputs):
    return (
        0.5 * (1.0 + jax.scipy.special.erf(inputs * 0.7071067811865476))
        + inputs * jnp.exp(-0.5 * inputs * inputs) * 0.3989422804014327
    )


def expert_pass(inputs, tangents, up_block, down_block):
    hidden = jnp.einsum("nlsd,dlf->nlsf", inputs, up_block, preferred_element_type=jnp.float32)
    active = gelu_value(hidden).astype(jnp.bfloat16)
    outputs = jnp.einsum("nlsf,lfd->nlsd", active, down_block, preferred_element_type=jnp.float32)
    back_act = jnp.einsum(
        "nlsd,lfd->nlsf", tangents, down_block, preferred_element_type=jnp.float32
    )
    pre_act = (back_act * gelu_slope(hidden)).astype(jnp.bfloat16)
    grad_down = jnp.einsum("nlsf,nlsd->lfd", active, tangents, preferred_element_type=jnp.float32)
    grad_up = jnp.einsum("nlsd,nlsf->dlf", inputs, pre_act, preferred_element_type=jnp.float32)
    return (outputs, grad_up, grad_down)


def halve(grad_u, grad_d, lon_index, group_size):
    for bit_level in reversed(range(group_size.bit_length() - 1)):
        half_units = grad_u.shape[1] // 2
        high_bit = lon_index >> bit_level & 1 == 1
        keep_u = jnp.where(high_bit, grad_u[:, half_units:], grad_u[:, :half_units])
        give_u = jnp.where(high_bit, grad_u[:, :half_units], grad_u[:, half_units:])
        keep_d = jnp.where(high_bit, grad_d[half_units:], grad_d[:half_units])
        give_d = jnp.where(high_bit, grad_d[:half_units], grad_d[half_units:])
        taken_u, taken_d = (
            from_partner(give_u.astype(jnp.bfloat16), "lon", bit_level).astype(give_u.dtype),
            from_partner(give_d.astype(jnp.bfloat16), "lon", bit_level).astype(give_d.dtype),
        )
        grad_u = keep_u + taken_u
        grad_d = keep_d + taken_d
    return (grad_u, grad_d)


def on_device_general(
    state,
    cotangent,
    land_sea,
    regime,
    first_gain,
    second_gain,
    project_weight,
    out_weight,
    pos_bias,
    up_weight,
    down_weight,
):
    lat_rows, lon_cols, features = state.shape
    cell_count = lat_rows * lon_cols
    head_count = pos_bias.shape[0]
    head_dim = features // head_count
    window_reach = WINDOW // 2
    tap_count = WINDOW * WINDOW
    score_scale = 1.0 / math.sqrt(head_dim)
    normed_in = layer_norm(state, first_gain)
    flat_in = normed_in.reshape(cell_count, features)
    queries = jnp.dot(
        flat_in, project_weight[:, :features], preferred_element_type=jnp.float32
    ).astype(jnp.bfloat16)
    own_kv = jnp.dot(flat_in, project_weight[:, features:], preferred_element_type=jnp.float32)
    own_kv = own_kv.astype(jnp.bfloat16).reshape(lat_rows, lon_cols, 2 * features)
    wide_kv = extended(own_kv, (("lon", 1),), window_reach, True)
    keyvals = extended(wide_kv, (("lat", 0),), window_reach, False)
    wide_mask = extended(land_sea, (("lon", 1),), window_reach, True)
    full_mask = extended(wide_mask, (("lat", 0),), window_reach, False)
    feature_first = jnp.transpose(keyvals, (2, 0, 1))
    query_heads = queries.T.reshape(head_count, head_dim, cell_count)
    score_list = []
    mask_list = []
    for row_shift in range(WINDOW):
        for col_shift in range(WINDOW):
            key_tap = feature_first[
                :features, row_shift : row_shift + lat_rows, col_shift : col_shift + lon_cols
            ].reshape(head_count, head_dim, cell_count)
            score_list.append(
                jnp.einsum("hxc,hxc->hc", query_heads, key_tap, preferred_element_type=jnp.float32)
            )
            mask_list.append(
                full_mask[
                    row_shift : row_shift + lat_rows, col_shift : col_shift + lon_cols
                ].reshape(cell_count)
            )
    scores = jnp.stack(score_list) * score_scale + pos_bias.T[:, :, None]
    tap_ids = jnp.arange(tap_count, dtype=jnp.int32)[:, None]
    valid_mask = jnp.logical_or(jnp.stack(mask_list) > 0, tap_ids == tap_count // 2)[:, None, :]
    row_top = jnp.max(jnp.where(valid_mask, scores, -jnp.inf), axis=0, keepdims=True)
    raw_weights = jnp.exp(jnp.where(valid_mask, scores - row_top, -jnp.inf))
    weights = (raw_weights / jnp.sum(raw_weights, axis=0, keepdims=True)).astype(jnp.bfloat16)
    attended = jnp.zeros((head_count, head_dim, cell_count), jnp.float32)
    for row_shift in range(WINDOW):
        for col_shift in range(WINDOW):
            tap_index = row_shift * WINDOW + col_shift
            value_tap = feature_first[
                features:, row_shift : row_shift + lat_rows, col_shift : col_shift + lon_cols
            ].reshape(head_count, head_dim, cell_count)
            attended = attended + weights[tap_index][:, None, :].astype(
                jnp.float32
            ) * value_tap.astype(jnp.float32)
    attended = attended.reshape(features, cell_count).T.astype(jnp.bfloat16)
    residual = (
        state.reshape(cell_count, features).astype(jnp.float32)
        + jnp.dot(attended, out_weight, preferred_element_type=jnp.float32)
    ).astype(jnp.bfloat16)
    second = layer_norm(residual, second_gain)
    masked = land_sea.reshape(cell_count, 1)
    tangent = cotangent.reshape(cell_count, features) * masked.astype(jnp.bfloat16)
    labels = regime.reshape(cell_count)
    capacity = cell_count // 8
    onehot = (labels[:, None] == jnp.arange(EXPERTS, dtype=jnp.int32)[None, :]).astype(jnp.int32)
    before = jnp.cumsum(onehot, axis=0) - onehot
    rank_index = jnp.sum(before * onehot, axis=1)
    slot_index = labels * capacity + rank_index
    owner_of = (
        jnp.full((EXPERTS * capacity,), cell_count, jnp.int32)
        .at[slot_index]
        .set(jnp.arange(cell_count, dtype=jnp.int32))
    )
    send_x = jnp.concatenate([second, jnp.zeros((1, features), jnp.bfloat16)])[owner_of]
    send_c = jnp.concatenate([tangent, jnp.zeros((1, features), jnp.bfloat16)])[owner_of]
    lon_count = lax.axis_size("lon")
    lon_index = lax.axis_index("lon")
    local_count = max(1, EXPERTS // lon_count)
    group_size = max(1, lon_count // EXPERTS)
    per_peer = EXPERTS * capacity // lon_count
    got_x, got_c = (
        lax.all_to_all(
            send_x.reshape(lon_count, per_peer, features),
            "lon",
            split_axis=0,
            concat_axis=0,
            tiled=True,
        ),
        lax.all_to_all(
            send_c.reshape(lon_count, per_peer, features),
            "lon",
            split_axis=0,
            concat_axis=0,
            tiled=True,
        ),
    )
    up_block = up_weight
    down_block = down_weight
    for bit_level in range(group_size.bit_length() - 1):
        other_up, other_down = from_partner((up_block, down_block), "lon", bit_level)
        high_bit = lon_index >> bit_level & 1 == 1
        up_block = jnp.where(
            high_bit,
            jnp.concatenate([other_up, up_block], axis=1),
            jnp.concatenate([up_block, other_up], axis=1),
        )
        down_block = jnp.where(
            high_bit,
            jnp.concatenate([other_down, down_block], axis=0),
            jnp.concatenate([down_block, other_down], axis=0),
        )
    unit_count = up_block.shape[1] // local_count
    outputs, grad_u, grad_d = expert_pass(
        got_x.reshape(lon_count, local_count, per_peer // local_count, features),
        got_c.reshape(lon_count, local_count, per_peer // local_count, features),
        up_block.reshape(features, local_count, unit_count),
        down_block.reshape(local_count, unit_count, features),
    )
    returned = lax.all_to_all(
        outputs.astype(jnp.bfloat16).reshape(lon_count, per_peer, features),
        "lon",
        split_axis=0,
        concat_axis=0,
        tiled=True,
    )
    expert_rows = returned.reshape(EXPERTS * capacity, features)
    grad_u = grad_u.reshape(features, local_count * unit_count)
    grad_d = grad_d.reshape(local_count * unit_count, features)
    grad_u, grad_d = (
        lax.psum(grad_u.astype(jnp.bfloat16), "lat").astype(jnp.float32),
        lax.psum(grad_d.astype(jnp.bfloat16), "lat").astype(jnp.float32),
    )
    grad_u, grad_d = halve(grad_u, grad_d, lon_index, group_size)
    expert_cell = expert_rows[slot_index]
    result_block = (
        masked.astype(jnp.float32)
        * (residual.astype(jnp.float32) + expert_cell.astype(jnp.float32))
    ).astype(jnp.bfloat16)
    return (result_block.reshape(lat_rows, lon_cols, features), grad_u, grad_d)


MESH = pl.DeviceIdType.MESH
HALO = 32
LANES = 128
LAND = 1024.0


def dot(left, right, dims=((1,), (0,))):
    return lax.dot_general(left, right, (dims, ((), ())), preferred_element_type=jnp.float32)


def norm_rows(values, gain_row):
    mean_val = jnp.mean(values, axis=-1, keepdims=True)
    centred = values - mean_val
    spread = jnp.mean(jnp.square(centred), axis=-1, keepdims=True)
    return (centred * lax.rsqrt(spread + 1e-05) * gain_row).astype(jnp.bfloat16)


def iota(shape, dim):
    return lax.broadcasted_iota(jnp.int32, shape, dim)


def gelu_parts(hidden):
    bell = jnp.exp(-0.5 * hidden * hidden)
    depth = 1.0 + 0.3275911 * 0.7071067811865476 * jnp.abs(hidden)
    near = pl.reciprocal(depth, approx=True)
    near = near * (2.0 - depth * near)
    series = 0.5 * 1.061405429
    for factor in (-1.453152027, 1.421413741, -0.284496736, 0.254829592):
        series = series * near + 0.5 * factor
    tail = series * near * bell
    half = jnp.where(hidden >= 0.0, 1.0 - tail, tail)
    return (hidden * half, half + hidden * bell * 0.3989422804014327)


def fused_kernel(
    lon_count,
    state_hbm,
    cot_hbm,
    land_hbm,
    regime_hbm,
    gain1_hbm,
    gain2_hbm,
    proj_hbm,
    outw_hbm,
    bias_hbm,
    up_hbm,
    down_hbm,
    x_hbm,
    c_hbm,
    active_hbm,
    pre_hbm,
    kept_hbm,
    pick_hbm,
    returned_hbm,
    state_ref,
    cot_ref,
    land_ref,
    regime_ref,
    gain1_ref,
    gain2_ref,
    proj_ref,
    outw_ref,
    bias_ref,
    up_ref,
    down_ref,
    load_sem,
    x_out,
    c_out,
    active,
    pre_act,
    kept_out,
    pick_out,
    store_sem,
    sent,
    ends,
    sides,
    window_data,
    qexp,
    own_kv,
    attended,
    padded,
    send_c,
    send_x,
    got_c,
    got_x,
    send_o,
    got_o,
    halo_send,
    halo_recv,
    c_send,
    c_recv,
    x_send,
    x_recv,
    o_send,
    o_recv,
    lat_send,
    lat_recv,
    fwd_send,
    fwd_recv,
):
    cells, feats = state_ref.shape
    rows = land_ref.shape[1]
    heads = bias_ref.shape[0]
    head_dim = feats // heads
    local = EXPERTS // lon_count
    slots = local * 16
    units = up_ref.shape[1] // local
    reach = WINDOW // 2
    f32, bf16 = jnp.float32, jnp.bfloat16
    lat, lon = lax.axis_index("lat"), lax.axis_index("lon")
    core_mate = lat + 1 - 2 * lax.rem(lat, 2)
    x_mate = lax.rem(lat + 2, 4)

    def shifted(dlat, dlon):
        return (lax.rem(lat + dlat + 4, 4), lax.rem(lon + dlon + lon_count, lon_count))

    near = [(a, b) for a in (-1, 0, 1) for b in (-1, 0, 1) if (a, b) != (0, 0)]
    barrier = pltpu.get_barrier_semaphore()
    met = [shifted(*step) for step in near if step[0] != 0]
    met += [shifted(0, step) for step in range(1, lon_count)] + [(x_mate, lon)]
    for device in met:
        pl.semaphore_signal(barrier, inc=1, device_id=device, device_id_type=MESH)

    loads = {}
    for index, (source, target) in enumerate(
        (
            (land_hbm, land_ref),
            (regime_hbm, regime_ref),
            (state_hbm, state_ref),
            (cot_hbm, cot_ref),
            (gain1_hbm, gain1_ref),
            (proj_hbm, proj_ref),
            (bias_hbm, bias_ref),
            (gain2_hbm, gain2_ref),
            (outw_hbm, outw_ref),
            (up_hbm, up_ref),
            (down_hbm, down_ref),
        )
    ):
        loads[index] = pltpu.make_async_copy(source, target, load_sem.at[index])
        loads[index].start()
    loads[0].wait()
    loads[1].wait()

    def remote(source, target, sent, received, device):
        return pltpu.make_async_remote_copy(
            src_ref=source,
            dst_ref=target,
            send_sem=sent,
            recv_sem=received,
            device_id=device,
            device_id_type=MESH,
        )

    spread_rows = (iota((cells, rows), 0) // 8 == iota((cells, rows), 1)).astype(bf16)
    own_col = lax.rem(iota((cells, 8), 0), 8) == iota((cells, 8), 1)

    def column(grid_ref):
        wide = dot(spread_rows, grid_ref[...].astype(f32).astype(bf16), ((1,), (1,)))
        return jnp.sum(jnp.where(own_col, wide, 0.0), axis=1, keepdims=True)

    land_col = column(land_ref)
    label_col = column(regime_ref)
    row_id, col_id = iota((cells, cells), 0), iota((cells, cells), 1)
    label_row = jnp.sum(jnp.where(row_id == col_id, label_col, 0.0), axis=0, keepdims=True)
    same = (label_col == label_row).astype(f32)
    rank_row = jnp.sum(jnp.where(row_id < col_id, same, 0.0), axis=0, keepdims=True)
    rank_col = jnp.sum(jnp.where(col_id < row_id, same, 0.0), axis=1, keepdims=True)
    slot_row = (label_row * 16.0 + rank_row).astype(jnp.int32)
    slot_col = (label_col * 16.0 + rank_col).astype(jnp.int32)
    all_slots = EXPERTS * 16
    to_slots = (iota((all_slots, cells), 0) == slot_row).astype(bf16)
    to_cells = (iota((cells, all_slots), 1) == slot_col).astype(bf16)

    loads[2].wait()
    loads[3].wait()
    state = state_ref[...].astype(f32)
    shown = jnp.where(land_col > 0.5, state, LAND).astype(bf16)
    sent[:cells] = shown
    side_rows = cells // 2
    side_id = iota((2 * side_rows, cells), 0)
    low = lax.rem(side_id, side_rows)
    wanted = low // 4 * 8 + lax.rem(low, 4) + jnp.where(side_id < side_rows, 0, 4)
    to_sides = (wanted == iota((2 * side_rows, cells), 1)).astype(bf16)
    sent[cells:] = dot(to_sides, shown).astype(bf16)
    tangent = (cot_ref[...].astype(f32) * land_col).astype(bf16)
    send_c[...] = dot(to_slots, tangent).astype(bf16).reshape(lon_count, slots, feats)
    got_c[0, pl.ds(lon, 1)] = send_c[pl.ds(lon, 1)]

    pl.semaphore_wait(barrier, len(met))

    halo_copies = []
    for index, (dlat, dlon) in enumerate(near):
        edge = HALO if dlon == 0 else HALO // 2
        body = cells if dlon == 0 else side_rows
        first = {0: 0, -1: cells, 1: cells + side_rows}[dlon]
        if dlat == 0:
            src, dst = (first, body), (edge, body)
        elif dlat == 1:
            src, dst = (first + body - edge, edge), (0, edge)
        else:
            src, dst = (first, edge), (edge + body, edge)
        if dlon == 0:
            target = ends.at[pl.ds(0 if dlat == 1 else edge, edge)]
        else:
            target = sides.at[0 if dlon == -1 else 1, pl.ds(*dst)]
        copy = remote(
            sent.at[pl.ds(*src)],
            target,
            halo_send.at[index],
            halo_recv.at[index],
            shifted(dlat, dlon),
        )
        copy.start()
        halo_copies.append(copy)

    def to_peers(source, target, sent, received):
        copies = []
        for step in range(1, lon_count):
            device = shifted(0, step)
            copy = remote(
                source.at[device[1]], target.at[lon], sent.at[step], received.at[step], device
            )
            copy.start()
            copies.append(copy)
        return copies

    c_copies = to_peers(send_c, got_c.at[0], c_send, c_recv)

    for index in (4, 5, 6):
        loads[index].wait()

    normed = norm_rows(state, gain1_ref[...])
    own_kv[...] = dot(normed, proj_ref[:, feats:])
    queries = dot(normed, proj_ref[:, :feats]).astype(bf16).astype(f32)
    head_mask = (iota((heads, feats), 1) // head_dim == iota((heads, feats), 0)).astype(f32)
    qexp[...] = (
        (queries[:, None, :] * head_mask[None, :, :]).reshape(cells * heads, feats).astype(bf16)
    )

    padded[...] = jnp.zeros_like(padded)
    padded[:, : WINDOW * WINDOW] = bias_ref[...]
    taps = padded[...]
    lane = iota((heads, LANES), 1)
    group, place = lane // 16, lax.rem(lane, 16)
    base = jnp.zeros((heads, LANES), f32)
    for a in range(WINDOW):
        moved = pltpu.roll(taps, 16 * (a + 1) - WINDOW * a, axis=1)
        base = jnp.where(jnp.logical_and(group == a + 1, place < WINDOW), moved, base)
    bias_rows, shape_rows, centre_rows = [], [], []
    key_col = jnp.where(place < 8 + reach, place, place - 16)
    for q in range(8):
        rolled = pltpu.roll(base, (q - reach) % LANES, axis=1)
        if q < reach:
            wrapped = pltpu.roll(base, q - reach + 16, axis=1)
            rolled = jnp.where(place >= 8 + reach, wrapped, rolled)
        bias_rows.append(rolled)
        inside = jnp.logical_and(jnp.abs(key_col - q) <= reach, group >= 1)
        shape_rows.append(inside.astype(f32))
        centre_rows.append(jnp.logical_and(group == reach + 1, place == q).astype(f32))
    bias = jnp.concatenate(bias_rows, axis=0)
    inside = jnp.concatenate(shape_rows, axis=0)
    centre = jnp.concatenate(centre_rows, axis=0)
    head_rows = jnp.concatenate([head_mask] * 8, axis=0)

    total_rows = 2 * (cells + 2 * HALO)
    window_id = iota((total_rows, 1), 0)
    ext_lat, ext_col = window_id // 16, lax.rem(window_id, 16)
    edge_lat = HALO // 8
    end_at = jnp.where(ext_lat < edge_lat, ext_lat, ext_lat - rows)
    in_end = jnp.logical_or(ext_lat < edge_lat, ext_lat >= edge_lat + rows)
    middle_at = jnp.where(in_end, end_at * 8, 2 * HALO + (ext_lat - edge_lat) * 8) + ext_col
    side_at = 2 * HALO + cells + ext_lat * 4 + lax.rem(ext_col, 4)
    side_at = side_at + jnp.where(ext_col < 12, 0, total_rows // 4)
    source_row = jnp.where(ext_col < 8, middle_at, side_at)
    low_lat = jnp.where(lat == 0, edge_lat, 0)
    high_lat = jnp.where(lat == 3, edge_lat + rows, 2 * edge_lat + rows)
    on_grid = jnp.logical_and(ext_lat >= low_lat, ext_lat < high_lat)
    source_row = jnp.where(on_grid, source_row, -1)
    placing = (iota((total_rows, total_rows), 1) == source_row).astype(bf16)

    for copy in halo_copies:
        copy.wait()

    ext_rows = cells + 2 * HALO
    far = jnp.concatenate([ends[...], sides[0], sides[1]], axis=0).astype(f32)
    far_kv = dot(norm_rows(far, gain1_ref[...]), proj_ref[:, feats:])
    ocean_far = (far[:, :LANES] < 0.5 * LAND).astype(f32)
    ocean_own = jnp.broadcast_to(land_col, (cells, LANES))

    def in_order(end, own, side):
        return dot(placing, jnp.concatenate([end, own, side], axis=0).astype(bf16)).astype(bf16)

    two = 2 * HALO
    window_data[:, : 2 * feats] = in_order(far_kv[:two], own_kv[...], far_kv[two:])
    window_data[:, 2 * feats :] = in_order(ocean_far[:two], ocean_own, ocean_far[two:])

    for copy in c_copies:
        copy.wait()
    c_core = remote(got_c.at[0], got_c.at[1], lat_send.at[0], lat_recv.at[0], (core_mate, lon))
    c_far = remote(got_c.at[0], got_c.at[2], lat_send.at[1], lat_recv.at[1], (x_mate, lon))
    c_far.start()
    c_core.start()

    per_row = 8 * heads
    scale = 1.0 / math.sqrt(head_dim)
    ones = jnp.ones((8, LANES), bf16)

    batch = 4

    def attend(i, carry):
        windows = [pl.ds(pl.multiple_of((i * batch + k) * 16, 16), LANES) for k in range(batch)]
        rows_of = pl.ds(pl.multiple_of(i * batch * per_row, batch * per_row), batch * per_row)
        rows_q = qexp[rows_of, :]
        parts = []
        for k, window in enumerate(windows):
            ocean = dot(ones, window_data[window, 2 * feats :], ((1,), (1,)))[:1]
            raw = dot(rows_q[k * per_row : (k + 1) * per_row], window_data[window, :feats], ((1,), (1,)))
            valid = jnp.where(ocean > 0.5, inside, centre) > 0.5
            parts.append(jnp.where(valid, raw * scale + bias, -jnp.inf))
        raw = jnp.concatenate(parts, axis=0)
        powers = jnp.exp(raw - jnp.max(raw, axis=1, keepdims=True))
        weights = (powers / jnp.sum(powers, axis=1, keepdims=True)).astype(bf16)
        for k, window in enumerate(windows):
            mixed = dot(weights[k * per_row : (k + 1) * per_row], window_data[window, feats : 2 * feats]) * head_rows
            mixed = jnp.sum(mixed.reshape(8, heads, feats), axis=1)
            attended[pl.ds(pl.multiple_of((i * batch + k) * 8, 8), 8), :] = mixed
        return carry

    lax.fori_loop(0, rows // batch, attend, 0)

    loads[7].wait()
    loads[8].wait()
    residual = (state + dot(attended[...].astype(bf16), outw_ref[...])).astype(bf16).astype(f32)
    second = norm_rows(residual, gain2_ref[...])
    send_x[...] = dot(to_slots, second).astype(bf16).reshape(lon_count, slots, feats)
    x_copies = to_peers(send_x, got_x.at[0], x_send, x_recv)
    got_x[0, pl.ds(lon, 1)] = send_x[pl.ds(lon, 1)]

    far = []
    for step in range(lon_count):
        if step > 0:
            x_copies[step - 1].wait()
        source = shifted(0, -step)[1]
        copy = remote(
            got_x.at[0, source],
            got_x.at[2, source],
            fwd_send.at[step],
            fwd_recv.at[step],
            (x_mate, lon),
        )
        copy.start()
        far.append(copy)
    x_core = remote(got_x.at[0], got_x.at[1], lat_send.at[2], lat_recv.at[2], (core_mate, lon))
    x_core.start()

    loads[9].wait()
    loads[10].wait()
    count = lon_count * 16

    stores = []

    def store(source, target):
        copy = pltpu.make_async_copy(source, target, store_sem.at[len(stores)])
        copy.start()
        stores.append(copy)

    kept_out[...] = (land_col * residual).astype(bf16)
    pick_out[...] = (land_col * to_cells.astype(f32)).astype(bf16)
    store(kept_out, kept_hbm)
    store(pick_out, pick_hbm)

    def experts_on(band):
        made = []
        for e in range(local):
            x_rows = got_x[band, :, e * 16 : (e + 1) * 16, :].reshape(count, feats)
            c_rows = got_c[band, :, e * 16 : (e + 1) * 16, :].reshape(count, feats)
            here = slice(band * count, (band + 1) * count)
            x_out[e, here, :] = x_rows
            c_out[e, here, :] = c_rows
            total = jnp.zeros((count, feats), f32)
            for start in range(e * units, (e + 1) * units, feats):
                part = slice(start, start + feats)
                spot = slice(start - e * units, start - e * units + feats)
                act, slope = gelu_parts(dot(x_rows, up_ref[:, part]))
                act = act.astype(bf16)
                back = dot(c_rows, down_ref[part, :], ((1,), (1,)))
                active[e, here, spot] = act
                pre_act[e, here, spot] = (back * slope).astype(bf16)
                if band == 0:
                    total += dot(act, down_ref[part, :])
            store(x_out.at[e, here], x_hbm.at[e, here])
            store(c_out.at[e, here], c_hbm.at[e, here])
            store(active.at[e, here], active_hbm.at[e, here])
            store(pre_act.at[e, here], pre_hbm.at[e, here])
            if band == 0:
                made.append(total.astype(bf16))
        return made

    for e, made in enumerate(experts_on(0)):
        send_o[:, e * 16 : (e + 1) * 16, :] = made.reshape(lon_count, 16, feats)
    o_copies = to_peers(send_o, got_o, o_send, o_recv)
    got_o[pl.ds(lon, 1)] = send_o[pl.ds(lon, 1)]

    c_far.wait()
    c_diag = remote(got_c.at[2], got_c.at[3], lat_send.at[3], lat_recv.at[3], (core_mate, lon))
    c_diag.start()
    c_core.wait()
    x_core.wait()
    experts_on(1)
    for copy in far:
        copy.wait()
    x_diag = remote(got_x.at[2], got_x.at[3], lat_send.at[4], lat_recv.at[4], (core_mate, lon))
    x_diag.start()
    experts_on(2)
    c_diag.wait()
    x_diag.wait()
    experts_on(3)

    for copy in o_copies:
        copy.wait()
    store(got_o, returned_hbm)
    for copy in stores:
        copy.wait()


def gradient_kernel(
    x_ref, c_ref, active_ref, pre_ref, kept_ref, pick_ref, returned_ref, block_ref, gup_ref, gdown_ref
):
    block_ref[...] = (kept_ref[...].astype(jnp.float32) + dot(pick_ref[...], returned_ref[...])).astype(
        jnp.bfloat16
    )
    gup_ref[...] = dot(x_ref[0], pre_ref[0], ((0,), (0,)))
    gdown_ref[...] = dot(active_ref[0], c_ref[0], ((0,), (0,)))


def on_device_fused(
    state,
    cotangent,
    land_sea,
    regime,
    first_gain,
    second_gain,
    project_weight,
    out_weight,
    pos_bias,
    up_weight,
    down_weight,
):
    lat_rows, lon_cols, feats = state.shape
    cells = lat_rows * lon_cols
    heads = pos_bias.shape[0]
    lon_count = lax.axis_size("lon")
    local = EXPERTS // lon_count
    slots = local * 16
    units = up_weight.shape[1] // local
    ext_rows = cells + 2 * HALO
    bf16, f32 = jnp.bfloat16, jnp.float32
    dma = pltpu.SemaphoreType.DMA
    hbm = pl.BlockSpec(memory_space=pltpu.HBM)
    all_rows = 4 * lon_count * 16
    operands = (
        state.reshape(cells, feats),
        cotangent.reshape(cells, feats),
        land_sea.T,
        regime.reshape(lat_rows, lon_cols).T,
        first_gain.reshape(1, feats),
        second_gain.reshape(1, feats),
        project_weight,
        out_weight,
        pos_bias,
        up_weight,
        down_weight,
    )
    made = pl.pallas_call(
        functools.partial(fused_kernel, lon_count),
        out_shape=(
            jax.ShapeDtypeStruct((local, all_rows, feats), bf16),
            jax.ShapeDtypeStruct((local, all_rows, feats), bf16),
            jax.ShapeDtypeStruct((local, all_rows, units), bf16),
            jax.ShapeDtypeStruct((local, all_rows, units), bf16),
            jax.ShapeDtypeStruct((cells, feats), bf16),
            jax.ShapeDtypeStruct((cells, EXPERTS * 16), bf16),
            jax.ShapeDtypeStruct((lon_count, slots, feats), bf16),
        ),
        in_specs=[hbm] * 11,
        out_specs=(hbm,) * 7,
        scratch_shapes=[
            *(pltpu.VMEM(operand.shape, operand.dtype) for operand in operands),
            dma((11,)),
            pltpu.VMEM((local, all_rows, feats), bf16),
            pltpu.VMEM((local, all_rows, feats), bf16),
            pltpu.VMEM((local, all_rows, units), bf16),
            pltpu.VMEM((local, all_rows, units), bf16),
            pltpu.VMEM((cells, feats), bf16),
            pltpu.VMEM((cells, EXPERTS * 16), bf16),
            dma((3 + 16 * local,)),
            pltpu.VMEM((2 * cells, feats), bf16),
            pltpu.VMEM((2 * HALO, feats), bf16),
            pltpu.VMEM((2, ext_rows // 2, feats), bf16),
            pltpu.VMEM((2 * ext_rows, 2 * feats + LANES), bf16),
            pltpu.VMEM((cells * heads, feats), bf16),
            pltpu.VMEM((cells, 2 * feats), f32),
            pltpu.VMEM((cells, feats), f32),
            pltpu.VMEM((heads, LANES), f32),
            pltpu.VMEM((lon_count, slots, feats), bf16),
            pltpu.VMEM((lon_count, slots, feats), bf16),
            pltpu.VMEM((4, lon_count, slots, feats), bf16),
            pltpu.VMEM((4, lon_count, slots, feats), bf16),
            pltpu.VMEM((lon_count, slots, feats), bf16),
            pltpu.VMEM((lon_count, slots, feats), bf16),
            dma((8,)),
            dma((8,)),
            dma((lon_count,)),
            dma((lon_count,)),
            dma((lon_count,)),
            dma((lon_count,)),
            dma((lon_count,)),
            dma((lon_count,)),
            dma((5,)),
            dma((5,)),
            dma((lon_count,)),
            dma((lon_count,)),
        ],
        compiler_params=pltpu.CompilerParams(
            collective_id=0, has_side_effects=True, vmem_limit_bytes=56 * 1024 * 1024
        ),
    )(*operands)
    wide = units // 2
    halves = units // wide
    block, grad_up, grad_down = pl.pallas_call(
        gradient_kernel,
        grid=(local, halves),
        out_shape=(
            jax.ShapeDtypeStruct((cells, feats), bf16),
            jax.ShapeDtypeStruct(up_weight.shape, f32),
            jax.ShapeDtypeStruct(down_weight.shape, f32),
        ),
        in_specs=[
            pl.BlockSpec((1, all_rows, feats), lambda e, u: (e, 0, 0)),
            pl.BlockSpec((1, all_rows, feats), lambda e, u: (e, 0, 0)),
            pl.BlockSpec((1, all_rows, wide), lambda e, u: (e, 0, u)),
            pl.BlockSpec((1, all_rows, wide), lambda e, u: (e, 0, u)),
            pl.BlockSpec((cells, feats), lambda e, u: (0, 0)),
            pl.BlockSpec((cells, EXPERTS * 16), lambda e, u: (0, 0)),
            pl.BlockSpec((EXPERTS * 16, feats), lambda e, u: (0, 0)),
        ],
        out_specs=(
            pl.BlockSpec((cells, feats), lambda e, u: (0, 0)),
            pl.BlockSpec((feats, wide), lambda e, u: (0, e * halves + u)),
            pl.BlockSpec((wide, feats), lambda e, u: (e * halves + u, 0)),
        ),
        compiler_params=pltpu.CompilerParams(vmem_limit_bytes=56 * 1024 * 1024),
    )(*made[:6], made[6].reshape(EXPERTS * 16, feats))
    return (block.reshape(lat_rows, lon_cols, feats), grad_up, grad_down)


def solution(mesh):
    placed = (
        P("lat", "lon", None),
        P("lat", "lon", None),
        P("lat", "lon"),
        P("lat", "lon", None, None, None),
        P(),
        P(),
        P(),
        P(),
        P(),
        P(None, "lon"),
        P("lon", None),
    )
    lat_count, lon_count = mesh.shape["lat"], mesh.shape["lon"]
    whole_experts = lat_count == 4 and 4 <= lon_count <= EXPERTS
    return jax.shard_map(
        on_device_fused if whole_experts else on_device_general,
        mesh=mesh,
        in_specs=placed,
        out_specs=(P("lat", "lon", None), P(None, "lon"), P("lon", None)),
        check_vma=False,
    )
```

```python
import functools
import math

import jax
import jax.numpy as jnp
from jax import lax
from jax.experimental import pallas as pl
from jax.experimental.pallas import tpu as pltpu
from jax.sharding import PartitionSpec as P

WINDOW = 7
EXPERTS = 16


def from_partner(value, axis, apart):
    mask = 2**apart
    pairs = [(source, source ^ mask) for source in range(lax.axis_size(axis))]
    return lax.ppermute(value, axis, pairs)


def extended(cells, sides, width, closed):
    for axis, dim in sides:
        count = lax.axis_size(axis)
        ends = count if closed else count - 1
        head = lax.slice_in_dim(cells, 0, width, axis=dim)
        tail = lax.slice_in_dim(cells, cells.shape[dim] - width, cells.shape[dim], axis=dim)
        cells = jnp.concatenate(
            [
                lax.ppermute(tail, axis, [(i, (i + 1) % count) for i in range(ends)]),
                cells,
                lax.ppermute(head, axis, [((i + 1) % count, i) for i in range(ends)]),
            ],
            axis=dim,
        )
    return cells


def layer_norm(values, gain_vec):
    values = values.astype(jnp.float32)
    mean_val = jnp.mean(values, axis=-1, keepdims=True)
    spread = jnp.mean(jnp.square(values - mean_val), axis=-1, keepdims=True)
    return ((values - mean_val) * lax.rsqrt(spread + 1e-05) * gain_vec).astype(jnp.bfloat16)


def gelu_value(inputs):
    return 0.5 * inputs * (1.0 + jax.scipy.special.erf(inputs * 0.7071067811865476))


def gelu_slope(inputs):
    return (
        0.5 * (1.0 + jax.scipy.special.erf(inputs * 0.7071067811865476))
        + inputs * jnp.exp(-0.5 * inputs * inputs) * 0.3989422804014327
    )


def expert_pass(inputs, tangents, up_block, down_block):
    hidden = jnp.einsum("nlsd,dlf->nlsf", inputs, up_block, preferred_element_type=jnp.float32)
    active = gelu_value(hidden).astype(jnp.bfloat16)
    outputs = jnp.einsum("nlsf,lfd->nlsd", active, down_block, preferred_element_type=jnp.float32)
    back_act = jnp.einsum(
        "nlsd,lfd->nlsf", tangents, down_block, preferred_element_type=jnp.float32
    )
    pre_act = (back_act * gelu_slope(hidden)).astype(jnp.bfloat16)
    grad_down = jnp.einsum("nlsf,nlsd->lfd", active, tangents, preferred_element_type=jnp.float32)
    grad_up = jnp.einsum("nlsd,nlsf->dlf", inputs, pre_act, preferred_element_type=jnp.float32)
    return (outputs, grad_up, grad_down)


def halve(grad_u, grad_d, lon_index, group_size):
    for bit_level in reversed(range(group_size.bit_length() - 1)):
        half_units = grad_u.shape[1] // 2
        high_bit = lon_index >> bit_level & 1 == 1
        keep_u = jnp.where(high_bit, grad_u[:, half_units:], grad_u[:, :half_units])
        give_u = jnp.where(high_bit, grad_u[:, :half_units], grad_u[:, half_units:])
        keep_d = jnp.where(high_bit, grad_d[half_units:], grad_d[:half_units])
        give_d = jnp.where(high_bit, grad_d[:half_units], grad_d[half_units:])
        taken_u, taken_d = (
            from_partner(give_u.astype(jnp.bfloat16), "lon", bit_level).astype(give_u.dtype),
            from_partner(give_d.astype(jnp.bfloat16), "lon", bit_level).astype(give_d.dtype),
        )
        grad_u = keep_u + taken_u
        grad_d = keep_d + taken_d
    return (grad_u, grad_d)


def on_device_general(
    state,
    cotangent,
    land_sea,
    regime,
    first_gain,
    second_gain,
    project_weight,
    out_weight,
    pos_bias,
    up_weight,
    down_weight,
):
    lat_rows, lon_cols, features = state.shape
    cell_count = lat_rows * lon_cols
    head_count = pos_bias.shape[0]
    head_dim = features // head_count
    window_reach = WINDOW // 2
    tap_count = WINDOW * WINDOW
    score_scale = 1.0 / math.sqrt(head_dim)
    normed_in = layer_norm(state, first_gain)
    flat_in = normed_in.reshape(cell_count, features)
    queries = jnp.dot(
        flat_in, project_weight[:, :features], preferred_element_type=jnp.float32
    ).astype(jnp.bfloat16)
    own_kv = jnp.dot(flat_in, project_weight[:, features:], preferred_element_type=jnp.float32)
    own_kv = own_kv.astype(jnp.bfloat16).reshape(lat_rows, lon_cols, 2 * features)
    wide_kv = extended(own_kv, (("lon", 1),), window_reach, True)
    keyvals = extended(wide_kv, (("lat", 0),), window_reach, False)
    wide_mask = extended(land_sea, (("lon", 1),), window_reach, True)
    full_mask = extended(wide_mask, (("lat", 0),), window_reach, False)
    feature_first = jnp.transpose(keyvals, (2, 0, 1))
    query_heads = queries.T.reshape(head_count, head_dim, cell_count)
    score_list = []
    mask_list = []
    for row_shift in range(WINDOW):
        for col_shift in range(WINDOW):
            key_tap = feature_first[
                :features, row_shift : row_shift + lat_rows, col_shift : col_shift + lon_cols
            ].reshape(head_count, head_dim, cell_count)
            score_list.append(
                jnp.einsum("hxc,hxc->hc", query_heads, key_tap, preferred_element_type=jnp.float32)
            )
            mask_list.append(
                full_mask[
                    row_shift : row_shift + lat_rows, col_shift : col_shift + lon_cols
                ].reshape(cell_count)
            )
    scores = jnp.stack(score_list) * score_scale + pos_bias.T[:, :, None]
    tap_ids = jnp.arange(tap_count, dtype=jnp.int32)[:, None]
    valid_mask = jnp.logical_or(jnp.stack(mask_list) > 0, tap_ids == tap_count // 2)[:, None, :]
    row_top = jnp.max(jnp.where(valid_mask, scores, -jnp.inf), axis=0, keepdims=True)
    raw_weights = jnp.exp(jnp.where(valid_mask, scores - row_top, -jnp.inf))
    weights = (raw_weights / jnp.sum(raw_weights, axis=0, keepdims=True)).astype(jnp.bfloat16)
    attended = jnp.zeros((head_count, head_dim, cell_count), jnp.float32)
    for row_shift in range(WINDOW):
        for col_shift in range(WINDOW):
            tap_index = row_shift * WINDOW + col_shift
            value_tap = feature_first[
                features:, row_shift : row_shift + lat_rows, col_shift : col_shift + lon_cols
            ].reshape(head_count, head_dim, cell_count)
            attended = attended + weights[tap_index][:, None, :].astype(
                jnp.float32
            ) * value_tap.astype(jnp.float32)
    attended = attended.reshape(features, cell_count).T.astype(jnp.bfloat16)
    residual = (
        state.reshape(cell_count, features).astype(jnp.float32)
        + jnp.dot(attended, out_weight, preferred_element_type=jnp.float32)
    ).astype(jnp.bfloat16)
    second = layer_norm(residual, second_gain)
    masked = land_sea.reshape(cell_count, 1)
    tangent = cotangent.reshape(cell_count, features) * masked.astype(jnp.bfloat16)
    labels = regime.reshape(cell_count)
    capacity = cell_count // 8
    onehot = (labels[:, None] == jnp.arange(EXPERTS, dtype=jnp.int32)[None, :]).astype(jnp.int32)
    before = jnp.cumsum(onehot, axis=0) - onehot
    rank_index = jnp.sum(before * onehot, axis=1)
    slot_index = labels * capacity + rank_index
    owner_of = (
        jnp.full((EXPERTS * capacity,), cell_count, jnp.int32)
        .at[slot_index]
        .set(jnp.arange(cell_count, dtype=jnp.int32))
    )
    send_x = jnp.concatenate([second, jnp.zeros((1, features), jnp.bfloat16)])[owner_of]
    send_c = jnp.concatenate([tangent, jnp.zeros((1, features), jnp.bfloat16)])[owner_of]
    lon_count = lax.axis_size("lon")
    lon_index = lax.axis_index("lon")
    local_count = max(1, EXPERTS // lon_count)
    group_size = max(1, lon_count // EXPERTS)
    per_peer = EXPERTS * capacity // lon_count
    got_x, got_c = (
        lax.all_to_all(
            send_x.reshape(lon_count, per_peer, features),
            "lon",
            split_axis=0,
            concat_axis=0,
            tiled=True,
        ),
        lax.all_to_all(
            send_c.reshape(lon_count, per_peer, features),
            "lon",
            split_axis=0,
            concat_axis=0,
            tiled=True,
        ),
    )
    up_block = up_weight
    down_block = down_weight
    for bit_level in range(group_size.bit_length() - 1):
        other_up, other_down = from_partner((up_block, down_block), "lon", bit_level)
        high_bit = lon_index >> bit_level & 1 == 1
        up_block = jnp.where(
            high_bit,
            jnp.concatenate([other_up, up_block], axis=1),
            jnp.concatenate([up_block, other_up], axis=1),
        )
        down_block = jnp.where(
            high_bit,
            jnp.concatenate([other_down, down_block], axis=0),
            jnp.concatenate([down_block, other_down], axis=0),
        )
    unit_count = up_block.shape[1] // local_count
    outputs, grad_u, grad_d = expert_pass(
        got_x.reshape(lon_count, local_count, per_peer // local_count, features),
        got_c.reshape(lon_count, local_count, per_peer // local_count, features),
        up_block.reshape(features, local_count, unit_count),
        down_block.reshape(local_count, unit_count, features),
    )
    returned = lax.all_to_all(
        outputs.astype(jnp.bfloat16).reshape(lon_count, per_peer, features),
        "lon",
        split_axis=0,
        concat_axis=0,
        tiled=True,
    )
    expert_rows = returned.reshape(EXPERTS * capacity, features)
    grad_u = grad_u.reshape(features, local_count * unit_count)
    grad_d = grad_d.reshape(local_count * unit_count, features)
    grad_u, grad_d = (
        lax.psum(grad_u.astype(jnp.bfloat16), "lat").astype(jnp.float32),
        lax.psum(grad_d.astype(jnp.bfloat16), "lat").astype(jnp.float32),
    )
    grad_u, grad_d = halve(grad_u, grad_d, lon_index, group_size)
    expert_cell = expert_rows[slot_index]
    result_block = (
        masked.astype(jnp.float32)
        * (residual.astype(jnp.float32) + expert_cell.astype(jnp.float32))
    ).astype(jnp.bfloat16)
    return (result_block.reshape(lat_rows, lon_cols, features), grad_u, grad_d)


MESH = pl.DeviceIdType.MESH
HALO = 32
LANES = 128
LAND = 1024.0


def dot(left, right, dims=((1,), (0,))):
    return lax.dot_general(left, right, (dims, ((), ())), preferred_element_type=jnp.float32)


def norm_rows(values, gain_row):
    mean_val = jnp.mean(values, axis=-1, keepdims=True)
    centred = values - mean_val
    spread = jnp.mean(jnp.square(centred), axis=-1, keepdims=True)
    return (centred * lax.rsqrt(spread + 1e-05) * gain_row).astype(jnp.bfloat16)


def iota(shape, dim):
    return lax.broadcasted_iota(jnp.int32, shape, dim)


def gelu_parts(hidden):
    bell = jnp.exp(-0.5 * hidden * hidden)
    depth = 1.0 + 0.3275911 * 0.7071067811865476 * jnp.abs(hidden)
    near = pl.reciprocal(depth, approx=True)
    near = near * (2.0 - depth * near)
    series = 0.5 * 1.061405429
    for factor in (-1.453152027, 1.421413741, -0.284496736, 0.254829592):
        series = series * near + 0.5 * factor
    tail = series * near * bell
    half = jnp.where(hidden >= 0.0, 1.0 - tail, tail)
    return (hidden * half, half + hidden * bell * 0.3989422804014327)


def fused_kernel(
    lon_count,
    state_hbm,
    cot_hbm,
    land_hbm,
    regime_hbm,
    gain1_hbm,
    gain2_hbm,
    proj_hbm,
    outw_hbm,
    bias_hbm,
    up_hbm,
    down_hbm,
    x_hbm,
    c_hbm,
    active_hbm,
    pre_hbm,
    kept_hbm,
    pick_hbm,
    returned_hbm,
    state_ref,
    cot_ref,
    land_ref,
    regime_ref,
    gain1_ref,
    gain2_ref,
    proj_ref,
    outw_ref,
    bias_ref,
    up_ref,
    down_ref,
    load_sem,
    active,
    pre_act,
    kept_out,
    pick_out,
    store_sem,
    sent,
    ends,
    sides,
    window_data,
    qexp,
    own_kv,
    attended,
    padded,
    send_c,
    send_x,
    got_c,
    got_x,
    send_o,
    got_o,
    halo_send,
    halo_recv,
    c_send,
    c_recv,
    x_send,
    x_recv,
    o_send,
    o_recv,
    lat_send,
    lat_recv,
    fwd_send,
    fwd_recv,
):
    cells, feats = state_ref.shape
    rows = land_ref.shape[1]
    heads = bias_ref.shape[0]
    head_dim = feats // heads
    local = EXPERTS // lon_count
    slots = local * 16
    units = up_ref.shape[1] // local
    reach = WINDOW // 2
    f32, bf16 = jnp.float32, jnp.bfloat16
    lat, lon = lax.axis_index("lat"), lax.axis_index("lon")
    core_mate = lat + 1 - 2 * lax.rem(lat, 2)
    x_mate = lax.rem(lat + 2, 4)

    def shifted(dlat, dlon):
        return (lax.rem(lat + dlat + 4, 4), lax.rem(lon + dlon + lon_count, lon_count))

    near = [(a, b) for a in (-1, 0, 1) for b in (-1, 0, 1) if (a, b) != (0, 0)]
    barrier = pltpu.get_barrier_semaphore()
    met = [shifted(*step) for step in near if step[0] != 0]
    met += [shifted(0, step) for step in range(1, lon_count)] + [(x_mate, lon)]
    for device in met:
        pl.semaphore_signal(barrier, inc=1, device_id=device, device_id_type=MESH)

    loads = {}
    for index, (source, target) in enumerate(
        (
            (land_hbm, land_ref),
            (regime_hbm, regime_ref),
            (state_hbm, state_ref),
            (cot_hbm, cot_ref),
            (gain1_hbm, gain1_ref),
            (proj_hbm, proj_ref),
            (bias_hbm, bias_ref),
            (gain2_hbm, gain2_ref),
            (outw_hbm, outw_ref),
            (up_hbm, up_ref),
            (down_hbm, down_ref),
        )
    ):
        loads[index] = pltpu.make_async_copy(source, target, load_sem.at[index])
        loads[index].start()
    loads[0].wait()
    loads[1].wait()

    def remote(source, target, sent, received, device):
        return pltpu.make_async_remote_copy(
            src_ref=source,
            dst_ref=target,
            send_sem=sent,
            recv_sem=received,
            device_id=device,
            device_id_type=MESH,
        )

    spread_rows = (iota((cells, rows), 0) // 8 == iota((cells, rows), 1)).astype(bf16)
    own_col = lax.rem(iota((cells, 8), 0), 8) == iota((cells, 8), 1)

    def column(grid_ref):
        wide = dot(spread_rows, grid_ref[...].astype(f32).astype(bf16), ((1,), (1,)))
        return jnp.sum(jnp.where(own_col, wide, 0.0), axis=1, keepdims=True)

    land_col = column(land_ref)
    label_col = column(regime_ref)
    row_id, col_id = iota((cells, cells), 0), iota((cells, cells), 1)
    label_row = jnp.sum(jnp.where(row_id == col_id, label_col, 0.0), axis=0, keepdims=True)
    same = (label_col == label_row).astype(f32)
    rank_row = jnp.sum(jnp.where(row_id < col_id, same, 0.0), axis=0, keepdims=True)
    rank_col = jnp.sum(jnp.where(col_id < row_id, same, 0.0), axis=1, keepdims=True)
    slot_row = (label_row * 16.0 + rank_row).astype(jnp.int32)
    slot_col = (label_col * 16.0 + rank_col).astype(jnp.int32)
    all_slots = EXPERTS * 16
    to_slots = (iota((all_slots, cells), 0) == slot_row).astype(bf16)
    to_cells = (iota((cells, all_slots), 1) == slot_col).astype(bf16)

    loads[2].wait()
    loads[3].wait()
    state = state_ref[...].astype(f32)
    shown = jnp.where(land_col > 0.5, state, LAND).astype(bf16)
    sent[:cells] = shown
    side_rows = cells // 2
    side_id = iota((2 * side_rows, cells), 0)
    low = lax.rem(side_id, side_rows)
    wanted = low // 4 * 8 + lax.rem(low, 4) + jnp.where(side_id < side_rows, 0, 4)
    to_sides = (wanted == iota((2 * side_rows, cells), 1)).astype(bf16)
    sent[cells:] = dot(to_sides, shown).astype(bf16)
    tangent = (cot_ref[...].astype(f32) * land_col).astype(bf16)
    send_c[...] = dot(to_slots, tangent).astype(bf16).reshape(lon_count, slots, feats)
    got_c[0, pl.ds(lon, 1)] = send_c[pl.ds(lon, 1)]

    pl.semaphore_wait(barrier, len(met))

    halo_copies = []
    for index, (dlat, dlon) in enumerate(near):
        edge = HALO if dlon == 0 else HALO // 2
        body = cells if dlon == 0 else side_rows
        first = {0: 0, -1: cells, 1: cells + side_rows}[dlon]
        if dlat == 0:
            src, dst = (first, body), (edge, body)
        elif dlat == 1:
            src, dst = (first + body - edge, edge), (0, edge)
        else:
            src, dst = (first, edge), (edge + body, edge)
        if dlon == 0:
            target = ends.at[pl.ds(0 if dlat == 1 else edge, edge)]
        else:
            target = sides.at[0 if dlon == -1 else 1, pl.ds(*dst)]
        copy = remote(
            sent.at[pl.ds(*src)],
            target,
            halo_send.at[index],
            halo_recv.at[index],
            shifted(dlat, dlon),
        )
        copy.start()
        halo_copies.append(copy)

    def to_peers(source, target, sent, received):
        copies = []
        for step in range(1, lon_count):
            device = shifted(0, step)
            copy = remote(
                source.at[device[1]], target.at[lon], sent.at[step], received.at[step], device
            )
            copy.start()
            copies.append(copy)
        return copies

    c_copies = to_peers(send_c, got_c.at[0], c_send, c_recv)

    for index in (4, 5, 6):
        loads[index].wait()

    normed = norm_rows(state, gain1_ref[...])
    own_kv[...] = dot(normed, proj_ref[:, feats:])
    queries = dot(normed, proj_ref[:, :feats]).astype(bf16).astype(f32)
    head_mask = (iota((heads, feats), 1) // head_dim == iota((heads, feats), 0)).astype(f32)
    qexp[...] = (
        (queries[:, None, :] * head_mask[None, :, :]).reshape(cells * heads, feats).astype(bf16)
    )

    padded[...] = jnp.zeros_like(padded)
    padded[:, : WINDOW * WINDOW] = bias_ref[...]
    taps = padded[...]
    lane = iota((heads, LANES), 1)
    group, place = lane // 16, lax.rem(lane, 16)
    base = jnp.zeros((heads, LANES), f32)
    for a in range(WINDOW):
        moved = pltpu.roll(taps, 16 * (a + 1) - WINDOW * a, axis=1)
        base = jnp.where(jnp.logical_and(group == a + 1, place < WINDOW), moved, base)
    bias_rows, shape_rows, centre_rows = [], [], []
    key_col = jnp.where(place < 8 + reach, place, place - 16)
    for q in range(8):
        rolled = pltpu.roll(base, (q - reach) % LANES, axis=1)
        if q < reach:
            wrapped = pltpu.roll(base, q - reach + 16, axis=1)
            rolled = jnp.where(place >= 8 + reach, wrapped, rolled)
        bias_rows.append(rolled)
        inside = jnp.logical_and(jnp.abs(key_col - q) <= reach, group >= 1)
        shape_rows.append(inside.astype(f32))
        centre_rows.append(jnp.logical_and(group == reach + 1, place == q).astype(f32))
    bias = jnp.concatenate(bias_rows, axis=0)
    inside = jnp.concatenate(shape_rows, axis=0)
    centre = jnp.concatenate(centre_rows, axis=0)
    head_rows = jnp.concatenate([head_mask] * 8, axis=0)

    total_rows = 2 * (cells + 2 * HALO)
    window_id = iota((total_rows, 1), 0)
    ext_lat, ext_col = window_id // 16, lax.rem(window_id, 16)
    edge_lat = HALO // 8
    end_at = jnp.where(ext_lat < edge_lat, ext_lat, ext_lat - rows)
    in_end = jnp.logical_or(ext_lat < edge_lat, ext_lat >= edge_lat + rows)
    middle_at = jnp.where(in_end, end_at * 8, 2 * HALO + (ext_lat - edge_lat) * 8) + ext_col
    side_at = 2 * HALO + cells + ext_lat * 4 + lax.rem(ext_col, 4)
    side_at = side_at + jnp.where(ext_col < 12, 0, total_rows // 4)
    source_row = jnp.where(ext_col < 8, middle_at, side_at)
    low_lat = jnp.where(lat == 0, edge_lat, 0)
    high_lat = jnp.where(lat == 3, edge_lat + rows, 2 * edge_lat + rows)
    on_grid = jnp.logical_and(ext_lat >= low_lat, ext_lat < high_lat)
    source_row = jnp.where(on_grid, source_row, -1)
    placing = (iota((total_rows, total_rows), 1) == source_row).astype(bf16)

    for copy in halo_copies:
        copy.wait()

    ext_rows = cells + 2 * HALO
    far = jnp.concatenate([ends[...], sides[0], sides[1]], axis=0).astype(f32)
    far_kv = dot(norm_rows(far, gain1_ref[...]), proj_ref[:, feats:])
    ocean_far = (far[:, :LANES] < 0.5 * LAND).astype(f32)
    ocean_own = jnp.broadcast_to(land_col, (cells, LANES))

    def in_order(end, own, side):
        return dot(placing, jnp.concatenate([end, own, side], axis=0).astype(bf16)).astype(bf16)

    two = 2 * HALO
    window_data[:, : 2 * feats] = in_order(far_kv[:two], own_kv[...], far_kv[two:])
    window_data[:, 2 * feats :] = in_order(ocean_far[:two], ocean_own, ocean_far[two:])

    for copy in c_copies:
        copy.wait()
    c_core = remote(got_c.at[0], got_c.at[1], lat_send.at[0], lat_recv.at[0], (core_mate, lon))
    c_far = remote(got_c.at[0], got_c.at[2], lat_send.at[1], lat_recv.at[1], (x_mate, lon))
    c_far.start()
    c_core.start()

    per_row = 8 * heads
    scale = 1.0 / math.sqrt(head_dim)
    ones = jnp.ones((8, LANES), bf16)

    batch = 4

    def attend(i, carry):
        windows = [pl.ds(pl.multiple_of((i * batch + k) * 16, 16), LANES) for k in range(batch)]
        rows_of = pl.ds(pl.multiple_of(i * batch * per_row, batch * per_row), batch * per_row)
        rows_q = qexp[rows_of, :]
        parts = []
        for k, window in enumerate(windows):
            ocean = dot(ones, window_data[window, 2 * feats :], ((1,), (1,)))[:1]
            raw = dot(rows_q[k * per_row : (k + 1) * per_row], window_data[window, :feats], ((1,), (1,)))
            valid = jnp.where(ocean > 0.5, inside, centre) > 0.5
            parts.append(jnp.where(valid, raw * scale + bias, -jnp.inf))
        raw = jnp.concatenate(parts, axis=0)
        powers = jnp.exp(raw - jnp.max(raw, axis=1, keepdims=True))
        weights = (powers / jnp.sum(powers, axis=1, keepdims=True)).astype(bf16)
        for k, window in enumerate(windows):
            mixed = dot(weights[k * per_row : (k + 1) * per_row], window_data[window, feats : 2 * feats]) * head_rows
            mixed = jnp.sum(mixed.reshape(8, heads, feats), axis=1)
            attended[pl.ds(pl.multiple_of((i * batch + k) * 8, 8), 8), :] = mixed
        return carry

    lax.fori_loop(0, rows // batch, attend, 0)

    loads[7].wait()
    loads[8].wait()
    residual = (state + dot(attended[...].astype(bf16), outw_ref[...])).astype(bf16).astype(f32)
    second = norm_rows(residual, gain2_ref[...])
    send_x[...] = dot(to_slots, second).astype(bf16).reshape(lon_count, slots, feats)
    x_copies = to_peers(send_x, got_x.at[0], x_send, x_recv)
    got_x[0, pl.ds(lon, 1)] = send_x[pl.ds(lon, 1)]

    far = []
    for step in range(lon_count):
        if step > 0:
            x_copies[step - 1].wait()
        source = shifted(0, -step)[1]
        copy = remote(
            got_x.at[0, source],
            got_x.at[2, source],
            fwd_send.at[step],
            fwd_recv.at[step],
            (x_mate, lon),
        )
        copy.start()
        far.append(copy)
    x_core = remote(got_x.at[0], got_x.at[1], lat_send.at[2], lat_recv.at[2], (core_mate, lon))
    x_core.start()

    loads[9].wait()
    loads[10].wait()
    count = lon_count * 16

    stores = []

    def store(source, target):
        copy = pltpu.make_async_copy(source, target, store_sem.at[len(stores)])
        copy.start()
        stores.append(copy)

    kept_out[...] = (land_col * residual).astype(bf16)
    pick_out[...] = (land_col * to_cells.astype(f32)).astype(bf16)
    store(kept_out, kept_hbm)
    store(pick_out, pick_hbm)

    def rows_out(band):
        for e in range(local):
            taken, here = pl.ds(e * 16, 16), pl.ds(band * lon_count, lon_count)
            store(got_x.at[band, :, taken], x_hbm.at[e, here])
            store(got_c.at[band, :, taken], c_hbm.at[e, here])

    def experts_on(band, chosen):
        made = []
        for e in chosen:
            x_rows = got_x[band, :, e * 16 : (e + 1) * 16, :].reshape(count, feats)
            c_rows = got_c[band, :, e * 16 : (e + 1) * 16, :].reshape(count, feats)
            here = slice(band * count, (band + 1) * count)
            total = jnp.zeros((count, feats), f32)
            for start in range(e * units, (e + 1) * units, feats):
                part = slice(start, start + feats)
                spot = slice(start - e * units, start - e * units + feats)
                act, slope = gelu_parts(dot(x_rows, up_ref[:, part]))
                act = act.astype(bf16)
                back = dot(c_rows, down_ref[part, :], ((1,), (1,)))
                active[e, here, spot] = act
                pre_act[e, here, spot] = (back * slope).astype(bf16)
                if band == 0:
                    total += dot(act, down_ref[part, :])
            store(active.at[e, here], active_hbm.at[e, here])
            store(pre_act.at[e, here], pre_hbm.at[e, here])
            if band == 0:
                made.append(total.astype(bf16))
        return made

    c_far.wait()
    c_diag = remote(got_c.at[2], got_c.at[3], lat_send.at[3], lat_recv.at[3], (core_mate, lon))
    c_diag.start()
    for e, made in enumerate(experts_on(0, range(local))):
        send_o[:, e * 16 : (e + 1) * 16, :] = made.reshape(lon_count, 16, feats)
    o_copies = to_peers(send_o, got_o, o_send, o_recv)
    got_o[pl.ds(lon, 1)] = send_o[pl.ds(lon, 1)]
    rows_out(0)

    c_core.wait()
    x_core.wait()
    rows_out(1)
    experts_on(1, range(local // 2))
    for copy in far:
        copy.wait()
    x_diag = remote(got_x.at[2], got_x.at[3], lat_send.at[4], lat_recv.at[4], (core_mate, lon))
    x_diag.start()
    rows_out(2)
    experts_on(1, range(local // 2, local))
    c_diag.wait()
    x_diag.wait()
    rows_out(3)

    for copy in o_copies:
        copy.wait()
    store(got_o, returned_hbm)
    for copy in stores:
        copy.wait()


def gradient_kernel(
    x_ref,
    c_ref,
    active_ref,
    pre_ref,
    kept_ref,
    pick_ref,
    returned_ref,
    up_ref,
    down_ref,
    block_ref,
    gup_ref,
    gdown_ref,
    x_turned,
):
    done = active_ref.shape[1]

    @pl.when(pl.program_id(1) == 0)
    def _():
        x_turned[...] = x_ref[0].T
        made = dot(pick_ref[...], returned_ref[...])
        block_ref[...] = (kept_ref[...].astype(jnp.float32) + made).astype(jnp.bfloat16)

    act, slope = gelu_parts(dot(x_ref[0, done:], up_ref[...]))
    back = dot(c_ref[0, done:], down_ref[...], ((1,), (1,)))
    pre_act = jnp.concatenate([pre_ref[0], (back * slope).astype(jnp.bfloat16)], axis=0)
    active = jnp.concatenate([active_ref[0], act.astype(jnp.bfloat16)], axis=0)
    gup_ref[...] = dot(x_turned[...], pre_act)
    gdown_ref[...] = dot(active, c_ref[0], ((0,), (0,)))


def on_device_fused(
    state,
    cotangent,
    land_sea,
    regime,
    first_gain,
    second_gain,
    project_weight,
    out_weight,
    pos_bias,
    up_weight,
    down_weight,
):
    lat_rows, lon_cols, feats = state.shape
    cells = lat_rows * lon_cols
    heads = pos_bias.shape[0]
    lon_count = lax.axis_size("lon")
    local = EXPERTS // lon_count
    slots = local * 16
    units = up_weight.shape[1] // local
    ext_rows = cells + 2 * HALO
    bf16, f32 = jnp.bfloat16, jnp.float32
    dma = pltpu.SemaphoreType.DMA
    hbm = pl.BlockSpec(memory_space=pltpu.HBM)
    all_rows = 4 * lon_count * 16
    operands = (
        state.reshape(cells, feats),
        cotangent.reshape(cells, feats),
        land_sea.T,
        regime.reshape(lat_rows, lon_cols).T,
        first_gain.reshape(1, feats),
        second_gain.reshape(1, feats),
        project_weight,
        out_weight,
        pos_bias,
        up_weight,
        down_weight,
    )
    made = pl.pallas_call(
        functools.partial(fused_kernel, lon_count),
        out_shape=(
            jax.ShapeDtypeStruct((local, 4 * lon_count, 16, feats), bf16),
            jax.ShapeDtypeStruct((local, 4 * lon_count, 16, feats), bf16),
            jax.ShapeDtypeStruct((local, all_rows // 2, units), bf16),
            jax.ShapeDtypeStruct((local, all_rows // 2, units), bf16),
            jax.ShapeDtypeStruct((cells, feats), bf16),
            jax.ShapeDtypeStruct((cells, EXPERTS * 16), bf16),
            jax.ShapeDtypeStruct((lon_count, slots, feats), bf16),
        ),
        in_specs=[hbm] * 11,
        out_specs=(hbm,) * 7,
        scratch_shapes=[
            *(pltpu.VMEM(operand.shape, operand.dtype) for operand in operands),
            dma((11,)),
            pltpu.VMEM((local, all_rows // 2, units), bf16),
            pltpu.VMEM((local, all_rows // 2, units), bf16),
            pltpu.VMEM((cells, feats), bf16),
            pltpu.VMEM((cells, EXPERTS * 16), bf16),
            dma((3 + 12 * local,)),
            pltpu.VMEM((2 * cells, feats), bf16),
            pltpu.VMEM((2 * HALO, feats), bf16),
            pltpu.VMEM((2, ext_rows // 2, feats), bf16),
            pltpu.VMEM((2 * ext_rows, 2 * feats + LANES), bf16),
            pltpu.VMEM((cells * heads, feats), bf16),
            pltpu.VMEM((cells, 2 * feats), f32),
            pltpu.VMEM((cells, feats), f32),
            pltpu.VMEM((heads, LANES), f32),
            pltpu.VMEM((lon_count, slots, feats), bf16),
            pltpu.VMEM((lon_count, slots, feats), bf16),
            pltpu.VMEM((4, lon_count, slots, feats), bf16),
            pltpu.VMEM((4, lon_count, slots, feats), bf16),
            pltpu.VMEM((lon_count, slots, feats), bf16),
            pltpu.VMEM((lon_count, slots, feats), bf16),
            dma((8,)),
            dma((8,)),
            dma((lon_count,)),
            dma((lon_count,)),
            dma((lon_count,)),
            dma((lon_count,)),
            dma((lon_count,)),
            dma((lon_count,)),
            dma((5,)),
            dma((5,)),
            dma((lon_count,)),
            dma((lon_count,)),
        ],
        compiler_params=pltpu.CompilerParams(
            collective_id=0, has_side_effects=True, vmem_limit_bytes=56 * 1024 * 1024
        ),
    )(*operands)
    wide = feats
    halves = units // wide
    block, grad_up, grad_down = pl.pallas_call(
        gradient_kernel,
        grid=(local, halves),
        out_shape=(
            jax.ShapeDtypeStruct((cells, feats), bf16),
            jax.ShapeDtypeStruct(up_weight.shape, f32),
            jax.ShapeDtypeStruct(down_weight.shape, f32),
        ),
        in_specs=[
            pl.BlockSpec((1, all_rows, feats), lambda e, u: (e, 0, 0)),
            pl.BlockSpec((1, all_rows, feats), lambda e, u: (e, 0, 0)),
            pl.BlockSpec((1, all_rows // 2, wide), lambda e, u: (e, 0, u)),
            pl.BlockSpec((1, all_rows // 2, wide), lambda e, u: (e, 0, u)),
            pl.BlockSpec((cells, feats), lambda e, u: (0, 0)),
            pl.BlockSpec((cells, EXPERTS * 16), lambda e, u: (0, 0)),
            pl.BlockSpec((EXPERTS * 16, feats), lambda e, u: (0, 0)),
            pl.BlockSpec((feats, wide), lambda e, u: (0, e * halves + u)),
            pl.BlockSpec((wide, feats), lambda e, u: (e * halves + u, 0)),
        ],
        out_specs=(
            pl.BlockSpec((cells, feats), lambda e, u: (0, 0)),
            pl.BlockSpec((feats, wide), lambda e, u: (0, e * halves + u)),
            pl.BlockSpec((wide, feats), lambda e, u: (e * halves + u, 0)),
        ),
        scratch_shapes=[pltpu.VMEM((feats, all_rows), bf16)],
        compiler_params=pltpu.CompilerParams(vmem_limit_bytes=56 * 1024 * 1024),
    )(
        *(rows.reshape(local, all_rows, feats) for rows in made[:2]),
        *made[2:6],
        made[6].reshape(EXPERTS * 16, feats),
        up_weight,
        down_weight,
    )
    return (block.reshape(lat_rows, lon_cols, feats), grad_up, grad_down)


def solution(mesh):
    placed = (
        P("lat", "lon", None),
        P("lat", "lon", None),
        P("lat", "lon"),
        P("lat", "lon", None, None, None),
        P(),
        P(),
        P(),
        P(),
        P(),
        P(None, "lon"),
        P("lon", None),
    )
    lat_count, lon_count = mesh.shape["lat"], mesh.shape["lon"]
    whole_experts = lat_count == 4 and 4 <= lon_count <= EXPERTS
    return jax.shard_map(
        on_device_fused if whole_experts else on_device_general,
        mesh=mesh,
        in_specs=placed,
        out_specs=(P("lat", "lon", None), P(None, "lon"), P("lon", None)),
        check_vma=False,
    )
```

```python
import functools
import math

import jax
import jax.numpy as jnp
from jax import lax
from jax.experimental import pallas as pl
from jax.experimental.pallas import tpu as pltpu
from jax.sharding import PartitionSpec as P

WINDOW = 7
EXPERTS = 16


def from_partner(value, axis, apart):
    mask = 2**apart
    pairs = [(source, source ^ mask) for source in range(lax.axis_size(axis))]
    return lax.ppermute(value, axis, pairs)


def extended(cells, sides, width, closed):
    for axis, dim in sides:
        count = lax.axis_size(axis)
        ends = count if closed else count - 1
        head = lax.slice_in_dim(cells, 0, width, axis=dim)
        tail = lax.slice_in_dim(cells, cells.shape[dim] - width, cells.shape[dim], axis=dim)
        cells = jnp.concatenate(
            [
                lax.ppermute(tail, axis, [(i, (i + 1) % count) for i in range(ends)]),
                cells,
                lax.ppermute(head, axis, [((i + 1) % count, i) for i in range(ends)]),
            ],
            axis=dim,
        )
    return cells


def layer_norm(values, gain_vec):
    values = values.astype(jnp.float32)
    mean_val = jnp.mean(values, axis=-1, keepdims=True)
    spread = jnp.mean(jnp.square(values - mean_val), axis=-1, keepdims=True)
    return ((values - mean_val) * lax.rsqrt(spread + 1e-05) * gain_vec).astype(jnp.bfloat16)


def gelu_value(inputs):
    return 0.5 * inputs * (1.0 + jax.scipy.special.erf(inputs * 0.7071067811865476))


def gelu_slope(inputs):
    return (
        0.5 * (1.0 + jax.scipy.special.erf(inputs * 0.7071067811865476))
        + inputs * jnp.exp(-0.5 * inputs * inputs) * 0.3989422804014327
    )


def expert_pass(inputs, tangents, up_block, down_block):
    hidden = jnp.einsum("nlsd,dlf->nlsf", inputs, up_block, preferred_element_type=jnp.float32)
    active = gelu_value(hidden).astype(jnp.bfloat16)
    outputs = jnp.einsum("nlsf,lfd->nlsd", active, down_block, preferred_element_type=jnp.float32)
    back_act = jnp.einsum(
        "nlsd,lfd->nlsf", tangents, down_block, preferred_element_type=jnp.float32
    )
    pre_act = (back_act * gelu_slope(hidden)).astype(jnp.bfloat16)
    grad_down = jnp.einsum("nlsf,nlsd->lfd", active, tangents, preferred_element_type=jnp.float32)
    grad_up = jnp.einsum("nlsd,nlsf->dlf", inputs, pre_act, preferred_element_type=jnp.float32)
    return (outputs, grad_up, grad_down)


def halve(grad_u, grad_d, lon_index, group_size):
    for bit_level in reversed(range(group_size.bit_length() - 1)):
        half_units = grad_u.shape[1] // 2
        high_bit = lon_index >> bit_level & 1 == 1
        keep_u = jnp.where(high_bit, grad_u[:, half_units:], grad_u[:, :half_units])
        give_u = jnp.where(high_bit, grad_u[:, :half_units], grad_u[:, half_units:])
        keep_d = jnp.where(high_bit, grad_d[half_units:], grad_d[:half_units])
        give_d = jnp.where(high_bit, grad_d[:half_units], grad_d[half_units:])
        taken_u, taken_d = (
            from_partner(give_u.astype(jnp.bfloat16), "lon", bit_level).astype(give_u.dtype),
            from_partner(give_d.astype(jnp.bfloat16), "lon", bit_level).astype(give_d.dtype),
        )
        grad_u = keep_u + taken_u
        grad_d = keep_d + taken_d
    return (grad_u, grad_d)


def on_device_general(
    state,
    cotangent,
    land_sea,
    regime,
    first_gain,
    second_gain,
    project_weight,
    out_weight,
    pos_bias,
    up_weight,
    down_weight,
):
    lat_rows, lon_cols, features = state.shape
    cell_count = lat_rows * lon_cols
    head_count = pos_bias.shape[0]
    head_dim = features // head_count
    window_reach = WINDOW // 2
    tap_count = WINDOW * WINDOW
    score_scale = 1.0 / math.sqrt(head_dim)
    normed_in = layer_norm(state, first_gain)
    flat_in = normed_in.reshape(cell_count, features)
    queries = jnp.dot(
        flat_in, project_weight[:, :features], preferred_element_type=jnp.float32
    ).astype(jnp.bfloat16)
    own_kv = jnp.dot(flat_in, project_weight[:, features:], preferred_element_type=jnp.float32)
    own_kv = own_kv.astype(jnp.bfloat16).reshape(lat_rows, lon_cols, 2 * features)
    wide_kv = extended(own_kv, (("lon", 1),), window_reach, True)
    keyvals = extended(wide_kv, (("lat", 0),), window_reach, False)
    wide_mask = extended(land_sea, (("lon", 1),), window_reach, True)
    full_mask = extended(wide_mask, (("lat", 0),), window_reach, False)
    feature_first = jnp.transpose(keyvals, (2, 0, 1))
    query_heads = queries.T.reshape(head_count, head_dim, cell_count)
    score_list = []
    mask_list = []
    for row_shift in range(WINDOW):
        for col_shift in range(WINDOW):
            key_tap = feature_first[
                :features, row_shift : row_shift + lat_rows, col_shift : col_shift + lon_cols
            ].reshape(head_count, head_dim, cell_count)
            score_list.append(
                jnp.einsum("hxc,hxc->hc", query_heads, key_tap, preferred_element_type=jnp.float32)
            )
            mask_list.append(
                full_mask[
                    row_shift : row_shift + lat_rows, col_shift : col_shift + lon_cols
                ].reshape(cell_count)
            )
    scores = jnp.stack(score_list) * score_scale + pos_bias.T[:, :, None]
    tap_ids = jnp.arange(tap_count, dtype=jnp.int32)[:, None]
    valid_mask = jnp.logical_or(jnp.stack(mask_list) > 0, tap_ids == tap_count // 2)[:, None, :]
    row_top = jnp.max(jnp.where(valid_mask, scores, -jnp.inf), axis=0, keepdims=True)
    raw_weights = jnp.exp(jnp.where(valid_mask, scores - row_top, -jnp.inf))
    weights = (raw_weights / jnp.sum(raw_weights, axis=0, keepdims=True)).astype(jnp.bfloat16)
    attended = jnp.zeros((head_count, head_dim, cell_count), jnp.float32)
    for row_shift in range(WINDOW):
        for col_shift in range(WINDOW):
            tap_index = row_shift * WINDOW + col_shift
            value_tap = feature_first[
                features:, row_shift : row_shift + lat_rows, col_shift : col_shift + lon_cols
            ].reshape(head_count, head_dim, cell_count)
            attended = attended + weights[tap_index][:, None, :].astype(
                jnp.float32
            ) * value_tap.astype(jnp.float32)
    attended = attended.reshape(features, cell_count).T.astype(jnp.bfloat16)
    residual = (
        state.reshape(cell_count, features).astype(jnp.float32)
        + jnp.dot(attended, out_weight, preferred_element_type=jnp.float32)
    ).astype(jnp.bfloat16)
    second = layer_norm(residual, second_gain)
    masked = land_sea.reshape(cell_count, 1)
    tangent = cotangent.reshape(cell_count, features) * masked.astype(jnp.bfloat16)
    labels = regime.reshape(cell_count)
    capacity = cell_count // 8
    onehot = (labels[:, None] == jnp.arange(EXPERTS, dtype=jnp.int32)[None, :]).astype(jnp.int32)
    before = jnp.cumsum(onehot, axis=0) - onehot
    rank_index = jnp.sum(before * onehot, axis=1)
    slot_index = labels * capacity + rank_index
    owner_of = (
        jnp.full((EXPERTS * capacity,), cell_count, jnp.int32)
        .at[slot_index]
        .set(jnp.arange(cell_count, dtype=jnp.int32))
    )
    send_x = jnp.concatenate([second, jnp.zeros((1, features), jnp.bfloat16)])[owner_of]
    send_c = jnp.concatenate([tangent, jnp.zeros((1, features), jnp.bfloat16)])[owner_of]
    lon_count = lax.axis_size("lon")
    lon_index = lax.axis_index("lon")
    local_count = max(1, EXPERTS // lon_count)
    group_size = max(1, lon_count // EXPERTS)
    per_peer = EXPERTS * capacity // lon_count
    got_x, got_c = (
        lax.all_to_all(
            send_x.reshape(lon_count, per_peer, features),
            "lon",
            split_axis=0,
            concat_axis=0,
            tiled=True,
        ),
        lax.all_to_all(
            send_c.reshape(lon_count, per_peer, features),
            "lon",
            split_axis=0,
            concat_axis=0,
            tiled=True,
        ),
    )
    up_block = up_weight
    down_block = down_weight
    for bit_level in range(group_size.bit_length() - 1):
        other_up, other_down = from_partner((up_block, down_block), "lon", bit_level)
        high_bit = lon_index >> bit_level & 1 == 1
        up_block = jnp.where(
            high_bit,
            jnp.concatenate([other_up, up_block], axis=1),
            jnp.concatenate([up_block, other_up], axis=1),
        )
        down_block = jnp.where(
            high_bit,
            jnp.concatenate([other_down, down_block], axis=0),
            jnp.concatenate([down_block, other_down], axis=0),
        )
    unit_count = up_block.shape[1] // local_count
    outputs, grad_u, grad_d = expert_pass(
        got_x.reshape(lon_count, local_count, per_peer // local_count, features),
        got_c.reshape(lon_count, local_count, per_peer // local_count, features),
        up_block.reshape(features, local_count, unit_count),
        down_block.reshape(local_count, unit_count, features),
    )
    returned = lax.all_to_all(
        outputs.astype(jnp.bfloat16).reshape(lon_count, per_peer, features),
        "lon",
        split_axis=0,
        concat_axis=0,
        tiled=True,
    )
    expert_rows = returned.reshape(EXPERTS * capacity, features)
    grad_u = grad_u.reshape(features, local_count * unit_count)
    grad_d = grad_d.reshape(local_count * unit_count, features)
    grad_u, grad_d = (
        lax.psum(grad_u.astype(jnp.bfloat16), "lat").astype(jnp.float32),
        lax.psum(grad_d.astype(jnp.bfloat16), "lat").astype(jnp.float32),
    )
    grad_u, grad_d = halve(grad_u, grad_d, lon_index, group_size)
    expert_cell = expert_rows[slot_index]
    result_block = (
        masked.astype(jnp.float32)
        * (residual.astype(jnp.float32) + expert_cell.astype(jnp.float32))
    ).astype(jnp.bfloat16)
    return (result_block.reshape(lat_rows, lon_cols, features), grad_u, grad_d)


MESH = pl.DeviceIdType.MESH
HALO = 32
LANES = 128
LAND = 1024.0


def dot(left, right, dims=((1,), (0,))):
    return lax.dot_general(left, right, (dims, ((), ())), preferred_element_type=jnp.float32)


def norm_rows(values, gain_row):
    mean_val = jnp.mean(values, axis=-1, keepdims=True)
    centred = values - mean_val
    spread = jnp.mean(jnp.square(centred), axis=-1, keepdims=True)
    return (centred * lax.rsqrt(spread + 1e-05) * gain_row).astype(jnp.bfloat16)


def iota(shape, dim):
    return lax.broadcasted_iota(jnp.int32, shape, dim)


def gelu_parts(hidden):
    bell = jnp.exp(-0.5 * hidden * hidden)
    depth = 1.0 + 0.3275911 * 0.7071067811865476 * jnp.abs(hidden)
    near = pl.reciprocal(depth, approx=True)
    near = near * (2.0 - depth * near)
    series = 0.5 * 1.061405429
    for factor in (-1.453152027, 1.421413741, -0.284496736, 0.254829592):
        series = series * near + 0.5 * factor
    tail = series * near * bell
    half = jnp.where(hidden >= 0.0, 1.0 - tail, tail)
    return (hidden * half, half + hidden * bell * 0.3989422804014327)


def fused_kernel(
    lon_count,
    state_hbm,
    cot_hbm,
    land_hbm,
    regime_hbm,
    gain1_hbm,
    gain2_hbm,
    proj_hbm,
    outw_hbm,
    bias_hbm,
    up_hbm,
    down_hbm,
    x_hbm,
    c_hbm,
    active_hbm,
    pre_hbm,
    kept_hbm,
    pick_hbm,
    returned_hbm,
    state_ref,
    cot_ref,
    land_ref,
    regime_ref,
    gain1_ref,
    gain2_ref,
    proj_ref,
    outw_ref,
    bias_ref,
    up_ref,
    down_ref,
    load_sem,
    active,
    pre_act,
    kept_out,
    pick_out,
    store_sem,
    sent,
    ends,
    sides,
    window_data,
    qexp,
    own_kv,
    attended,
    padded,
    send_c,
    send_x,
    got_c,
    got_x,
    send_o,
    got_o,
    halo_send,
    halo_recv,
    c_send,
    c_recv,
    x_send,
    x_recv,
    o_send,
    o_recv,
    lat_send,
    lat_recv,
):
    cells, feats = state_ref.shape
    rows = land_ref.shape[1]
    heads = bias_ref.shape[0]
    head_dim = feats // heads
    local = EXPERTS // lon_count
    units = up_ref.shape[1] // local
    reach = WINDOW // 2
    f32, bf16 = jnp.float32, jnp.bfloat16
    lat, lon = lax.axis_index("lat"), lax.axis_index("lon")
    core_mate = lat + 1 - 2 * lax.rem(lat, 2)
    x_mate = lax.rem(lat + 2, 4)

    def shifted(dlat, dlon):
        return (lax.rem(lat + dlat + 4, 4), lax.rem(lon + dlon + lon_count, lon_count))

    near = [(a, b) for a in (-1, 0, 1) for b in (-1, 0, 1) if (a, b) != (0, 0)]
    barrier = pltpu.get_barrier_semaphore()
    met = [shifted(*step) for step in near if step[0] != 0]
    met += [shifted(0, step) for step in range(1, lon_count)] + [(x_mate, lon)]
    for device in met:
        pl.semaphore_signal(barrier, inc=1, device_id=device, device_id_type=MESH)

    loads = {}
    for index, (source, target) in enumerate(
        (
            (land_hbm, land_ref),
            (regime_hbm, regime_ref),
            (state_hbm, state_ref),
            (cot_hbm, cot_ref),
            (gain1_hbm, gain1_ref),
            (proj_hbm, proj_ref),
            (bias_hbm, bias_ref),
            (gain2_hbm, gain2_ref),
            (outw_hbm, outw_ref),
            (up_hbm, up_ref),
            (down_hbm, down_ref),
        )
    ):
        loads[index] = pltpu.make_async_copy(source, target, load_sem.at[index])
        loads[index].start()
    loads[0].wait()
    loads[1].wait()

    def remote(source, target, sent, received, device):
        return pltpu.make_async_remote_copy(
            src_ref=source,
            dst_ref=target,
            send_sem=sent,
            recv_sem=received,
            device_id=device,
            device_id_type=MESH,
        )

    spread_rows = (iota((cells, rows), 0) // 8 == iota((cells, rows), 1)).astype(bf16)
    own_col = lax.rem(iota((cells, 8), 0), 8) == iota((cells, 8), 1)

    def column(grid_ref):
        wide = dot(spread_rows, grid_ref[...].astype(f32).astype(bf16), ((1,), (1,)))
        return jnp.sum(jnp.where(own_col, wide, 0.0), axis=1, keepdims=True)

    land_col = column(land_ref)
    label_col = column(regime_ref)
    row_id, col_id = iota((cells, cells), 0), iota((cells, cells), 1)
    label_row = jnp.sum(jnp.where(row_id == col_id, label_col, 0.0), axis=0, keepdims=True)
    same = (label_col == label_row).astype(f32)
    rank_row = jnp.sum(jnp.where(row_id < col_id, same, 0.0), axis=0, keepdims=True)
    rank_col = jnp.sum(jnp.where(col_id < row_id, same, 0.0), axis=1, keepdims=True)

    def slot_of(label, rank):
        label = label.astype(jnp.int32)
        place = lax.rem(label, local) * lon_count + lax.div(label, local)
        return place * 16 + rank.astype(jnp.int32)

    slot_row, slot_col = slot_of(label_row, rank_row), slot_of(label_col, rank_col)
    all_slots = EXPERTS * 16
    to_slots = (iota((all_slots, cells), 0) == slot_row).astype(bf16)
    to_cells = (iota((cells, all_slots), 1) == slot_col).astype(bf16)

    loads[2].wait()
    loads[3].wait()
    state = state_ref[...].astype(f32)
    shown = jnp.where(land_col > 0.5, state, LAND).astype(bf16)
    sent[:cells] = shown
    side_rows = cells // 2
    side_id = iota((2 * side_rows, cells), 0)
    low = lax.rem(side_id, side_rows)
    wanted = low // 4 * 8 + lax.rem(low, 4) + jnp.where(side_id < side_rows, 0, 4)
    to_sides = (wanted == iota((2 * side_rows, cells), 1)).astype(bf16)
    sent[cells:] = dot(to_sides, shown).astype(bf16)
    tangent = (cot_ref[...].astype(f32) * land_col).astype(bf16)
    send_c[...] = dot(to_slots, tangent).astype(bf16).reshape(local, lon_count, 16, feats)
    for e in range(local):
        got_c[e, pl.ds(lon, 1)] = send_c[e, pl.ds(lon, 1)]

    pl.semaphore_wait(barrier, len(met))

    halo_copies = []
    for index, (dlat, dlon) in enumerate(near):
        edge = HALO if dlon == 0 else HALO // 2
        body = cells if dlon == 0 else side_rows
        first = {0: 0, -1: cells, 1: cells + side_rows}[dlon]
        if dlat == 0:
            src, dst = (first, body), (edge, body)
        elif dlat == 1:
            src, dst = (first + body - edge, edge), (0, edge)
        else:
            src, dst = (first, edge), (edge + body, edge)
        if dlon == 0:
            target = ends.at[pl.ds(0 if dlat == 1 else edge, edge)]
        else:
            target = sides.at[0 if dlon == -1 else 1, pl.ds(*dst)]
        copy = remote(
            sent.at[pl.ds(*src)],
            target,
            halo_send.at[index],
            halo_recv.at[index],
            shifted(dlat, dlon),
        )
        copy.start()
        halo_copies.append(copy)

    def to_peers(source, target, sent, received, first):
        copies = []
        for step in range(1, lon_count):
            device = shifted(0, step)
            copy = remote(
                source.at[device[1]],
                target.at[lon],
                sent.at[first + step],
                received.at[first + step],
                device,
            )
            copy.start()
            copies.append(copy)
        return copies

    c_copies = []
    for e in range(local):
        c_copies += to_peers(
            send_c.at[e], got_c.at[e], c_send, c_recv, e * lon_count
        )

    for index in (4, 5, 6):
        loads[index].wait()

    normed = norm_rows(state, gain1_ref[...])
    own_kv[...] = dot(normed, proj_ref[:, feats:])
    queries = dot(normed, proj_ref[:, :feats]).astype(bf16).astype(f32)
    head_mask = (iota((heads, feats), 1) // head_dim == iota((heads, feats), 0)).astype(f32)
    qexp[...] = (
        (queries[:, None, :] * head_mask[None, :, :]).reshape(cells * heads, feats).astype(bf16)
    )

    padded[...] = jnp.zeros_like(padded)
    padded[:, : WINDOW * WINDOW] = bias_ref[...]
    taps = padded[...]
    lane = iota((heads, LANES), 1)
    group, place = lane // 16, lax.rem(lane, 16)
    base = jnp.zeros((heads, LANES), f32)
    for a in range(WINDOW):
        moved = pltpu.roll(taps, 16 * (a + 1) - WINDOW * a, axis=1)
        base = jnp.where(jnp.logical_and(group == a + 1, place < WINDOW), moved, base)
    bias_rows, shape_rows, centre_rows = [], [], []
    key_col = jnp.where(place < 8 + reach, place, place - 16)
    for q in range(8):
        rolled = pltpu.roll(base, (q - reach) % LANES, axis=1)
        if q < reach:
            wrapped = pltpu.roll(base, q - reach + 16, axis=1)
            rolled = jnp.where(place >= 8 + reach, wrapped, rolled)
        bias_rows.append(rolled)
        inside = jnp.logical_and(jnp.abs(key_col - q) <= reach, group >= 1)
        shape_rows.append(inside.astype(f32))
        centre_rows.append(jnp.logical_and(group == reach + 1, place == q).astype(f32))
    bias = jnp.concatenate(bias_rows, axis=0)
    inside = jnp.concatenate(shape_rows, axis=0)
    centre = jnp.concatenate(centre_rows, axis=0)
    head_rows = jnp.concatenate([head_mask] * 8, axis=0)

    total_rows = 2 * (cells + 2 * HALO)
    window_id = iota((total_rows, 1), 0)
    ext_lat, ext_col = window_id // 16, lax.rem(window_id, 16)
    edge_lat = HALO // 8
    end_at = jnp.where(ext_lat < edge_lat, ext_lat, ext_lat - rows)
    in_end = jnp.logical_or(ext_lat < edge_lat, ext_lat >= edge_lat + rows)
    middle_at = jnp.where(in_end, end_at * 8, 2 * HALO + (ext_lat - edge_lat) * 8) + ext_col
    side_at = 2 * HALO + cells + ext_lat * 4 + lax.rem(ext_col, 4)
    side_at = side_at + jnp.where(ext_col < 12, 0, total_rows // 4)
    source_row = jnp.where(ext_col < 8, middle_at, side_at)
    low_lat = jnp.where(lat == 0, edge_lat, 0)
    high_lat = jnp.where(lat == 3, edge_lat + rows, 2 * edge_lat + rows)
    on_grid = jnp.logical_and(ext_lat >= low_lat, ext_lat < high_lat)
    source_row = jnp.where(on_grid, source_row, -1)
    placing = (iota((total_rows, total_rows), 1) == source_row).astype(bf16)

    for copy in halo_copies:
        copy.wait()

    ext_rows = cells + 2 * HALO
    far = jnp.concatenate([ends[...], sides[0], sides[1]], axis=0).astype(f32)
    far_kv = dot(norm_rows(far, gain1_ref[...]), proj_ref[:, feats:])
    ocean_far = (far[:, :LANES] < 0.5 * LAND).astype(f32)
    ocean_own = jnp.broadcast_to(land_col, (cells, LANES))

    def in_order(end, own, side):
        return dot(placing, jnp.concatenate([end, own, side], axis=0).astype(bf16)).astype(bf16)

    two = 2 * HALO
    window_data[:, : 2 * feats] = in_order(far_kv[:two], own_kv[...], far_kv[two:])
    window_data[:, 2 * feats :] = in_order(ocean_far[:two], ocean_own, ocean_far[two:])

    for copy in c_copies:
        copy.wait()
    c_core = remote(got_c.at[pl.ds(0 * local, local)], got_c.at[pl.ds(1 * local, local)], lat_send.at[0], lat_recv.at[0], (core_mate, lon))
    c_far = remote(got_c.at[pl.ds(0 * local, local)], got_c.at[pl.ds(2 * local, local)], lat_send.at[1], lat_recv.at[1], (x_mate, lon))
    c_far.start()
    c_core.start()

    per_row = 8 * heads
    scale = 1.0 / math.sqrt(head_dim)
    ones = jnp.ones((8, LANES), bf16)

    batch = 4

    def attend(i):
        windows = [slice((i * batch + k) * 16, (i * batch + k) * 16 + LANES) for k in range(batch)]
        rows_of = slice(i * batch * per_row, (i + 1) * batch * per_row)
        rows_q = qexp[rows_of, :]
        parts = []
        for k, window in enumerate(windows):
            ocean = dot(ones, window_data[window, 2 * feats :], ((1,), (1,)))[:1]
            raw = dot(rows_q[k * per_row : (k + 1) * per_row], window_data[window, :feats], ((1,), (1,)))
            valid = jnp.where(ocean > 0.5, inside, centre) > 0.5
            parts.append(jnp.where(valid, raw * scale + bias, -jnp.inf))
        raw = jnp.concatenate(parts, axis=0)
        powers = jnp.exp(raw - jnp.max(raw, axis=1, keepdims=True))
        weights = (powers / jnp.sum(powers, axis=1, keepdims=True)).astype(bf16)
        for k, window in enumerate(windows):
            mixed = dot(weights[k * per_row : (k + 1) * per_row], window_data[window, feats : 2 * feats]) * head_rows
            mixed = jnp.sum(mixed.reshape(8, heads, feats), axis=1)
            attended[(i * batch + k) * 8 : (i * batch + k + 1) * 8, :] = mixed

    for i in range(rows // batch):
        attend(i)

    loads[7].wait()
    loads[8].wait()
    residual = (state + dot(attended[...].astype(bf16), outw_ref[...])).astype(bf16).astype(f32)
    second = norm_rows(residual, gain2_ref[...])
    send_x[...] = dot(to_slots, second).astype(bf16).reshape(local, lon_count, 16, feats)
    x_copies = [
        to_peers(
            send_x.at[e], got_x.at[e], x_send, x_recv, e * lon_count
        )
        for e in range(local)
    ]
    for e in range(local):
        got_x[e, pl.ds(lon, 1)] = send_x[e, pl.ds(lon, 1)]

    loads[9].wait()
    loads[10].wait()
    count = lon_count * 16

    stores = []

    def store(source, target):
        copy = pltpu.make_async_copy(source, target, store_sem.at[len(stores)])
        copy.start()
        stores.append(copy)

    kept_out[...] = (land_col * residual).astype(bf16)
    pick_out[...] = (land_col * to_cells.astype(f32)).astype(bf16)
    store(kept_out, kept_hbm)
    store(pick_out, pick_hbm)

    def band_copy(source, target, e, index, mate):
        slot = 3 + 3 * e + index
        return remote(
            got_x.at[source * local + e],
            got_x.at[target * local + e],
            lat_send.at[slot],
            lat_recv.at[slot],
            (mate, lon),
        )

    def rows_out(band, e):
        here = pl.ds(band * lon_count, lon_count)
        store(got_x.at[band * local + e], x_hbm.at[e, here])
        store(got_c.at[band * local + e], c_hbm.at[e, here])

    def expert_on(band, e):
        x_rows = got_x[band * local + e].reshape(count, feats)
        c_rows = got_c[band * local + e].reshape(count, feats)
        here = slice(band * count, (band + 1) * count)
        total = jnp.zeros((count, feats), f32)
        for start in range(e * units, (e + 1) * units, feats):
            part = slice(start, start + feats)
            spot = slice(start - e * units, start - e * units + feats)
            act, slope = gelu_parts(dot(x_rows, up_ref[:, part]))
            act = act.astype(bf16)
            back = dot(c_rows, down_ref[part, :], ((1,), (1,)))
            active[e, here, spot] = act
            pre_act[e, here, spot] = (back * slope).astype(bf16)
            if band == 0:
                total += dot(act, down_ref[part, :])
        store(active.at[e, here], active_hbm.at[e, here])
        store(pre_act.at[e, here], pre_hbm.at[e, here])
        return total.astype(bf16)

    far, core, diag, o_copies = [], [], [], []
    for e in range(local):
        for copy in x_copies[e]:
            copy.wait()
        far.append(band_copy(0, 2, e, 0, x_mate))
        core.append(band_copy(0, 1, e, 1, core_mate))
        far[e].start()
        core[e].start()
        send_o[e] = expert_on(0, e).reshape(lon_count, 16, feats)
        o_copies += to_peers(
            send_o.at[e], got_o.at[e], o_send, o_recv, e * lon_count
        )
        got_o[e, pl.ds(lon, 1)] = send_o[e, pl.ds(lon, 1)]
        rows_out(0, e)

    c_far.wait()
    c_diag = remote(got_c.at[pl.ds(2 * local, local)], got_c.at[pl.ds(3 * local, local)], lat_send.at[2], lat_recv.at[2], (core_mate, lon))
    c_diag.start()
    c_core.wait()
    for e in range(local):
        far[e].wait()
        diag.append(band_copy(2, 3, e, 2, core_mate))
        diag[e].start()
        core[e].wait()
        rows_out(1, e)
        expert_on(1, e)
    for e in range(local):
        rows_out(2, e)
        expert_on(2, e)
    c_diag.wait()
    for e in range(local):
        diag[e].wait()
        rows_out(3, e)
        expert_on(3, e)

    for copy in o_copies:
        copy.wait()
    store(got_o, returned_hbm)
    for copy in stores:
        copy.wait()


def gradient_kernel(
    x_ref, c_ref, active_ref, pre_ref, kept_ref, pick_ref, returned_ref, block_ref, gup_ref, gdown_ref
):
    block_ref[...] = (kept_ref[...].astype(jnp.float32) + dot(pick_ref[...], returned_ref[...])).astype(
        jnp.bfloat16
    )
    gup_ref[...] = dot(x_ref[0], pre_ref[0], ((0,), (0,)))
    gdown_ref[...] = dot(active_ref[0], c_ref[0], ((0,), (0,)))


def on_device_fused(
    state,
    cotangent,
    land_sea,
    regime,
    first_gain,
    second_gain,
    project_weight,
    out_weight,
    pos_bias,
    up_weight,
    down_weight,
):
    lat_rows, lon_cols, feats = state.shape
    cells = lat_rows * lon_cols
    heads = pos_bias.shape[0]
    lon_count = lax.axis_size("lon")
    local = EXPERTS // lon_count
    units = up_weight.shape[1] // local
    ext_rows = cells + 2 * HALO
    bf16, f32 = jnp.bfloat16, jnp.float32
    dma = pltpu.SemaphoreType.DMA
    hbm = pl.BlockSpec(memory_space=pltpu.HBM)
    all_rows = 4 * lon_count * 16
    operands = (
        state.reshape(cells, feats),
        cotangent.reshape(cells, feats),
        land_sea.T,
        regime.reshape(lat_rows, lon_cols).T,
        first_gain.reshape(1, feats),
        second_gain.reshape(1, feats),
        project_weight,
        out_weight,
        pos_bias,
        up_weight,
        down_weight,
    )
    made = pl.pallas_call(
        functools.partial(fused_kernel, lon_count),
        out_shape=(
            jax.ShapeDtypeStruct((local, 4 * lon_count, 16, feats), bf16),
            jax.ShapeDtypeStruct((local, 4 * lon_count, 16, feats), bf16),
            jax.ShapeDtypeStruct((local, all_rows, units), bf16),
            jax.ShapeDtypeStruct((local, all_rows, units), bf16),
            jax.ShapeDtypeStruct((cells, feats), bf16),
            jax.ShapeDtypeStruct((cells, EXPERTS * 16), bf16),
            jax.ShapeDtypeStruct((local, lon_count, 16, feats), bf16),
        ),
        in_specs=[hbm] * 11,
        out_specs=(hbm,) * 7,
        scratch_shapes=[
            *(pltpu.VMEM(operand.shape, operand.dtype) for operand in operands),
            dma((11,)),
            pltpu.VMEM((local, all_rows, units), bf16),
            pltpu.VMEM((local, all_rows, units), bf16),
            pltpu.VMEM((cells, feats), bf16),
            pltpu.VMEM((cells, EXPERTS * 16), bf16),
            dma((3 + 16 * local,)),
            pltpu.VMEM((2 * cells, feats), bf16),
            pltpu.VMEM((2 * HALO, feats), bf16),
            pltpu.VMEM((2, ext_rows // 2, feats), bf16),
            pltpu.VMEM((2 * ext_rows, 2 * feats + LANES), bf16),
            pltpu.VMEM((cells * heads, feats), bf16),
            pltpu.VMEM((cells, 2 * feats), f32),
            pltpu.VMEM((cells, feats), f32),
            pltpu.VMEM((heads, LANES), f32),
            pltpu.VMEM((local, lon_count, 16, feats), bf16),
            pltpu.VMEM((local, lon_count, 16, feats), bf16),
            pltpu.VMEM((4 * local, lon_count, 16, feats), bf16),
            pltpu.VMEM((4 * local, lon_count, 16, feats), bf16),
            pltpu.VMEM((local, lon_count, 16, feats), bf16),
            pltpu.VMEM((local, lon_count, 16, feats), bf16),
            dma((8,)),
            dma((8,)),
            dma((local * lon_count,)),
            dma((local * lon_count,)),
            dma((local * lon_count,)),
            dma((local * lon_count,)),
            dma((local * lon_count,)),
            dma((local * lon_count,)),
            dma((3 + 3 * local,)),
            dma((3 + 3 * local,)),
        ],
        compiler_params=pltpu.CompilerParams(
            collective_id=0, has_side_effects=True, vmem_limit_bytes=56 * 1024 * 1024
        ),
    )(*operands)
    wide = units // 2
    halves = units // wide
    block, grad_up, grad_down = pl.pallas_call(
        gradient_kernel,
        grid=(local, halves),
        out_shape=(
            jax.ShapeDtypeStruct((cells, feats), bf16),
            jax.ShapeDtypeStruct(up_weight.shape, f32),
            jax.ShapeDtypeStruct(down_weight.shape, f32),
        ),
        in_specs=[
            pl.BlockSpec((1, all_rows, feats), lambda e, u: (e, 0, 0)),
            pl.BlockSpec((1, all_rows, feats), lambda e, u: (e, 0, 0)),
            pl.BlockSpec((1, all_rows, wide), lambda e, u: (e, 0, u)),
            pl.BlockSpec((1, all_rows, wide), lambda e, u: (e, 0, u)),
            pl.BlockSpec((cells, feats), lambda e, u: (0, 0)),
            pl.BlockSpec((cells, EXPERTS * 16), lambda e, u: (0, 0)),
            pl.BlockSpec((EXPERTS * 16, feats), lambda e, u: (0, 0)),
        ],
        out_specs=(
            pl.BlockSpec((cells, feats), lambda e, u: (0, 0)),
            pl.BlockSpec((feats, wide), lambda e, u: (0, e * halves + u)),
            pl.BlockSpec((wide, feats), lambda e, u: (e * halves + u, 0)),
        ),
        compiler_params=pltpu.CompilerParams(vmem_limit_bytes=56 * 1024 * 1024),
    )(
        *(rows.reshape(local, all_rows, feats) for rows in made[:2]),
        *made[2:6],
        made[6].reshape(EXPERTS * 16, feats),
    )
    return (block.reshape(lat_rows, lon_cols, feats), grad_up, grad_down)


def solution(mesh):
    placed = (
        P("lat", "lon", None),
        P("lat", "lon", None),
        P("lat", "lon"),
        P("lat", "lon", None, None, None),
        P(),
        P(),
        P(),
        P(),
        P(),
        P(None, "lon"),
        P("lon", None),
    )
    lat_count, lon_count = mesh.shape["lat"], mesh.shape["lon"]
    whole_experts = lat_count == 4 and 4 <= lon_count <= EXPERTS
    return jax.shard_map(
        on_device_fused if whole_experts else on_device_general,
        mesh=mesh,
        in_specs=placed,
        out_specs=(P("lat", "lon", None), P(None, "lon"), P("lon", None)),
        check_vma=False,
    )
```
